32 devices in a mesh: tower: 2 (over core), dp: 16 (over z, y, x).
Axes of the slice: x: 2, y: 2, z: 4, core: 2. Of those that a mesh axis runs over, the one named last changes fastest.
Arguments:
- picture_layer_entry: bfloat16 [768, 50, 768], P('dp'), may hold values from -6 to 6
- caption_layer_entry: bfloat16 [768, 16, 768], P('dp'), may hold values from -6 to 6
- usable_match_tallies: int32 [16], P('dp'), may hold values from 1 to 48, 576 in all
- similarity_exponent_factor: float32 [1], replicated, may hold values from 3.6 to 4.2
- picture_standardize_factors: bfloat16 [2, 768], replicated, may hold values from 0.5 to 1.5
- picture_layer_offsets: bfloat16 [6, 768], replicated, may hold values from -0.59765625 to 0.59765625
- picture_inner_offset: bfloat16 [3072], replicated, may hold values from -1.1953125 to 1.1953125
- picture_attend_entry_matrix: bfloat16 [768, 2304], replicated, may hold values from -0.21875 to 0.21875
- picture_attend_exit_matrix: bfloat16 [768, 768], replicated, may hold values from -1.5 to 1.5
- picture_widening_matrix: bfloat16 [768, 3072], replicated, may hold values from -0.21875 to 0.21875
- picture_narrowing_matrix: bfloat16 [3072, 768], replicated, may hold values from -0.109375 to 0.109375
- caption_standardize_factors: bfloat16 [2, 768], replicated, may hold values from 0.5 to 1.5
- caption_layer_offsets: bfloat16 [6, 768], replicated, may hold values from -0.59765625 to 0.59765625
- caption_inner_offset: bfloat16 [3072], replicated, may hold values from -1.1953125 to 1.1953125
- caption_attend_entry_matrix: bfloat16 [768, 2304], replicated, may hold values from -0.21875 to 0.21875
- caption_attend_exit_matrix: bfloat16 [768, 768], replicated, may hold values from -0.875 to 0.875
- caption_widening_matrix: bfloat16 [768, 3072], replicated, may hold values from -0.21875 to 0.21875
- caption_narrowing_matrix: bfloat16 [3072, 768], replicated, may hold values from -0.109375 to 0.109375
Outputs:
- loss: float32 [1], replicated
- exponent_derivative: float32 [1], replicated
- grad_tokens: float32 [768, 16, 768], P('dp', 'tower')
- grad_gains: float32 [2, 768], P('tower', 'dp')
- grad_biases: float32 [6, 768], P('tower', 'dp')
- grad_hidbias: float32 [3072], P(('tower', 'dp'))
- grad_qkv: float32 [768, 2304], P('dp', 'tower')
- grad_project: float32 [768, 768], P('dp', 'tower')
- grad_expand: float32 [768, 3072], P('dp', 'tower')
- grad_reduce: float32 [3072, 768], P(('tower', 'dp'))
The draws below stay inside these ranges and needn't reach their ends.
Inputs may be any that keep to these rules, and one draw needn't show every extreme that they name: Index d of dp holds usable_match_tallies[d] valid pairs in its first slots of 48; the others are padding.
All inputs are finite; a program needn't handle non-finite values. No bound on the sum of `usable_match_tallies` on one device may be relied on, other than what follows from the above.
Results may differ from the reference program's by a relative error of at most 0.01.
The reference program's roundings to bfloat16 on the way count: a program that leaves them out, or rounds other values in their place, can miss the bound.
Values may be sent and summed in bfloat16 or wider, within the bound.
No kernel may reach another device: no remote copies, remote signals or barrier semaphores. Data moves between devices by JAX's collectives and lax.ppermute only.
A program may use at most 192 MiB of HBM per device.

```python
import math
import jax
import jax.numpy as jnp
import numpy as np
from jax import lax

D = 768
HEAD_DIM = 64
FF = 3072
IMG_LEN = 50
TXT_LEN = 16
PAIRS_DEV = 48
SHARDS = 16
PAIRS = 768


def steps_of(own_key, shape, pieces, least, largest):
    level, own = 1.0, jax.random.fold_in(own_key, 6)
    for position, blocks in pieces:
        heights = jnp.exp(jax.random.uniform(jax.random.fold_in(own, position), (blocks,), jnp.float32, least / len(pieces), largest / len(pieces)))
        level = level * jnp.repeat(heights, shape[position] // blocks).reshape([-1 if axis == position else 1 for axis in range(len(shape))])
    return level


def split_up(number_of, total, reach, skew):
    weights = [(1 << 20) // math.isqrt(grade ** skew) + 1 for grade in range(2, number_of + 1)]
    rest, holding = total - reach - (number_of - 1), [1] * (number_of - 1)
    while rest > 0:
        free = [i for i in range(number_of - 1) if holding[i] < reach]
        pool, left = sum([weights[i] for i in free]), rest
        for i in free:
            addition = min(reach - holding[i], max(1, left * weights[i] // pool), rest)
            holding[i] = holding[i] + addition
            rest = rest - addition
    return np.array([reach] + holding)


def uneven(own_key, number_of, total, limit, lean):
    if number_of == 2:
        one = jax.random.randint(own_key, (), max(1, total - limit), min(limit, total - 1) + 1)
        return jnp.stack([one, total - one])
    tallies = jnp.asarray(split_up(number_of, total, limit, lean), jnp.int32)
    pairs = (number_of - 1) // 2
    donor, taker = tallies[1:1 + 2 * pairs:2], tallies[2:2 + 2 * pairs:2]
    room = jnp.minimum(donor - 1, limit - taker)
    passed = jax.random.randint(jax.random.fold_in(own_key, 1), (pairs,), 0, 1 << 20) % (room + 1)
    tallies = tallies.at[1:1 + 2 * pairs:2].set(donor - passed).at[2:2 + 2 * pairs:2].set(taker + passed)
    return tallies[jax.random.permutation(jax.random.fold_in(own_key, 2), number_of)]


def normal_values(stream_key, extent, scale, reach, shards=(), kind=jnp.bfloat16):
    entries = jax.random.normal(stream_key, extent, jnp.float32) * scale
    if len(shards) > 0:
        entries = steps_of(stream_key, extent, shards, -0.22, 0.18) * entries
    return jnp.clip(entries, min=-reach, max=reach).astype(kind)


def setup_inputs(seed: int = 0) -> dict:
    streams_of = jax.random.split(jax.random.key(seed), 19)
    return {
        "picture_layer_entry": normal_values(streams_of[0], (PAIRS, IMG_LEN, D), 1.0, 6.0, ((0, 16),)),
        "caption_layer_entry": normal_values(streams_of[1], (PAIRS, TXT_LEN, D), 1.0, 6.0, ((0, 16),)),
        "usable_match_tallies": uneven(streams_of[2], SHARDS, 3 * PAIRS // 4, PAIRS_DEV, 1).astype(jnp.int32),
        "similarity_exponent_factor": jnp.clip(jax.random.uniform(streams_of[3], (1,), jnp.float32, 3.6, 4.2), 3.6, 4.2),
        "picture_standardize_factors": jnp.clip(1.0 + 0.1 * jax.random.normal(streams_of[4], (2, D), jnp.float32), 0.5, 1.5).astype(jnp.bfloat16),
        "picture_layer_offsets": normal_values(streams_of[5], (6, D), 0.1, 0.59765625),
        "picture_inner_offset": normal_values(streams_of[6], (FF,), 0.2, 1.1953125),
        "picture_attend_entry_matrix": normal_values(streams_of[7], (D, 3 * D), D ** -0.5, 0.21875),
        "picture_attend_exit_matrix": normal_values(streams_of[8], (D, D), (D // 49) ** -0.5, 1.5),
        "picture_widening_matrix": normal_values(streams_of[9], (D, FF), D ** -0.5, 0.21875),
        "picture_narrowing_matrix": normal_values(streams_of[10], (FF, D), FF ** -0.5, 0.109375),
        "caption_standardize_factors": jnp.clip(1.0 + 0.1 * jax.random.normal(streams_of[11], (2, D), jnp.float32), 0.5, 1.5).astype(jnp.bfloat16),
        "caption_layer_offsets": normal_values(streams_of[12], (6, D), 0.1, 0.59765625),
        "caption_inner_offset": normal_values(streams_of[13], (FF,), 0.2, 1.1953125),
        "caption_attend_entry_matrix": normal_values(streams_of[14], (D, 3 * D), D ** -0.5, 0.21875),
        "caption_attend_exit_matrix": normal_values(streams_of[15], (D, D), (D // 16) ** -0.5, 0.875),
        "caption_widening_matrix": normal_values(streams_of[16], (D, FF), D ** -0.5, 0.21875),
        "caption_narrowing_matrix": normal_values(streams_of[17], (FF, D), FF ** -0.5, 0.109375),
    }


@jax.custom_vjp
def low(v):
    return lax.optimization_barrier(v.astype(jnp.bfloat16)).astype(jnp.float32)

@jax.custom_vjp
def low_back(v):
    return v

def low_keep(v):
    return (low(v), None)

def low_pass(kept, grad):
    return (grad,)

def back_keep(v):
    return (v, None)

def back_low(kept, grad):
    return (low(grad),)
low.defvjp(low_keep, low_pass)
low_back.defvjp(back_keep, back_low)
norm_eps = 1e-06
embed_eps = 1e-06

def multiplied_result(form, left, right):
    return jnp.einsum(form, left, right, precision=lax.Precision.HIGHEST, preferred_element_type=jnp.float32)

def layer_norm(hidden, gain, shift):
    row_mean = lax.optimization_barrier(jnp.mean(hidden, axis=-1, keepdims=True))
    centered = hidden - row_mean
    variance = lax.optimization_barrier(jnp.mean(centered * centered, axis=-1, keepdims=True))
    return centered * lax.rsqrt(variance + norm_eps) * gain + shift

def block(hidden, gain_rows, biases, hidbias, w_qkv, w_proj, w_expand, w_reduce):
    batch_size, length, features = hidden.shape
    head_count = features // HEAD_DIM
    normed = low(layer_norm(hidden, gain_rows[0], biases[0]))
    qkv_bias = jnp.concatenate([biases[2], jnp.zeros_like(biases[2]), biases[3]])
    qkv_all = low(low_back(multiplied_result('bsd,de->bse', normed, w_qkv) + qkv_bias))
    qkv_split = qkv_all.reshape(batch_size, length, 3, head_count, HEAD_DIM)
    queries = qkv_split[:, :, 0]
    key_part = qkv_split[:, :, 1]
    values = qkv_split[:, :, 2]
    scores = low_back(multiplied_result('bqhe,bkhe->bhqk', queries, key_part) * HEAD_DIM ** (-0.5))
    attn_probs = jax.nn.softmax(scores, axis=-1)
    mixed_out = low(low_back(multiplied_result('bhqk,bkhe->bqhe', low(attn_probs), values)))
    attended = multiplied_result('bsd,de->bse', mixed_out.reshape(batch_size, length, features), w_proj) + biases[4]
    middle = hidden + low_back(attended)
    normed_two = low(layer_norm(middle, gain_rows[1], biases[1]))
    inner_pre = low_back(multiplied_result('bsd,df->bsf', normed_two, w_expand) + hidbias)
    active = low(jax.nn.gelu(inner_pre, approximate=False))
    branch = multiplied_result('bsf,fd->bsd', active, w_reduce) + biases[5]
    return middle + low_back(branch)

def embed_rows(output):
    pooled = lax.optimization_barrier(jnp.mean(output, axis=1))
    return low(pooled * lax.rsqrt(lax.optimization_barrier(jnp.sum(pooled * pooled, axis=-1, keepdims=True)) + embed_eps))

def reference(picture_layer_entry, caption_layer_entry, usable_match_tallies, similarity_exponent_factor, picture_standardize_factors, picture_layer_offsets, picture_inner_offset, picture_attend_entry_matrix, picture_attend_exit_matrix, picture_widening_matrix, picture_narrowing_matrix, caption_standardize_factors, caption_layer_offsets, caption_inner_offset, caption_attend_entry_matrix, caption_attend_exit_matrix, caption_widening_matrix, caption_narrowing_matrix):
    image_set = (picture_standardize_factors.astype(jnp.float32), picture_layer_offsets.astype(jnp.float32), picture_inner_offset.astype(jnp.float32), picture_attend_entry_matrix.astype(jnp.float32), picture_attend_exit_matrix.astype(jnp.float32), picture_widening_matrix.astype(jnp.float32), picture_narrowing_matrix.astype(jnp.float32))

    def image_group(tokens):
        return embed_rows(block(tokens.astype(jnp.float32), *image_set))
    picture_batch = lax.map(image_group, picture_layer_entry.reshape(SHARDS, PAIRS_DEV, IMG_LEN, D)).reshape(PAIRS, D)
    slot_ids = jnp.arange(PAIRS, dtype=jnp.int32)
    valid = slot_ids % PAIRS_DEV < usable_match_tallies[slot_ids // PAIRS_DEV]
    row_valid = valid.astype(jnp.float32)
    caption_entry_lines = caption_layer_entry.astype(jnp.float32)
    caption_parameter_bundle = (caption_standardize_factors.astype(jnp.float32), caption_layer_offsets.astype(jnp.float32), caption_inner_offset.astype(jnp.float32), caption_attend_entry_matrix.astype(jnp.float32), caption_attend_exit_matrix.astype(jnp.float32), caption_widening_matrix.astype(jnp.float32), caption_narrowing_matrix.astype(jnp.float32))

    def paired_matching_loss(tokens_all, warmth_exponent, gain_rows, biases, hidbias, w_qkv, w_proj, w_expand, w_reduce):
        weight_set = (gain_rows, biases, hidbias, w_qkv, w_proj, w_expand, w_reduce)
        group_fn = jax.checkpoint(lambda tokens, weights_in: embed_rows(block(tokens, *weights_in)))

        def step_fn(carry, tokens):
            return (carry, group_fn(tokens, weight_set))
        _, caption_batch = lax.scan(step_fn, jnp.float32(0.0), tokens_all.reshape(SHARDS, PAIRS_DEV, TXT_LEN, D))
        caption_batch = caption_batch.reshape(PAIRS, D)
        similarity_multiplier = jnp.exp(warmth_exponent[0])
        caption_raw_scores = low_back(similarity_multiplier * multiplied_result('oq,fq->of', caption_batch, picture_batch))
        picture_raw_scores = low_back(similarity_multiplier * multiplied_result('oq,fq->of', picture_batch, caption_batch))

        def side_term(raw_scores_matrix):
            masked = jnp.where(valid[None, :], raw_scores_matrix, -1000000000.0)
            log_total = jax.scipy.special.logsumexp(masked, axis=1)
            return jnp.sum(row_valid * (log_total - jnp.diagonal(raw_scores_matrix)))
        return 0.5 * (side_term(caption_raw_scores) + side_term(picture_raw_scores))
    loss_overall, reverse_mode_rule = jax.vjp(paired_matching_loss, caption_entry_lines, similarity_exponent_factor.astype(jnp.float32), *caption_parameter_bundle)
    grads = reverse_mode_rule(jnp.ones((), jnp.float32))
    count_total = jnp.sum(usable_match_tallies).astype(jnp.float32)
    loss = (loss_overall / count_total).reshape(1)
    return (loss, grads[1], grads[0], grads[2], grads[3], grads[4], grads[5], grads[6], grads[7], grads[8])
```

```python
from functools import partial

import jax
import jax.numpy as jnp
import numpy as np
from jax import lax
from jax.experimental import pallas as pl
from jax.experimental.pallas import tpu as pltpu
from jax.sharding import PartitionSpec as P

F32 = jnp.float32
BF16 = jnp.bfloat16
HEAD_DIM = 64
LANES = 128
norm_eps = 1e-06
embed_eps = 1e-06
NEG = -1000000000.0
VMEM_LIMIT = 60 * 1024 * 1024
CDF_Q = (
    7.97884942e-01,
    3.63330840e-02,
    -3.25942309e-05,
    -5.53065609e-05,
    3.96482302e-06,
    -1.32270645e-07,
    1.75640958e-09,
)


def normal_cdf(x):
    sq = x * x
    q = CDF_Q[-1] * sq + CDF_Q[-2]
    for coef in CDF_Q[-3::-1]:
        q = q * sq + coef
    return 0.5 + 0.5 * jnp.tanh(x * q)


def dot(a, b):
    return jnp.dot(a, b, preferred_element_type=F32)


def dot_nt(a, b):
    return lax.dot_general(a, b, (((1,), (1,)), ((), ())), preferred_element_type=F32)


def dot_tn(a, b):
    return lax.dot_general(a, b, (((0,), (0,)), ((), ())), preferred_element_type=F32)


def norm_stats(x):
    mean = jnp.mean(x, axis=-1, keepdims=True)
    centered = x - mean
    rstd = lax.rsqrt(jnp.mean(centered * centered, axis=-1, keepdims=True) + norm_eps)
    return centered * rstd, rstd


def norm_back(dxhat, xhat, rstd):
    return rstd * (
        dxhat
        - jnp.mean(dxhat, axis=-1, keepdims=True)
        - xhat * jnp.mean(dxhat * xhat, axis=-1, keepdims=True)
    )


def row(ref, i):
    return ref[i : i + 1, :].astype(F32)


def head_masks():
    lane = lax.broadcasted_iota(jnp.int32, (1, LANES), 1)
    first = (lane < HEAD_DIM).astype(BF16)
    return first, (1 - first).astype(BF16)


def two_heads(x, masks):
    return jnp.concatenate([x * masks[0], x * masks[1]], axis=0)


def softmax_parts(scores, bias):
    keys = scores.shape[1] // 2
    parts = []
    for e in range(2):
        s = scores[:, e * keys : (e + 1) * keys] + bias
        parts.append(jnp.exp(s - jnp.max(s, axis=-1, keepdims=True)))
    return parts


def attend(q2, k2, v2, bias, masks):
    e0, e1 = softmax_parts(dot_nt(q2 * BF16(0.125), two_heads(k2, masks)), bias)
    weights = jnp.concatenate([e0.astype(BF16), e1.astype(BF16)], axis=1)
    ones = jnp.ones((k2.shape[0], LANES), BF16)
    right = jnp.concatenate([two_heads(v2, masks), two_heads(ones, masks)], axis=1)
    out = dot(weights, right)
    return (out[:, :LANES] / out[:, LANES:]).astype(BF16)


def split_dot(x, w):
    hi = x.astype(BF16)
    lo = (x - hi.astype(F32)).astype(BF16)
    n = x.shape[0]
    out = dot(jnp.concatenate([hi, lo], axis=0), w)
    return out[:n] + out[n:]


def text_forward_kernel(
    scal, h_any, gains, biases, hid, wq_any, wp_any, we_any, wr_any,
    a_out, qkv_out, o_out, m_out, c_out, gp_out, gs_out, emb_out, r_out,
    h_v, wq, wp, we, wr, av, cv, gsum, sems,
):
    n, width = m_out.shape
    caps = emb_out.shape[0]
    length = n // caps
    hidden = hid.shape[1]
    t = scal[0]
    copies = [
        pltpu.make_async_copy(h_any.at[pl.ds(pl.multiple_of(t * n, n), n)], h_v, sems.at[0]),
        pltpu.make_async_copy(wq_any, wq, sems.at[1]),
        pltpu.make_async_copy(wp_any, wp, sems.at[2]),
        pltpu.make_async_copy(we_any, we, sems.at[3]),
        pltpu.make_async_copy(wr_any, wr, sems.at[4]),
    ]
    for c in copies:
        c.start()
    copies[0].wait()
    masks = head_masks()
    blocks = width // a_out.shape[1]

    def put_transposed(out, value):
        turned = value.T.astype(BF16)
        rows = out.shape[1]
        for e in range(out.shape[0]):
            out[scal[4 + e]] = turned[e * rows : (e + 1) * rows, :]

    h = h_v[...].astype(F32)
    xhat, _ = norm_stats(h)
    a = xhat * row(gains, 0) + row(biases, 0)
    av[...] = a.astype(BF16)
    copies[1].wait()
    zero = jnp.zeros((1, width), F32)
    qkv_bias = (row(biases, 2), zero, row(biases, 3))
    for j in range(3 * width // 256):
        part, off = divmod(j * 256, width)
        bias = qkv_bias[part][:, off : off + 256]
        qkv_out[:, j * 256 : (j + 1) * 256] = (
            dot(av[...], wq[:, j * 256 : (j + 1) * 256]) + bias
        ).astype(BF16)
    put_transposed(a_out, a)
    same = (
        lax.broadcasted_iota(jnp.int32, (LANES, LANES), 0) // length
        == lax.broadcasted_iota(jnp.int32, (LANES, LANES), 1) // length
    )
    bias = jnp.where(same, 0.0, -1e30)

    def attention(g, carry):
        rows = pl.ds(pl.multiple_of(g * LANES, LANES), LANES)
        for p in range(width // LANES):
            lanes = slice(p * LANES, (p + 1) * LANES)
            q2 = qkv_out[rows, lanes]
            k2 = qkv_out[rows, width + p * LANES : width + (p + 1) * LANES]
            v2 = qkv_out[rows, 2 * width + p * LANES : 2 * width + (p + 1) * LANES]
            av[rows, lanes] = attend(q2, k2, v2, bias, masks)
        return carry

    lax.fori_loop(0, n // LANES, attention, 0)
    copies[2].wait()
    m = h + dot(av[...], wp[...]) + row(biases, 4)
    m_out[...] = m
    xhat, _ = norm_stats(m)
    c = xhat * row(gains, 1) + row(biases, 1)
    cv[...] = c.astype(BF16)
    copies[3].wait()

    def feed(j, carry):
        cols = pl.ds(pl.multiple_of(j * 256, 256), 256)
        f = dot(cv[...], we[:, cols]) + hid[:, cols].astype(F32)
        cdf = normal_cdf(f)
        density = jnp.exp(f * f * -0.5) * 0.3989422804014327
        gp_out[:, cols] = (cdf + f * density).astype(BF16)
        gelu = f * cdf
        gsum[:, cols] = jnp.sum(gelu.reshape(caps, length, 256), axis=1)
        return carry

    lax.fori_loop(0, hidden // 256, feed, 0)
    put_transposed(c_out, c)
    put_transposed(o_out, av[...].astype(F32))
    copies[4].wait()
    total = gsum[...]
    pooled = (
        jnp.mean(m_out[...].reshape(caps, length, width), axis=1)
        + split_dot(total * (1.0 / length), wr[...])
        + row(biases, 5)
    )
    r = lax.rsqrt(jnp.sum(pooled * pooled, axis=-1, keepdims=True) + embed_eps)
    emb_out[...] = pooled * r
    r_out[...] = jnp.broadcast_to(r, r_out.shape)
    gs_out[...] = (total * r).astype(BF16)


PAD = 56


def image_forward_kernel(
    scal, x_any, emb, r, gains, biases, hid, wq_any, wp_any, we_any, wr_any,
    out,
    x_v, hv, av, qkv, mv, msum, gsum, wq, wp, we, wr, sems,
):
    caps, length, width = x_v.shape
    n = caps * PAD
    hidden = hid.shape[1]
    t = scal[0]
    copies = [
        pltpu.make_async_copy(x_any.at[pl.ds(t * caps, caps)], x_v, sems.at[0]),
        pltpu.make_async_copy(wq_any, wq, sems.at[1]),
        pltpu.make_async_copy(wp_any, wp, sems.at[2]),
        pltpu.make_async_copy(we_any, we, sems.at[3]),
        pltpu.make_async_copy(wr_any, wr, sems.at[4]),
    ]
    for c in copies:
        c.start()
    masks = head_masks()
    qkv[n:, :] = jnp.zeros((qkv.shape[0] - n, 3 * width), BF16)
    copies[0].wait()

    def first_norm(j, carry):
        base = pl.multiple_of(j * 2 * PAD, 16)
        for e in range(2):
            x = x_v[j * 2 + e].astype(F32)
            x = jnp.concatenate([x, jnp.zeros((PAD - length, width), F32)], axis=0)
            hv[pl.ds(base + e * PAD, PAD), :] = x
        h = hv[pl.ds(base, 2 * PAD), :]
        xhat, _ = norm_stats(h)
        av[pl.ds(base, 2 * PAD), :] = (xhat * row(gains, 0) + row(biases, 0)).astype(BF16)
        return carry

    lax.fori_loop(0, caps // 2, first_norm, 0)
    copies[1].wait()
    zero = jnp.zeros((1, width), F32)
    qkv_bias = (row(biases, 2), zero, row(biases, 3))
    for j in range(3 * width // 256):
        part, off = divmod(j * 256, width)
        qkv[:n, j * 256 : (j + 1) * 256] = (
            dot(av[...], wq[:, j * 256 : (j + 1) * 256]) + qkv_bias[part][:, off : off + 256]
        ).astype(BF16)
    q_at = lax.broadcasted_iota(jnp.int32, (2 * PAD, LANES), 0)
    k_at = lax.broadcasted_iota(jnp.int32, (2 * PAD, LANES), 1)
    low = (q_at < PAD) & (k_at < length)
    high = (q_at >= PAD) & (k_at >= PAD) & (k_at < PAD + length)
    bias = jnp.where(low | high, 0.0, -1e30)

    def attention(j, carry):
        base = pl.multiple_of(j * 2 * PAD, 16)
        rows, keys = pl.ds(base, 2 * PAD), pl.ds(base, LANES)
        for p in range(width // LANES):
            lanes = slice(p * LANES, (p + 1) * LANES)
            q2 = qkv[rows, lanes]
            k2 = qkv[keys, width + p * LANES : width + (p + 1) * LANES]
            v2 = qkv[keys, 2 * width + p * LANES : 2 * width + (p + 1) * LANES]
            av[rows, lanes] = attend(q2, k2, v2, bias, masks)
        return carry

    lax.fori_loop(0, caps // 2, attention, 0)
    copies[2].wait()
    for j in range(width // 256):
        cols = slice(j * 256, (j + 1) * 256)
        mv[:, cols] = hv[:, cols] + dot(av[...], wp[:, cols]) + row(biases, 4)[:, cols]
    group = 8 * PAD
    tail = (lax.broadcasted_iota(jnp.int32, (1, 8, 1), 1) < length - (PAD - 8)).astype(F32)

    def token_sum(x, count):
        tiles = x.reshape(count, PAD // 8, 8, x.shape[1])
        acc = tiles[:, PAD // 8 - 1] * tail
        for i in range(PAD // 8 - 1):
            acc = acc + tiles[:, i]
        return jnp.sum(acc, axis=1)

    def second_norm(j, carry):
        rows = pl.ds(pl.multiple_of(j * group, 16), group)
        m = mv[rows, :]
        xhat, _ = norm_stats(m)
        av[rows, :] = (xhat * row(gains, 1) + row(biases, 1)).astype(BF16)
        msum[pl.ds(pl.multiple_of(j * 8, 8), 8), :] = token_sum(m, 8)
        return carry

    lax.fori_loop(0, caps // 8, second_norm, 0)
    copies[3].wait()

    def feed(j, carry):
        cols = pl.ds(pl.multiple_of(j * 256, 256), 256)
        f = dot(av[...], we[:, cols]) + hid[:, cols].astype(F32)
        gsum[:, cols] = token_sum(f * normal_cdf(f), caps)
        return carry

    lax.fori_loop(0, hidden // 256, feed, 0)
    copies[4].wait()
    scale = 1.0 / length
    pooled = msum[...] * scale + split_dot(gsum[...] * scale, wr[...]) + row(biases, 5)
    r_img = lax.rsqrt(jnp.sum(pooled * pooled, axis=-1, keepdims=True) + embed_eps)
    out[:, :width] = (pooled * r_img).astype(BF16)
    out[:, width : 2 * width] = emb[...].astype(BF16)
    rv = r[...]
    hi = rv.astype(BF16)
    mid = (rv - hi.astype(F32)).astype(BF16)
    lo = (rv - hi.astype(F32) - mid.astype(F32)).astype(BF16)
    lane = lax.broadcasted_iota(jnp.int32, rv.shape, 1)
    slot = lax.broadcasted_iota(jnp.int32, rv.shape, 0) + t * caps
    flag = jnp.where(slot < scal[2], 1.0, 0.0)
    extra = jnp.where(lane == 0, hi.astype(F32), 0.0)
    extra = jnp.where(lane == 1, mid.astype(F32), extra)
    extra = jnp.where(lane == 2, lo.astype(F32), extra)
    extra = jnp.where(lane == 3, flag, extra)
    out[:, 2 * width :] = extra.astype(BF16)


def loss_kernel(
    rows_block, scal, own_any, par_any, expo, emb, r, gall, gains, biases,
    gp_any, ct_any, m_any, we_any, wr_any,
    loss_out, temp_out, keep_out, send_out, dm_out, red_out, vec_out,
    own_v, par_v, texts, images, extra, col_flag, sims, grad_t, grad_i, dt_v, dt_own,
    gp, ct, mv, we, wr, dc, exp_s, sems,
):
    chips, caps, _ = own_any.shape
    staged = own_v.shape[0] == chips
    total, width = texts.shape
    hidden = gp.shape[1]
    n = mv.shape[0]
    length = n // caps
    t, d = scal[0], scal[1]
    loads = [
        pltpu.make_async_copy(src, dst, sems.at[i])
        for i, (src, dst) in enumerate(
            ((own_any, own_v), (par_any, par_v), (wr_any, wr), (we_any, we), (gp_any, gp),
             (ct_any, ct), (m_any, mv))
        )
        if staged or i > 1
    ]
    for c in loads:
        c.start()
    if staged:
        loads[0].wait()
        loads[1].wait()
        loads = loads[2:]
    first = (jnp.zeros((1, 1), jnp.int32) + t) == 0

    def place(e, carry):
        slot = scal[4 + 16 + e]
        if not staged:
            for i, (src, dst) in enumerate(((own_any, own_v), (par_any, par_v))):
                one = pltpu.make_async_copy(src.at[pl.ds(slot, 1)], dst, sems.at[i])
                one.start()
                one.wait()
            slot = 0
        x0 = own_v[slot].astype(F32)
        x1 = par_v[slot].astype(F32)
        both = jnp.concatenate([jnp.where(first, x0, x1), jnp.where(first, x1, x0)], axis=0)
        rows = pl.ds(pl.multiple_of(e * 2 * caps, 16), 2 * caps)
        images[rows, :] = both[:, :width].astype(BF16)
        texts[rows, :] = both[:, width : 2 * width].astype(BF16)
        extra[rows, :] = both[:, 2 * width :]
        return carry

    lax.fori_loop(0, chips, place, 0)
    pick = (lax.broadcasted_iota(jnp.int32, (8, LANES), 1) == 3).astype(F32)
    step = min(256, total)

    def flags(j, carry):
        cols = pl.ds(pl.multiple_of(j * step, step), step)
        col_flag[:, cols] = dot_nt(pick, extra[cols, :])
        return carry

    lax.fori_loop(0, total // step, flags, 0)
    scale = jnp.exp(jnp.full((1, 1), expo[0], F32))
    chunk = 48
    blocks = total // rows_block

    def similarities(b):
        base = pl.multiple_of(b * rows_block, 16)

        def cols_step(j, carry):
            cols = pl.ds(pl.multiple_of(j * step, step), step)
            sims[:, cols] = scale * dot_nt(texts[pl.ds(base, rows_block), :], images[cols, :])
            return carry

        lax.fori_loop(0, total // step, cols_step, 0)

    def chunk_at(b, i):
        local = pl.ds(pl.multiple_of(i * chunk, 16), chunk)
        whole = pl.ds(pl.multiple_of(b * rows_block + i * chunk, 16), chunk)
        return local, whole

    per_block = rows_block // chunk
    col_max = jnp.full((1, total), NEG, F32)
    col_sum = jnp.zeros((1, total), F32)

    def column_block(b, carry):
        cm, cs = carry
        similarities(b)

        def peak(i, best):
            local, whole = chunk_at(b, i)
            live = extra[whole, 3:4] > 0.0
            return jnp.maximum(
                best, jnp.max(jnp.where(live, sims[local, :], NEG), axis=0, keepdims=True)
            )

        new = lax.fori_loop(0, per_block, peak, cm)

        def adding(i, acc):
            local, whole = chunk_at(b, i)
            live = extra[whole, 3:4] > 0.0
            return acc + jnp.sum(
                jnp.exp(jnp.where(live, sims[local, :], NEG) - new), axis=0, keepdims=True
            )

        return new, lax.fori_loop(0, per_block, adding, cs * jnp.exp(cm - new))

    if blocks == 1:
        col_max, col_sum = column_block(0, (col_max, col_sum))
    else:
        col_max, col_sum = lax.fori_loop(0, blocks, column_block, (col_max, col_sum))
    col_live = col_flag[0:1, :] > 0.0
    col_half = 0.5 * col_flag[0:1, :]
    col_lse = col_max + jnp.log(col_sum)
    inv_col = 1.0 / col_sum

    def row_block(b, carry):
        if blocks > 1:
            similarities(b)

        def rows_step(i, acc):
            loss, temp, rb = acc
            local, whole = chunk_at(b, i)
            s = sims[local, :]
            flag = extra[whole, 3:4]
            at = lax.broadcasted_iota(jnp.int32, (chunk, total), 0) + (b * rows_block + i * chunk)
            eye = (at == lax.broadcasted_iota(jnp.int32, (chunk, total), 1)).astype(F32)
            masked = jnp.where(col_live, s, NEG)
            top = jnp.max(masked, axis=1, keepdims=True)
            expd = jnp.exp(masked - top)
            rsum = jnp.sum(expd, axis=1, keepdims=True)
            gt = (0.5 * flag * (expd * (1.0 / rsum) - eye)).astype(BF16)
            expc = jnp.exp(jnp.where(flag > 0.0, s, NEG) - col_max) * inv_col
            gi = (col_half * (expc - eye)).astype(BF16)
            grad_t[local, :] = gt
            grad_i[local, :] = gi
            both = gt.astype(F32) + gi.astype(F32)
            temp = temp + jnp.sum(both * s, axis=0, keepdims=True)
            diag = jnp.sum(eye * s, axis=1, keepdims=True)
            loss = loss + flag * (0.5 * (top + jnp.log(rsum)) - diag)
            return loss, temp, rb

        loss, temp, rb = lax.fori_loop(0, per_block, rows_step, carry)
        dt_v[...] = scale * (dot(grad_t[...], images[...]) + dot(grad_i[...], images[...]))

        def project(i, rb):
            local, whole = chunk_at(b, i)
            dt = dt_v[local, :]
            tx = texts[whole, :].astype(F32)
            part = (dt - tx * jnp.sum(tx * dt, axis=1, keepdims=True)) * (1.0 / length)
            part = part.astype(BF16)
            texts[whole, :] = part
            inv = extra[whole, 0:1] + extra[whole, 1:2] + extra[whole, 2:3]
            return rb + jnp.sum(part.astype(F32) * inv, axis=0, keepdims=True)

        rb = lax.fori_loop(0, per_block, project, rb)
        mine = d * (2 * caps) + t * caps - b * rows_block

        @pl.when((mine >= 0) & (mine < rows_block))
        def _():
            dt_own[...] = dt_v[pl.ds(pl.multiple_of(mine, 8), caps), :]

        return loss, temp, rb

    start = (jnp.zeros((chunk, 1), F32), jnp.zeros((1, total), F32), jnp.zeros((1, width), F32))
    if blocks == 1:
        loss, temp, rb = row_block(0, start)
    else:
        loss, temp, rb = lax.fori_loop(0, blocks, row_block, start)
    objective = jnp.sum(loss, axis=0, keepdims=True) + jnp.sum(
        col_half * col_lse, axis=1, keepdims=True
    )
    valid_count = jnp.sum(col_flag[0:1, :], axis=1, keepdims=True)
    loss_out[...] = jnp.broadcast_to(objective / valid_count, loss_out.shape)
    temp_out[...] = jnp.broadcast_to(jnp.sum(temp, axis=1, keepdims=True), temp_out.shape)

    tx = emb[...]
    dt = dt_own[...]
    dy = r[:, 0:1] * (dt - tx * jnp.sum(tx * dt, axis=1, keepdims=True)) * (1.0 / length)
    dyb = dy.astype(BF16)
    for c in loads[:4]:
        c.wait()
    dc[...] = jnp.zeros_like(dc)

    def feed(j, carry):
        cols = pl.ds(pl.multiple_of(j * 256, 256), 256)
        dg = dot_nt(dyb, wr[cols, :])
        df = gp[:, cols].astype(F32).reshape(caps, length, 256) * dg[:, None, :]
        df = df.reshape(n, 256).astype(BF16)
        per_row = width // 256
        vec_out[pl.ds(4 + j // per_row, 1), pl.ds(pl.multiple_of((j % per_row) * 256, 256), 256)] = (
            jnp.sum(df.astype(F32), axis=0, keepdims=True)
        )
        dc[...] += dot_nt(df, we[:, cols])
        half = hidden // 512
        out_cols = pl.ds(pl.multiple_of((j % half) * 256, 256), 256)
        exp_s[j // half, :, out_cols] = dot(ct[...].reshape(width, n), df).astype(BF16)
        return carry

    lax.fori_loop(0, hidden // 256, feed, 0)
    stores = [
        pltpu.make_async_copy(exp_s.at[t], keep_out, sems.at[0]),
        pltpu.make_async_copy(exp_s.at[1 - t], send_out, sems.at[1]),
    ]
    for c in stores:
        c.start()
    red_out[...] = dot_tn(gall[...], texts[...])
    loads[4].wait()
    xhat, rstd = norm_stats(mv[...])
    dcv = dc[...]
    vec_out[0:1, :] = jnp.sum(dcv * xhat, axis=0, keepdims=True)
    vec_out[1:2, :] = jnp.sum(dcv, axis=0, keepdims=True)
    back = norm_back(dcv * row(gains, 1), xhat, rstd)
    dm = (back.reshape(caps, length, width) + dy[:, None, :]).reshape(n, width)
    dm_out[...] = dm
    vec_out[2:3, :] = jnp.sum(dm.astype(BF16).astype(F32), axis=0, keepdims=True)
    vec_out[3:4, :] = rb * float(length)
    for c in stores:
        c.wait()


def attention_back_kernel(
    scal, dm, h_any, gains, biases, qkv, at, ot, wp_any, wq_any,
    keep_out, send_out, tok_keep, tok_send, vec_out,
    h_v, wp, wq, dmb, dov, dqkv, grads, sems,
):
    n, width = dm.shape
    caps, half_len, _ = tok_keep.shape
    length = 2 * half_len
    t = scal[0]
    loads = [
        pltpu.make_async_copy(wp_any, wp, sems.at[0]),
        pltpu.make_async_copy(wq_any, wq, sems.at[1]),
        pltpu.make_async_copy(h_any.at[pl.ds(pl.multiple_of(t * n, n), n)], h_v, sems.at[2]),
    ]
    for c in loads:
        c.start()
    masks = head_masks()
    same = (
        lax.broadcasted_iota(jnp.int32, (LANES, LANES), 0) // length
        == lax.broadcasted_iota(jnp.int32, (LANES, LANES), 1) // length
    )
    bias = jnp.where(same, 0.0, -1e30)
    dmb[...] = dm[...].astype(BF16)
    loads[0].wait()
    dov[...] = dot_nt(dmb[...], wp[...]).astype(BF16)

    def attention(g, carry):
        rows = pl.ds(pl.multiple_of(g * LANES, LANES), LANES)
        for p in range(width // LANES):
            lanes = slice(p * LANES, (p + 1) * LANES)
            k_lanes = slice(width + p * LANES, width + (p + 1) * LANES)
            v_lanes = slice(2 * width + p * LANES, 2 * width + (p + 1) * LANES)
            q2 = qkv[rows, lanes] * BF16(0.125)
            km = two_heads(qkv[rows, k_lanes], masks)
            vm = two_heads(qkv[rows, v_lanes], masks)
            do2 = dov[rows, lanes]
            parts = softmax_parts(dot_nt(q2, km), bias)
            dp = dot_nt(do2, vm)
            pb, ds = [], []
            for e in range(2):
                prob = parts[e] * (1.0 / jnp.sum(parts[e], axis=-1, keepdims=True))
                dpe = dp[:, e * LANES : (e + 1) * LANES]
                inner = jnp.sum(prob * dpe, axis=-1, keepdims=True)
                pb.append(prob.astype(BF16))
                ds.append((prob * (dpe - inner)).astype(BF16))
            dqkv[rows, lanes] = (dot(jnp.concatenate(ds, axis=1), km) * 0.125).astype(BF16)
            dqkv[rows, k_lanes] = dot_tn(jnp.concatenate(ds, axis=0), two_heads(q2, masks)).astype(
                BF16
            )
            dqkv[rows, v_lanes] = dot_tn(
                jnp.concatenate(pb, axis=0), two_heads(do2, masks)
            ).astype(BF16)
        return carry

    lax.fori_loop(0, n // LANES, attention, 0)
    half = width // 2
    otv = ot[...].reshape(width, n)
    atv = at[...].reshape(width, n)
    for hh in range(2):
        grads[hh, :, :half] = dot(otv, dmb[:, hh * half : (hh + 1) * half]).astype(BF16)
        for j in range(3):
            src = hh * 3 * half + j * half
            grads[hh, :, (j + 1) * half : (j + 2) * half] = dot(
                atv, dqkv[:, src : src + half]
            ).astype(BF16)
    stores = [
        pltpu.make_async_copy(grads.at[t], keep_out, sems.at[3]),
        pltpu.make_async_copy(grads.at[1 - t], send_out, sems.at[4]),
    ]
    for c in stores:
        c.start()
    loads[1].wait()
    loads[2].wait()
    da = dot_nt(dqkv[...], wq[...])
    xhat, rstd = norm_stats(h_v[...].astype(F32))
    vec_out[0:1, :] = jnp.sum(da * xhat, axis=0, keepdims=True)
    vec_out[1:2, :] = jnp.sum(da, axis=0, keepdims=True)
    vec_out[2:3, :] = jnp.sum(dqkv[:, :width].astype(F32), axis=0, keepdims=True)
    vec_out[3:4, :] = jnp.sum(dqkv[:, 2 * width :].astype(F32), axis=0, keepdims=True)
    vec_out[4:8, :] = jnp.zeros((4, width), F32)
    grad = dm[...] + norm_back(da * row(gains, 0), xhat, rstd)
    halves = grad.reshape(caps, 2, half_len, width)
    first = (jnp.zeros((1, 1, 1), jnp.int32) + t) == 0
    tok_keep[...] = jnp.where(first, halves[:, 0], halves[:, 1])
    tok_send[...] = jnp.where(first, halves[:, 1], halves[:, 0]).astype(BF16)
    for c in stores:
        c.wait()


def xor_permute(x, axis, bit):
    return lax.ppermute(x, axis, [(i, i ^ bit) for i in range(lax.axis_size(axis))])


def bit_groups(count):
    bits = [1 << i for i in range(count.bit_length() - 1)]
    groups = [tuple(bits[i : i + 2]) for i in range(0, len(bits), 2)]
    return groups[::-1]


def reaches(group):
    out = [0]
    for bit in group:
        out = out + [r ^ bit for r in out]
    return out


def slot_reaches(count):
    order = [0]
    for group in bit_groups(count):
        order = [r ^ o for r in reaches(group) for o in order]
    return order


def gather_slots(x, count):
    y = x[None]
    for group in bit_groups(count):
        y = jnp.concatenate(
            [y if r == 0 else xor_permute(y, "dp", r) for r in reaches(group)], axis=0
        )
    return y


def scatter_sum(s, count, to_wire, from_wire):
    for group in reversed(bit_groups(count)):
        hops = reaches(group)
        rows = s.shape[0] // len(hops)
        parts = [s[i * rows : (i + 1) * rows] for i in range(len(hops))]
        moved = [xor_permute(to_wire(parts[i]), "dp", r) for i, r in enumerate(hops) if r]
        s = parts[0]
        for piece in moved:
            s = s + from_wire(piece)
    return s


def flip_by(x, index, count):
    for i in range(count.bit_length() - 1):
        bit = 1 << i
        shape = x.shape
        pairs = x.reshape((count // (2 * bit), 2, bit) + shape[1:])
        x = jnp.where((index & bit) != 0, pairs[:, ::-1], pairs).reshape(shape)
    return x


SMEM = pl.BlockSpec(memory_space=pltpu.SMEM)
VMEM = pl.BlockSpec(memory_space=pltpu.VMEM)
ANY = pl.BlockSpec(memory_space=pl.ANY)


def call(kernel, name, in_specs, outs, out_specs, scratch, args, flops, moved):
    return pl.pallas_call(
        kernel,
        name=name,
        in_specs=in_specs,
        out_shape=[jax.ShapeDtypeStruct(s, d) for s, d in outs],
        out_specs=out_specs,
        scratch_shapes=scratch,
        compiler_params=pltpu.CompilerParams(vmem_limit_bytes=VMEM_LIMIT),
        cost_estimate=pl.CostEstimate(flops=flops, bytes_accessed=moved, transcendentals=0),
    )(*args)


def body(
    pictures, captions, tallies, exponent,
    p_gains, p_biases, p_hid, p_wq, p_wp, p_we, p_wr,
    c_gains, c_biases, c_hid, c_wq, c_wp, c_we, c_wr,
):
    t = lax.axis_index("tower")
    d = lax.axis_index("dp")
    chips = lax.axis_size("dp")
    pairs, length, width = captions.shape
    img_len = pictures.shape[1]
    hidden = c_hid.shape[0]
    caps = pairs // 2
    n = caps * length
    total = pairs * chips
    row_blocks = 16
    order = np.array(slot_reaches(chips))
    slot_of = np.zeros(chips, np.int32)
    slot_of[order] = np.arange(chips)
    table = np.stack([slot_of[np.arange(chips) ^ i] for i in range(chips)]).astype(np.int32)
    slots = lax.dynamic_slice_in_dim(jnp.asarray(table), d, 1, 0)[0]
    relative = chips == row_blocks
    row_slots = slots if relative else jnp.arange(row_blocks, dtype=jnp.int32)
    head = jnp.stack([t, d, tallies[0], t]).astype(jnp.int32)
    scal = jnp.concatenate([head, row_slots, slots])

    texts_in = captions.reshape(pairs * length, width)
    c_hid2, p_hid2 = c_hid.reshape(1, hidden), p_hid.reshape(1, hidden)
    blk = (row_blocks, width // row_blocks, n)
    vm = pltpu.VMEM
    a_t, qkv, o_t, m, c_t, gp, gs, emb, r = call(
        text_forward_kernel, "text_forward",
        [SMEM, ANY, VMEM, VMEM, VMEM, ANY, ANY, ANY, ANY],
        [(blk, BF16), ((n, 3 * width), BF16), (blk, BF16), ((n, width), F32), (blk, BF16),
         ((n, hidden), BF16), ((caps, hidden), BF16), ((caps, width), F32), ((caps, LANES), F32)],
        [VMEM] * 9,
        [vm((n, width), BF16), vm((width, 3 * width), BF16), vm((width, width), BF16),
         vm((width, hidden), BF16), vm((hidden, width), BF16), vm((n, width), BF16),
         vm((n, width), BF16), vm((caps, hidden), F32), pltpu.SemaphoreType.DMA((5,))],
        (scal, texts_in, c_gains, c_biases, c_hid2, c_wq, c_wp, c_we, c_wr),
        int(2 * n * width * (4 * width + hidden)), 20_000_000,
    )

    share = hidden // (2 * chips)
    pieces = jnp.transpose(gs.reshape(caps, 2, chips, share), (2, 0, 1, 3))
    pieces = lax.all_to_all(pieces, "dp", 0, 0, tiled=True)
    g_mine = jnp.where(t == 0, pieces[:, :, 0], pieces[:, :, 1])
    g_other = jnp.where(t == 0, pieces[:, :, 1], pieces[:, :, 0])
    g_back = xor_permute(g_other, "tower", 1)
    g_all = jnp.concatenate(
        [jnp.where(t == 0, g_mine, g_back), jnp.where(t == 0, g_back, g_mine)], axis=1
    ).reshape(total, share)

    rows = caps * PAD
    (payload,) = call(
        image_forward_kernel, "image_forward",
        [SMEM, ANY, VMEM, VMEM, VMEM, VMEM, VMEM, ANY, ANY, ANY, ANY],
        [((caps, 2 * width + LANES), BF16)],
        [VMEM],
        [vm((caps, img_len, width), BF16), vm((rows, width), F32), vm((rows, width), BF16),
         vm((rows + 16, 3 * width), BF16), vm((rows, width), F32), vm((caps, width), F32),
         vm((caps, hidden), F32), vm((width, 3 * width), BF16), vm((width, width), BF16),
         vm((width, hidden), BF16), vm((hidden, width), BF16), pltpu.SemaphoreType.DMA((5,))],
        (scal, pictures, emb, r, p_gains, p_biases, p_hid2, p_wq, p_wp, p_we, p_wr),
        int(2 * rows * width * (4 * width + hidden)), 20_000_000,
    )
    own_all = gather_slots(payload, chips)
    par_all = xor_permute(own_all, "tower", 1)

    block = total if total <= 768 else 96
    staging = (chips if total <= 768 else 1,) + payload.shape
    loss, temp, e_keep, e_send, dm, reduce_grad, vec_ff = call(
        partial(loss_kernel, block), "loss_and_feed_back",
        [SMEM, ANY, ANY, SMEM, VMEM, VMEM, VMEM, VMEM, VMEM, ANY, ANY, ANY, ANY, ANY],
        [((8, LANES), F32), ((8, LANES), F32), ((width, hidden // 2), BF16),
         ((width, hidden // 2), BF16), ((n, width), F32), ((share, width), F32), ((8, width), F32)],
        [VMEM, VMEM, ANY, ANY, VMEM, VMEM, VMEM],
        [vm(staging, BF16), vm(staging, BF16), vm((total, width), BF16),
         vm((total, width), BF16), vm((total, LANES), F32), vm((8, total), F32),
         vm((block, total), F32), vm((block, total), BF16), vm((block, total), BF16),
         vm((block, width), F32), vm((caps, width), F32),
         vm((n, hidden), BF16), vm(blk, BF16), vm((n, width), F32), vm((width, hidden), BF16),
         vm((hidden, width), BF16), vm((n, width), F32), vm((2, width, hidden // 2), BF16),
         pltpu.SemaphoreType.DMA((7,))],
        (scal, own_all, par_all, exponent, emb, r, g_all, c_gains, c_biases, gp, c_t, m, c_we, c_wr),
        int(4 * n * width * hidden), 20_000_000,
    )

    q_keep, q_send, tok_keep, tok_send, vec_at = call(
        attention_back_kernel, "attention_back",
        [SMEM, VMEM, ANY, VMEM, VMEM, VMEM, VMEM, VMEM, ANY, ANY],
        [((width, 2 * width), BF16), ((width, 2 * width), BF16),
         ((caps, length // 2, width), F32), ((caps, length // 2, width), BF16), ((8, width), F32)],
        [ANY, ANY, VMEM, VMEM, VMEM],
        [vm((n, width), BF16), vm((width, width), BF16), vm((width, 3 * width), BF16),
         vm((n, width), BF16), vm((n, width), BF16), vm((n, 3 * width), BF16),
         vm((2, width, 2 * width), BF16), pltpu.SemaphoreType.DMA((5,))],
        (scal, dm, texts_in, c_gains, c_biases, qkv, a_t, o_t, c_wp, c_wq),
        int(2 * n * width * 8 * width), 20_000_000,
    )

    def by_slot(x):
        if relative:
            return x
        x = flip_by(x.reshape((chips, width // chips) + x.shape[1:]), d, chips)
        return x[order].reshape((width,) + x.shape[2:])

    e_back = xor_permute(e_send, "tower", 1)
    e_sum = by_slot(e_keep.astype(F32) + e_back.astype(F32))
    expand_grad = scatter_sum(e_sum, chips, lambda x: x.astype(BF16), lambda x: x.astype(F32))

    tok_back = xor_permute(tok_send, "tower", 1).astype(F32)
    grad_tokens = jnp.concatenate(
        [jnp.where(t == 0, tok_keep, tok_back), jnp.where(t == 0, tok_back, tok_keep)], axis=0
    )

    zero = jnp.zeros((1, width), F32)
    for_zero = jnp.concatenate([vec_at[0:2], vec_ff[1:2], vec_at[2:3], vec_ff[4:6]])
    for_one = jnp.concatenate([vec_ff[0:1], vec_at[3:4], vec_ff[2:3], zero, vec_ff[6:8]])
    v_keep = jnp.where(t == 0, for_zero, for_one)
    v_send = jnp.where(t == 0, for_one, for_zero)
    v_sum = v_keep + xor_permute(v_send, "tower", 1)
    cols = width // chips
    lead = jnp.transpose(v_sum[:4].reshape(4, chips, cols), (1, 2, 0))
    tail = jnp.transpose(v_sum[4:].reshape(chips, 2, cols), (0, 2, 1))
    small = jnp.concatenate([lead, tail], axis=2)
    small = flip_by(small, d, chips)[order].reshape(width, 6)
    small = jnp.pad(small, ((0, 0), (0, LANES // 2 - 6)))

    q_back = xor_permute(q_send, "tower", 1)
    q_sum = by_slot(q_keep.astype(F32) + q_back.astype(F32))
    wide = q_sum.shape[1]
    q_full = jnp.concatenate([q_sum, small], axis=1)

    def q_to_wire(x):
        hi = x.astype(BF16)
        s = x[:, wide:]
        lo = (s - s.astype(BF16).astype(F32)).astype(BF16)
        return jnp.concatenate([hi, lo], axis=1)

    def q_from_wire(x):
        y = x.astype(F32)
        return jnp.concatenate([y[:, :wide], y[:, wide : wide + 64] + y[:, wide + 64 :]], axis=1)

    q_grad = scatter_sum(q_full, chips, q_to_wire, q_from_wire)
    half = width // 2
    project_grad, qkv_grad = q_grad[:, :half], q_grad[:, half:wide]
    small = q_grad[:, wide : wide + 6]
    gains_grad = small[:, 0].reshape(1, cols)
    rbias = lax.dynamic_slice_in_dim(vec_ff[3], d * cols, cols, 0)
    last = jnp.where(t == 0, small[:, 3], rbias)
    biases_grad = jnp.stack([small[:, 1], small[:, 2], last])
    hid_grad = small[:, 4:6].T.reshape(2 * cols)
    return (
        loss[0, :1], temp[0, :1], grad_tokens, gains_grad, biases_grad, hid_grad,
        qkv_grad, project_grad, expand_grad, reduce_grad,
    )


def solution(mesh):
    in_specs = (P("dp", None, None), P("dp", None, None), P("dp")) + (P(),) * 15
    out_specs = (
        P(), P(), P("dp", "tower", None), P("tower", "dp"), P("tower", "dp"),
        P(("tower", "dp")), P("dp", "tower"), P("dp", "tower"), P("dp", "tower"),
        P(("tower", "dp"), None),
    )
    return jax.shard_map(body, mesh=mesh, in_specs=in_specs, out_specs=out_specs, check_vma=False)
```

```python
from functools import partial

import jax
import jax.numpy as jnp
import numpy as np
from jax import lax
from jax.experimental import pallas as pl
from jax.experimental.pallas import tpu as pltpu
from jax.sharding import PartitionSpec as P

F32 = jnp.float32
BF16 = jnp.bfloat16
HEAD_DIM = 64
LANES = 128
EXTRA = 120
norm_eps = 1e-06
embed_eps = 1e-06
NEG = -1000000000.0
VMEM_LIMIT = 60 * 1024 * 1024


def normal_cdf(x):
    return 0.5 + 0.5 * lax.erf(x * 0.7071067811865476)


def load(src, dst, sem):
    copy = pltpu.make_async_copy(src, dst, sem)
    copy.start()
    return copy


def dot(a, b):
    return jnp.dot(a, b, preferred_element_type=F32)


def dot_nt(a, b):
    return lax.dot_general(a, b, (((1,), (1,)), ((), ())), preferred_element_type=F32)


def dot_tn(a, b):
    return lax.dot_general(a, b, (((0,), (0,)), ((), ())), preferred_element_type=F32)


def norm_stats(x):
    mean = jnp.mean(x, axis=-1, keepdims=True)
    centered = x - mean
    rstd = lax.rsqrt(jnp.mean(centered * centered, axis=-1, keepdims=True) + norm_eps)
    return centered * rstd, rstd


def norm_back(dxhat, xhat, rstd):
    return rstd * (
        dxhat
        - jnp.mean(dxhat, axis=-1, keepdims=True)
        - xhat * jnp.mean(dxhat * xhat, axis=-1, keepdims=True)
    )


def row(ref, i):
    return ref[i : i + 1, :].astype(F32)


def head_masks():
    lane = lax.broadcasted_iota(jnp.int32, (1, LANES), 1)
    first = (lane < HEAD_DIM).astype(BF16)
    return first, (1 - first).astype(BF16)


def two_heads(x, masks):
    return jnp.concatenate([x * masks[0], x * masks[1]], axis=0)


def softmax_parts(scores, bias):
    keys = scores.shape[1] // 2
    parts = []
    for e in range(2):
        s = scores[:, e * keys : (e + 1) * keys] + bias
        parts.append(jnp.exp(s - jnp.max(s, axis=-1, keepdims=True)))
    return parts


def attend(q2, k2, v2, bias, masks):
    e0, e1 = softmax_parts(dot_nt(q2 * BF16(0.125), two_heads(k2, masks)), bias)
    weights = jnp.concatenate([e0.astype(BF16), e1.astype(BF16)], axis=1)
    ones = jnp.ones((k2.shape[0], LANES), BF16)
    right = jnp.concatenate([two_heads(v2, masks), two_heads(ones, masks)], axis=1)
    out = dot(weights, right)
    return (out[:, :LANES] / out[:, LANES:]).astype(BF16)


def split_dot(x, w):
    hi = x.astype(BF16)
    lo = (x - hi.astype(F32)).astype(BF16)
    n = x.shape[0]
    out = dot(jnp.concatenate([hi, lo], axis=0), w)
    return out[:n] + out[n:]


def text_forward_kernel(
    scal, h_any, gains, biases, hid, wq_any, wp_any, we_any, wr_any,
    a_any, qkv_any, o_any, m_any, c_any, gpk_any, gps_any, send_out, emb_out, r_out,
    h_v, wq, wp, we, wr, av, cv, gsum, a_out, qkv_out, o_out, m_out, c_out, gp_keep, gp_send,
    sems, out_sems,
):
    n, width = m_out.shape
    caps = emb_out.shape[0]
    length = n // caps
    hidden = hid.shape[1]
    t, d = scal[0], scal[1]
    load_h = load(h_any.at[pl.ds(pl.multiple_of(t * n, n), n)], h_v, sems.at[0])
    load_q = load(wq_any, wq, sems.at[1])
    load_h.wait()
    masks = head_masks()

    def put_transposed(out, value):
        turned = value.T.astype(BF16)
        rows = out.shape[1]
        for e in range(out.shape[0]):
            out[scal[4 + e]] = turned[e * rows : (e + 1) * rows, :]

    h = h_v[...].astype(F32)
    xhat, _ = norm_stats(h)
    a = xhat * row(gains, 0) + row(biases, 0)
    av[...] = a.astype(BF16)
    load_q.wait()
    load_p = load(wp_any, wp, sems.at[2])
    load_e = load(we_any, we, sems.at[3])
    load_r = load(wr_any, wr, sems.at[4])
    zero = jnp.zeros((1, width), F32)
    qkv_bias = (row(biases, 2), zero, row(biases, 3))
    for j in range(3 * width // 256):
        part, off = divmod(j * 256, width)
        bias = qkv_bias[part][:, off : off + 256]
        qkv_out[:, j * 256 : (j + 1) * 256] = (
            dot(av[...], wq[:, j * 256 : (j + 1) * 256]) + bias
        ).astype(BF16)
    put_transposed(a_out, a)
    stores = [load(qkv_out, qkv_any, out_sems.at[0]), load(a_out, a_any, out_sems.at[1])]
    same = (
        lax.broadcasted_iota(jnp.int32, (LANES, LANES), 0) // length
        == lax.broadcasted_iota(jnp.int32, (LANES, LANES), 1) // length
    )
    bias = jnp.where(same, 0.0, -1e30)

    def attention(g, carry):
        rows = pl.ds(pl.multiple_of(g * LANES, LANES), LANES)
        for p in range(width // LANES):
            lanes = slice(p * LANES, (p + 1) * LANES)
            q2 = qkv_out[rows, lanes]
            k2 = qkv_out[rows, width + p * LANES : width + (p + 1) * LANES]
            v2 = qkv_out[rows, 2 * width + p * LANES : 2 * width + (p + 1) * LANES]
            av[rows, lanes] = attend(q2, k2, v2, bias, masks)
        return carry

    lax.fori_loop(0, n // LANES, attention, 0)
    load_p.wait()
    m = h_v[...].astype(F32) + dot(av[...], wp[...]) + row(biases, 4)
    m_out[...] = m
    stores.append(load(m_out, m_any, out_sems.at[2]))
    xhat, _ = norm_stats(m)
    c = xhat * row(gains, 1) + row(biases, 1)
    cv[...] = c.astype(BF16)
    put_transposed(c_out, c)
    put_transposed(o_out, av[...].astype(F32))
    stores.append(load(c_out, c_any, out_sems.at[3]))
    stores.append(load(o_out, o_any, out_sems.at[4]))
    load_e.wait()
    half = hidden // 512

    def feed(rel, gp_out):
        def step(j, carry):
            local = pl.ds(pl.multiple_of(j * 256, 256), 256)
            at = jnp.bitwise_xor(t, rel) * half + j
            cols = pl.ds(pl.multiple_of(at * 256, 256), 256)
            f = dot(cv[...], we[:, cols]) + hid[:, cols].astype(F32)
            cdf = normal_cdf(f)
            density = jnp.exp(f * f * -0.5) * 0.3989422804014327
            gp_out[:, local] = (cdf + f * density).astype(BF16)
            gsum[:, cols] = jnp.sum((f * cdf).reshape(caps, length, 256), axis=1)
            return carry

        lax.fori_loop(0, half, step, 0, unroll=2)

    feed(1, gp_send)
    stores.append(load(gp_send, gps_any, out_sems.at[5]))
    feed(0, gp_keep)
    stores.append(load(gp_keep, gpk_any, out_sems.at[6]))
    load_r.wait()
    total = gsum[...]
    pooled = (
        jnp.mean(m_out[...].reshape(caps, length, width), axis=1)
        + split_dot(total * (1.0 / length), wr[...])
        + row(biases, 5)
    )
    r = lax.rsqrt(jnp.sum(pooled * pooled, axis=-1, keepdims=True) + embed_eps)
    emb_out[...] = pooled * r
    r_out[...] = jnp.broadcast_to(r, r_out.shape)
    chips = send_out.shape[0]
    share = hidden // (2 * chips)
    scaled = total * r
    hi = r.astype(BF16).astype(F32)
    mid = (r - hi).astype(BF16).astype(F32)
    slot = lax.broadcasted_iota(jnp.int32, (caps, LANES), 0) + t * caps
    lane = lax.broadcasted_iota(jnp.int32, (caps, LANES), 1)
    extra = jnp.where(lane == EXTRA, hi, 0.0)
    extra = jnp.where(lane == EXTRA + 1, mid, extra)
    extra = jnp.where(lane == EXTRA + 2, r - hi - mid, extra)
    extra = jnp.where((lane == EXTRA + 3) & (slot < scal[2]), 1.0, extra)
    for e in range(chips):
        send_out[e, :, :width] = (pooled * r).astype(BF16)
        for half_at in range(2):
            src = (half_at * chips + e) * share
            piece = jnp.concatenate([scaled[:, src : src + share], extra[:, share:]], axis=1)
            to = width + jnp.bitwise_xor(t, half_at) * LANES
            send_out[e, :, pl.ds(pl.multiple_of(to, LANES), LANES)] = piece.astype(BF16)
    for c in stores:
        c.wait()


PAD = 56


def image_forward_kernel(
    scal, x_any, gains, biases, hid, wq_any, wp_any, we_any, wr_any,
    out,
    x_v, xs, hv, av, qkv, mv, msum, gsum, wq, wp, we, wr, sems,
):
    length, both_caps, width = x_v.shape
    caps = both_caps // 2
    n = caps * PAD
    hidden = hid.shape[1]
    t = scal[0]
    load_x = load(x_any, x_v, sems.at[0])
    load_q = load(wq_any, wq, sems.at[1])
    masks = head_masks()
    qkv[n:, :] = jnp.zeros((qkv.shape[0] - n, 3 * width), BF16)
    first = (jnp.zeros((1, 1), jnp.int32) + t) == 0
    load_x.wait()

    def pick(i, carry):
        x = x_v[i].astype(F32)
        x = jnp.where(first, x[:caps], x[caps:])
        for k in range(width // LANES):
            xs[k, pl.ds(pl.multiple_of(i * caps, 8), caps), :] = x[:, k * LANES : (k + 1) * LANES]
        return carry

    lax.fori_loop(0, length, pick, 0, unroll=2)

    def first_norm(j, carry):
        base = pl.multiple_of(j * 2 * PAD, 16)
        for e in range(2):
            x = jnp.concatenate(
                [
                    xs[k, pl.ds(j * 2 + e, length, stride=caps), :]
                    for k in range(width // LANES)
                ],
                axis=1,
            )
            x = jnp.concatenate([x, jnp.zeros((PAD - length, width), F32)], axis=0)
            hv[pl.ds(base + e * PAD, PAD), :] = x
            xhat, _ = norm_stats(x)
            x = xhat * row(gains, 0) + row(biases, 0)
            if e == 0:
                kept = x
        av[pl.ds(base, 2 * PAD), :] = jnp.concatenate([kept, x], axis=0).astype(BF16)
        return carry

    lax.fori_loop(0, caps // 2, first_norm, 0, unroll=4)
    load_q.wait()
    load_p = load(wp_any, wp, sems.at[2])
    load_e = load(we_any, we, sems.at[3])
    load_r = load(wr_any, wr, sems.at[4])
    zero = jnp.zeros((1, width), F32)
    qkv_bias = (row(biases, 2), zero, row(biases, 3))
    for j in range(3 * width // 256):
        part, off = divmod(j * 256, width)
        qkv[:n, j * 256 : (j + 1) * 256] = (
            dot(av[...], wq[:, j * 256 : (j + 1) * 256]) + qkv_bias[part][:, off : off + 256]
        ).astype(BF16)
    q_at = lax.broadcasted_iota(jnp.int32, (2 * PAD, LANES), 0)
    k_at = lax.broadcasted_iota(jnp.int32, (2 * PAD, LANES), 1)
    low = (q_at < PAD) & (k_at < length)
    high = (q_at >= PAD) & (k_at >= PAD) & (k_at < PAD + length)
    bias = jnp.where(low | high, 0.0, -1e30)

    def attention(j, carry):
        base = pl.multiple_of(j * 2 * PAD, 16)
        rows, keys = pl.ds(base, 2 * PAD), pl.ds(base, LANES)
        for p in range(width // LANES):
            lanes = slice(p * LANES, (p + 1) * LANES)
            q2 = qkv[rows, lanes]
            k2 = qkv[keys, width + p * LANES : width + (p + 1) * LANES]
            v2 = qkv[keys, 2 * width + p * LANES : 2 * width + (p + 1) * LANES]
            av[rows, lanes] = attend(q2, k2, v2, bias, masks)
        return carry

    lax.fori_loop(0, caps // 2, attention, 0, unroll=2)
    load_p.wait()
    for j in range(width // 256):
        cols = slice(j * 256, (j + 1) * 256)
        mv[:, cols] = hv[:, cols] + dot(av[...], wp[:, cols]) + row(biases, 4)[:, cols]
    group = 8 * PAD
    tail = (lax.broadcasted_iota(jnp.int32, (1, 8, 1), 1) < length - (PAD - 8)).astype(F32)

    def token_sum(x, count):
        tiles = x.reshape(count, PAD // 8, 8, x.shape[1])
        acc = tiles[:, PAD // 8 - 1] * tail
        for i in range(PAD // 8 - 1):
            acc = acc + tiles[:, i]
        return jnp.sum(acc, axis=1)

    def second_norm(j, carry):
        rows = pl.ds(pl.multiple_of(j * group, 16), group)
        m = mv[rows, :]
        xhat, _ = norm_stats(m)
        av[rows, :] = (xhat * row(gains, 1) + row(biases, 1)).astype(BF16)
        msum[pl.ds(pl.multiple_of(j * 8, 8), 8), :] = token_sum(m, 8)
        return carry

    lax.fori_loop(0, caps // 8, second_norm, 0)
    load_e.wait()

    def feed(j, carry):
        cols = pl.ds(pl.multiple_of(j * 256, 256), 256)
        f = dot(av[...], we[:, cols]) + hid[:, cols].astype(F32)
        gsum[:, cols] = token_sum(f * normal_cdf(f), caps)
        return carry

    lax.fori_loop(0, hidden // 256, feed, 0, unroll=2)
    load_r.wait()
    scale = 1.0 / length
    pooled = msum[...] * scale + split_dot(gsum[...] * scale, wr[...]) + row(biases, 5)
    r_img = lax.rsqrt(jnp.sum(pooled * pooled, axis=-1, keepdims=True) + embed_eps)
    out[...] = (pooled * r_img).astype(BF16)


QUARTERS = ((1, 3), (2, 3), (0, 2), (0, 1))


def loss_kernel(
    rows_block, parts, scal, *refs,
):
    own_any, refs = refs[:parts], refs[parts:]
    (par_any, text_any, text_par_any, expo, emb, r, gpk_any, gpr_any, ct_any, ctr_any,
     we_any, wr_any,
     loss_out, temp_out, ea, eb, ec, ed, g_any, images_any, texts_any, gall_any, extra_any,
     dc_any, dy_out, hid_out,
     own_v, par_v, text_v, text_par_v, texts, images, extra, gall, col_flag, sims, grad,
     chip_g, gpk, gpr, ct, we, wr, dc, exp_s, sems, out_sems) = refs
    chips, caps, width = par_any.shape
    staged = own_v.shape[0] == chips
    total = texts.shape[0]
    near_hidden = gpk.shape[1]
    n = dc.shape[0]
    length = n // caps
    t, d = scal[0], scal[1]
    first = (jnp.zeros((1, 1), jnp.int32) + t) == 0
    if staged:
        each = chips // parts
        waits = [
            load(par_any, par_v, sems.at[0]),
            load(text_any, text_v, sems.at[1]),
            load(text_par_any, text_par_v, sems.at[2]),
        ] + [
            load(own_any[i], own_v.at[pl.ds(i * each, each)], sems.at[3 + i]) for i in range(parts)
        ]
        for c in waits:
            c.wait()

    def place(e, carry):
        at, slot = e, scal[4 + 16 + e]
        if not staged:
            waits = [
                load(src.at[pl.ds(i, 1)], dst, sems.at[j])
                for j, (src, i, dst) in enumerate(
                    ((own_any[0], slot, own_v), (par_any, slot, par_v), (text_any, at, text_v),
                     (text_par_any, at, text_par_v))
                )
            ]
            for c in waits:
                c.wait()
            at = slot = 0

        def pair(x0, x1):
            x0, x1 = x0.astype(F32), x1.astype(F32)
            return jnp.concatenate([jnp.where(first, x0, x1), jnp.where(first, x1, x0)], axis=0)

        rows = pl.ds(pl.multiple_of(e * 2 * caps, 16), 2 * caps)
        images[rows, :] = pair(own_v[slot], par_v[slot]).astype(BF16)
        x0, x1 = text_v[at], text_par_v[at]
        texts[rows, :] = pair(x0[:, :width], x1[:, :width]).astype(BF16)
        last = pair(x0[:, width : width + LANES], x1[:, width + LANES :])
        extra[rows, :] = last
        gall[rows, :] = last.astype(BF16)
        return carry

    lax.fori_loop(0, chips, place, 0, unroll=2)
    half = near_hidden // 256
    later = [
        load(src, dst, sems.at[8 + i])
        for i, (src, dst) in enumerate(
            ((wr_any.at[pl.ds(pl.multiple_of(t * near_hidden, 256), near_hidden)], wr),
             (gpk_any, gpk), (gpr_any, gpr),
             (we_any.at[:, pl.ds(pl.multiple_of(t * near_hidden, 256), near_hidden)], we))
        )
    ]
    for i, src in enumerate((ct_any, ctr_any)):
        later.append(load(src, ct.at[i], sems.at[12 + i]))
    stores = [
        load(src, dst, out_sems.at[i])
        for i, (src, dst) in enumerate(
            ((images, images_any), (texts, texts_any), (gall, gall_any), (extra, extra_any))
        )
    ]
    pick = (lax.broadcasted_iota(jnp.int32, (8, LANES), 1) == EXTRA + 3).astype(F32)
    step = min(256, total)

    def flags(j, carry):
        cols = pl.ds(pl.multiple_of(j * step, step), step)
        col_flag[:, cols] = dot_nt(pick, extra[cols, :])
        return carry

    lax.fori_loop(0, total // step, flags, 0)
    scale = jnp.exp(jnp.full((1, 1), expo[0], F32))
    chunk = 48
    blocks = total // rows_block
    per_block = rows_block // chunk
    live = col_flag[0:1, :]

    def similarities(b):
        base = pl.multiple_of(b * rows_block, 16)

        def cols_step(j, carry):
            cols = pl.ds(pl.multiple_of(j * step, step), step)
            sims[:, cols] = scale * dot_nt(texts[pl.ds(base, rows_block), :], images[cols, :])
            return carry

        lax.fori_loop(0, total // step, cols_step, 0)

    def chunk_at(b, i):
        local = pl.ds(pl.multiple_of(i * chunk, 16), chunk)
        whole = pl.ds(pl.multiple_of(b * rows_block + i * chunk, 16), chunk)
        return local, whole

    def column_block(b, acc):
        similarities(b)

        def adding(i, acc):
            local, whole = chunk_at(b, i)
            live_row = extra[whole, EXTRA + 3 : EXTRA + 4]
            part = jnp.exp(sims[local, :]) * live_row
            return acc + jnp.sum(part.reshape(chunk // 8, 8, total), axis=0)

        return lax.fori_loop(0, per_block, adding, acc, unroll=2)

    col_acc = jnp.zeros((8, total), F32)
    if blocks == 1:
        col_acc = column_block(0, col_acc)
    else:
        col_acc = lax.fori_loop(0, blocks, column_block, col_acc)
    col_sum = jnp.sum(col_acc, axis=0, keepdims=True)
    col_part = 0.5 * live / col_sum

    def row_block(b, carry):
        if blocks > 1:
            similarities(b)

        def rows_step(i, acc):
            loss, temp, diag = acc
            local, whole = chunk_at(b, i)
            s = sims[local, :]
            flag = extra[whole, EXTRA + 3 : EXTRA + 4]
            at = lax.broadcasted_iota(jnp.int32, (chunk, total), 0) + (b * rows_block + i * chunk)
            eye = at == lax.broadcasted_iota(jnp.int32, (chunk, total), 1)
            expd = jnp.exp(s)
            rsum = jnp.sum(expd * live, axis=1, keepdims=True)
            g = expd * ((0.5 * flag / rsum) * live + flag * col_part)
            g = g - jnp.where(eye, 0.5 * (flag + live), 0.0)
            grad[local, :] = g.astype(BF16)
            temp = temp + jnp.sum((g * s).reshape(chunk // 8, 8, total), axis=0)
            diag = diag + jnp.sum(
                jnp.where(eye, s * flag, 0.0).reshape(chunk // 8, 8, total), axis=0
            )
            return loss + 0.5 * flag * jnp.log(rsum), temp, diag

        carry = lax.fori_loop(0, per_block, rows_step, carry, unroll=2)
        mine = d * (2 * caps) - b * rows_block

        @pl.when((mine >= 0) & (mine < rows_block))
        def _():
            chip_g[...] = grad[pl.ds(pl.multiple_of(mine, 16), 2 * caps), :]

        if blocks > 1:
            rows = pl.ds(pl.multiple_of(b * rows_block, 16), rows_block)
            load(grad, g_any.at[rows], out_sems.at[4]).wait()
        return carry

    start = (jnp.zeros((chunk, 1), F32), jnp.zeros((8, total), F32), jnp.zeros((8, total), F32))
    if blocks == 1:
        loss, temp, diag = row_block(0, start)
        stores.append(load(grad, g_any, out_sems.at[4]))
    else:
        loss, temp, diag = lax.fori_loop(0, blocks, row_block, start)
    objective = jnp.sum(loss) + 0.5 * jnp.sum(live * jnp.log(col_sum)) - jnp.sum(diag)
    loss_out[0] = objective / jnp.sum(live)
    temp_out[0] = jnp.sum(temp)

    both_dt = scale * dot(chip_g[...], images[...])
    chip = pl.ds(pl.multiple_of(d * 2 * caps, 16), 2 * caps)
    inv = jnp.sum(extra[chip, EXTRA : EXTRA + 3], axis=1, keepdims=True)
    dt = jnp.where(first, both_dt[:caps], both_dt[caps:])
    dt_far = jnp.where(first, both_dt[caps:], both_dt[:caps])
    both_tx = texts[chip, :].astype(F32)
    tx_far = jnp.where(first, both_tx[caps:], both_tx[:caps])
    inv_far = jnp.where(first, inv[caps:], inv[:caps])

    def pooled_back(tx, dt, inv):
        return inv * (dt - tx * jnp.sum(tx * dt, axis=1, keepdims=True)) * (1.0 / length)

    dy = pooled_back(emb[...], dt, r[:, 0:1])
    dy_out[...] = dy
    dyb = jnp.concatenate([dy, pooled_back(tx_far, dt_far, inv_far)], axis=0).astype(BF16)
    for c in later:
        c.wait()
    dc[...] = jnp.zeros_like(dc)

    def near(j, carry):
        cols = pl.ds(pl.multiple_of(j * 256, 256), 256)
        dg = dot_nt(dyb, wr[cols, :])
        df = (gpk[:, cols].astype(F32).reshape(caps, length, 256) * dg[:caps][:, None, :]).reshape(
            n, 256
        )
        far = (gpr[:, cols].astype(F32).reshape(caps, length, 256) * dg[caps:][:, None, :]).reshape(
            n, 256
        )
        df, far = df.astype(BF16), far.astype(BF16)
        hid_out[0:1, cols] = jnp.sum(df.astype(F32) + far.astype(F32), axis=0, keepdims=True)
        dc[...] += dot_nt(df, we[:, cols])
        side = near_hidden // 512
        local = pl.ds(pl.multiple_of((j % side) * 256, 256), 256)
        exp_s[j // side, :, local] = (
            dot(ct[0].reshape(width, n), df) + dot(ct[1].reshape(width, n), far)
        ).astype(BF16)
        return carry

    lax.fori_loop(0, half, near, 0, unroll=2)
    quarter = width // 4
    for i, out in enumerate((ea, eb, ec, ed)):
        for j, q in enumerate(QUARTERS[i]):
            stores.append(
                load(
                    exp_s.at[i % 2, pl.ds(q * quarter, quarter)],
                    out.at[pl.ds(j * quarter, quarter)],
                    out_sems.at[5 + 2 * i + j],
                )
            )
    stores.append(load(dc, dc_any, out_sems.at[13]))
    for c in stores:
        c.wait()


def middle_back_kernel(
    scal, dc_any, dy, gps_any, m_any, gains, we_any, wr_any, wp_any, qkv_any,
    dm_any, dqkv_any, vec_out,
    dc, gps, mv, we, wr, wp, qkv, dm, dmb, dov, dqkv, sems,
):
    n, width = dm.shape
    caps = dy.shape[0]
    length = n // caps
    far_hidden = gps.shape[1]
    t = scal[0]
    away = pl.ds(pl.multiple_of((1 - t) * far_hidden, 256), far_hidden)
    waits = [
        load(src, dst, sems.at[i])
        for i, (src, dst) in enumerate(
            ((dc_any, dc), (gps_any, gps), (wr_any.at[away], wr), (we_any.at[:, away], we))
        )
    ]
    for c in waits:
        c.wait()
    load_m = load(m_any, mv, sems.at[4])
    load_p = load(wp_any, wp, sems.at[5])
    load_qkv = load(qkv_any, qkv, sems.at[6])
    dyv = dy[...]
    dyb = dyv.astype(BF16)

    def feed(j, carry):
        cols = pl.ds(pl.multiple_of(j * 256, 256), 256)
        dg = dot_nt(dyb, wr[cols, :])
        df = gps[:, cols].astype(F32).reshape(caps, length, 256) * dg[:, None, :]
        dc[...] += dot_nt(df.reshape(n, 256).astype(BF16), we[:, cols])
        return carry

    lax.fori_loop(0, far_hidden // 256, feed, 0, unroll=2)
    load_m.wait()
    piece = 8 * length

    def norm(i, sums):
        rows = pl.ds(pl.multiple_of(i * piece, piece), piece)
        xhat, rstd = norm_stats(mv[rows, :])
        dcv = dc[rows, :]
        back = norm_back(dcv * row(gains, 1), xhat, rstd)
        dy_rows = dy[pl.ds(pl.multiple_of(i * 8, 8), 8), :]
        out = (back.reshape(piece // length, length, width) + dy_rows[:, None, :]).reshape(
            piece, width
        )
        dm[rows, :] = out
        low = out.astype(BF16)
        dmb[rows, :] = low

        def fold(x):
            return jnp.sum(x.reshape(piece // 8, 8, width), axis=0)

        return sums[0] + fold(dcv * xhat), sums[1] + fold(dcv), sums[2] + fold(low.astype(F32))

    blank = jnp.zeros((8, width), F32)
    sums = lax.fori_loop(0, n // piece, norm, (blank, blank, blank))
    store_dm = load(dm, dm_any, sems.at[7])
    load_p.wait()
    dov[...] = dot_nt(dmb[...], wp[...]).astype(BF16)
    load_qkv.wait()
    masks = head_masks()
    same = (
        lax.broadcasted_iota(jnp.int32, (LANES, LANES), 0) // length
        == lax.broadcasted_iota(jnp.int32, (LANES, LANES), 1) // length
    )
    bias = jnp.where(same, 0.0, -1e30)

    def attention(g, carry):
        rows = pl.ds(pl.multiple_of(g * LANES, LANES), LANES)
        for p in range(width // LANES):
            lanes = slice(p * LANES, (p + 1) * LANES)
            k_lanes = slice(width + p * LANES, width + (p + 1) * LANES)
            v_lanes = slice(2 * width + p * LANES, 2 * width + (p + 1) * LANES)
            q2 = qkv[rows, lanes] * BF16(0.125)
            km = two_heads(qkv[rows, k_lanes], masks)
            vm = two_heads(qkv[rows, v_lanes], masks)
            do2 = dov[rows, lanes]
            parts = softmax_parts(dot_nt(q2, km), bias)
            dp = dot_nt(do2, vm)
            pb, ds = [], []
            for e in range(2):
                prob = parts[e] * (1.0 / jnp.sum(parts[e], axis=-1, keepdims=True))
                dpe = dp[:, e * LANES : (e + 1) * LANES]
                inner = jnp.sum(prob * dpe, axis=-1, keepdims=True)
                pb.append(prob.astype(BF16))
                ds.append((prob * (dpe - inner)).astype(BF16))
            dqkv[rows, lanes] = (dot(jnp.concatenate(ds, axis=1), km) * 0.125).astype(BF16)
            dqkv[rows, k_lanes] = dot_tn(jnp.concatenate(ds, axis=0), two_heads(q2, masks)).astype(
                BF16
            )
            dqkv[rows, v_lanes] = dot_tn(
                jnp.concatenate(pb, axis=0), two_heads(do2, masks)
            ).astype(BF16)
        return carry

    lax.fori_loop(0, n // LANES, attention, 0)
    store = load(dqkv, dqkv_any, sems.at[8])
    for i in range(3):
        vec_out[i : i + 1, :] = jnp.sum(sums[i], axis=0, keepdims=True)
    vec_out[3:4, :] = jnp.sum(dqkv[:, :width].astype(F32), axis=0, keepdims=True)
    vec_out[4:5, :] = jnp.sum(dqkv[:, 2 * width :].astype(F32), axis=0, keepdims=True)
    vec_out[5:8, :] = jnp.zeros((3, width), F32)
    store_dm.wait()
    store.wait()


def weight_grad_kernel(with_hid, scal, dm_any, dqkv_any, at_any, ot_any, wq_any, gains, biases, vec,
                       hid, *rest):
    keep_a, keep_b, send_a, send_b = rest[-14:-10]
    dm, at, ot, dmb, dqkv, wq, side_a, side_b, small, sems = rest[-10:]
    n, width = dm.shape
    t = scal[0]
    load_dm = load(dm_any, dm, sems.at[0])
    load_o = load(ot_any, ot, sems.at[1])
    load_qkv = load(dqkv_any, dqkv, sems.at[2])
    load_a = load(at_any, at, sems.at[3])
    blocks, block = at.shape[:2]
    loads_w = [
        load(wq_any.at[pl.ds(e * block, block)], wq.at[scal[4 + e]], sems.at[8 + e])
        for e in range(blocks)
    ]
    load_dm.wait()
    dmb[...] = dm[...].astype(BF16)
    load_o.wait()
    half, quarter = width // 2, width // 4
    otv = ot[...].reshape(width, n)

    def put(out, hh, side, cols, value):
        value = value.astype(BF16)
        for i in range(2):
            for j, q in enumerate(QUARTERS[side + 2 * i]):
                out[hh, i, j * quarter : (j + 1) * quarter, cols] = value[
                    q * quarter : (q + 1) * quarter
                ]

    for hh in range(2):
        put(side_a, hh, 0, slice(0, half), dot(otv, dmb[:, hh * half : (hh + 1) * half]))
    load_qkv.wait()
    load_a.wait()
    for c in loads_w:
        c.wait()
    atv = at[...].reshape(width, n)
    inner = jnp.zeros((width, LANES), F32)
    for hh in range(2):
        for i in range(3):
            col = (hh * 3 + i) * half
            value = dot(atv, dqkv[:, col : col + half])
            if i == 0:
                put(side_a, hh, 0, slice(half, width), value)
            else:
                put(side_b, hh, 1, slice((i - 1) * half, i * half), value)
            prod = value * wq[:, :, col : col + half].reshape(width, half).astype(F32)
            for k in range(half // LANES):
                inner = inner + prod[:, k * LANES : (k + 1) * LANES]
    inner = jnp.sum(inner, axis=1, keepdims=True)
    sums = jnp.sum(dqkv[...].astype(F32), axis=0, keepdims=True)
    hi = sums.astype(BF16)
    lo = (sums - hi.astype(F32)).astype(BF16)
    both = jnp.concatenate([hi, lo, jnp.zeros((14, 3 * width), BF16)], axis=0)
    shift1 = dot_nt(wq[...].reshape(width, 3 * width), both)
    shift1 = shift1[:, 0:1] + shift1[:, 1:2]
    first = (jnp.zeros((1, 1), jnp.int32) + t) == 0
    zero = jnp.zeros((1, width), F32)
    for_zero = jnp.concatenate([zero, zero, vec[1:2, :], vec[3:4, :], zero, zero], axis=0)
    for_one = jnp.concatenate([vec[0:1, :], vec[4:5, :], vec[2:3, :], zero, zero, zero], axis=0)
    ends = jnp.concatenate([1.0 / row(gains, 0), row(biases, 0)], axis=0)
    lines = jnp.concatenate([for_zero, ends, for_one, ends], axis=0).T
    lane = lax.broadcasted_iota(jnp.int32, (1, 8), 1)
    if with_hid:
        columns = jnp.broadcast_to(hid[...], (8, hid.shape[1])).T
    for e in range(blocks):
        at_block = slice(e * block, (e + 1) * block)
        if with_hid:
            pick = columns[2 * e * block : (2 * e + 1) * block] * (lane == 4).astype(F32)
            pick = pick + columns[(2 * e + 1) * block : (2 * e + 2) * block] * (lane == 5).astype(F32)
        else:
            pick = jnp.zeros((block, 8), F32)
        small[scal[4 + e]] = jnp.concatenate(
            [lines[at_block, :8], lines[at_block, 8:], pick,
             jnp.zeros((block, LANES - 24), F32)], axis=1
        )
    sv = small[...].reshape(width, LANES)
    zeros_set, ones_set, own = sv[:, :8], sv[:, 8:16], sv[:, 16:24]
    gain1 = zeros_set[:, 6:7] * (inner - zeros_set[:, 7:8] * shift1)
    zeros_set = zeros_set + gain1 * (lane == 0).astype(F32) + shift1 * (lane == 1).astype(F32)
    used = (lane < 4).astype(F32)
    zeros_set, ones_set = zeros_set * used, ones_set * used
    keep_set = jnp.where(first, zeros_set, ones_set) + own
    send_set = jnp.where(first, ones_set, zeros_set)
    for hh in range(2):
        value = jnp.where((jnp.zeros((1, 1), jnp.int32) + t) == hh, keep_set, send_set)
        hi = value.astype(BF16).astype(F32)
        fill = jnp.zeros((width, LANES // 2 - 8), F32)
        value = jnp.concatenate([hi, fill, value - hi, fill], axis=1)
        put(side_b, hh, 1, slice(width, width + LANES), value)
    stores = [
        load(side_a.at[t], keep_a, sems.at[4]),
        load(side_b.at[t], keep_b, sems.at[5]),
        load(side_a.at[1 - t], send_a, sems.at[6]),
        load(side_b.at[1 - t], send_b, sems.at[7]),
    ]
    for c in stores:
        c.wait()


def input_back_kernel(
    scal, dm_any, h_any, gains, dqkv_any, wq_any, order_any,
    tok_keep, tok_send,
    h_v, wq, dm, dqkv, da, sems,
):
    n, width = dm.shape
    caps, half_len, _ = tok_keep.shape
    t = scal[0]
    loads = [
        load(src, dst, sems.at[i])
        for i, (src, dst) in enumerate(
            ((dqkv_any, dqkv), (wq_any, wq),
             (h_any.at[pl.ds(pl.multiple_of(t * n, n), n)], h_v), (dm_any, dm))
        )
    ]
    loads[0].wait()
    loads[1].wait()
    da[...] = dot_nt(dqkv[...], wq[...])
    loads[2].wait()
    loads[3].wait()
    piece = 8 * 2 * half_len
    first = (jnp.zeros((1, 1, 1), jnp.int32) + t) == 0

    def norm(i, carry):
        rows = pl.ds(pl.multiple_of(i * piece, piece), piece)
        xhat, rstd = norm_stats(h_v[rows, :].astype(F32))
        grad = dm[rows, :] + norm_back(da[rows, :] * row(gains, 0), xhat, rstd)
        halves = grad.reshape(8, 2, half_len, width)
        at = pl.ds(pl.multiple_of(i * 8, 8), 8)
        tok_keep[at] = jnp.where(first, halves[:, 0], halves[:, 1])
        tok_send[at] = jnp.where(first, halves[:, 1], halves[:, 0]).astype(BF16)
        return carry

    lax.fori_loop(0, n // piece, norm, 0)


def reduce_grad_kernel(
    rows_block, length, expo, g_any, images_any, texts_any, gall_any, extra_any, order_any,
    red_out, bias_out,
    g_v, images, texts, gall, extra, acc, sems,
):
    total, width = images.shape
    blocks = total // rows_block
    share = red_out.shape[0]
    whole = load(images_any, images, sems.at[0])
    scale = jnp.exp(jnp.full((1, 1), expo[0], F32))
    acc[...] = jnp.zeros_like(acc)
    whole.wait()

    def block(b, rb):
        rows = pl.ds(pl.multiple_of(b * rows_block, 16), rows_block)
        waits = [
            load(src.at[rows], dst, sems.at[1 + i])
            for i, (src, dst) in enumerate(
                ((g_any, g_v), (texts_any, texts), (gall_any, gall), (extra_any, extra))
            )
        ]
        for c in waits:
            c.wait()
        dt = scale * dot(g_v[...], images[...])
        tx = texts[...].astype(F32)
        part = (dt - tx * jnp.sum(tx * dt, axis=1, keepdims=True)) * (1.0 / length)
        part = part.astype(BF16)
        acc[...] += dot_tn(gall[...], part)
        inv = jnp.sum(extra[:, EXTRA : EXTRA + 3], axis=1, keepdims=True)
        return rb + jnp.sum(part.astype(F32) * inv, axis=0, keepdims=True)

    rb = lax.fori_loop(0, blocks, block, jnp.zeros((1, width), F32))
    red_out[...] = acc[:share, :]
    bias_out[...] = jnp.broadcast_to(rb * float(length), bias_out.shape)


def to_wire(x, width):
    low = x.astype(BF16)
    if x.shape[1] == width:
        return low
    rest = x[:, width:] - low[:, width:].astype(F32)
    return jnp.concatenate([low, rest.astype(BF16)], axis=1)


def from_wire(x, width):
    y = x.astype(F32)
    if x.shape[1] == width:
        return y
    return jnp.concatenate([y[:, :width], y[:, width : width + 64] + y[:, width + 64 :]], axis=1)


def merge_kernel(width, sum_a, sum_b, hop_a, hop_b, *rest):
    outs = rest[-4:]
    for i, out in enumerate(outs):
        rows = out.shape[0]
        at = slice(i * rows, (i + 1) * rows)
        a = sum_a[at, :] + hop_a[at, :].astype(F32)
        b = sum_b[at, :] + from_wire(hop_b[at, :], width)
        if i == 0:
            out[:, :width] = a
            out[:, width:] = b
        else:
            out[:, :width] = a.astype(BF16)
            out[:, width:] = to_wire(b, width)


def finish_kernel(width, scal, total, hop_1, hop_2, hop_3, rbias,
                  qkv_out, project_out, gains_out, biases_out, hid_out):
    half = width // 2
    rows, cols = project_out.shape[0], width
    t, d = scal[0], scal[1]
    acc = total[...]
    for hop in (hop_1, hop_2, hop_3):
        x = hop[...]
        acc = acc + jnp.concatenate(
            [x[:, :width].astype(F32), from_wire(x[:, width:], width)], axis=1
        )
    project_out[...] = acc[:, :half]
    qkv_out[...] = acc[:, half : 2 * width]
    small = acc[:, 2 * width : 2 * width + 8].T
    lane = lax.broadcasted_iota(jnp.int32, (rows, cols), 1)
    mine = lax.broadcasted_iota(jnp.int32, (rows, cols), 0) + d * rows
    last = jnp.sum(jnp.where(lane == mine, rbias[0:1, :], 0.0), axis=1, keepdims=True)
    last = jnp.broadcast_to(last, (rows, 8)).T
    first = (jnp.zeros((1, 1), jnp.int32) + t) == 0
    gains_out[...] = small[0:1]
    biases_out[...] = jnp.concatenate(
        [small[1:3], jnp.where(first, small[3:4], last[0:1])], axis=0
    )
    hid_out[...] = small[4:6]


def xor_permute(x, axis, bit):
    return lax.ppermute(x, axis, [(i, i ^ bit) for i in range(lax.axis_size(axis))])


def bit_groups(count):
    bits = [1 << i for i in range(count.bit_length() - 1)]
    groups = [tuple(bits[i : i + 2]) for i in range(0, len(bits), 2)]
    return groups[::-1]


def reaches(group):
    out = [0]
    for bit in group:
        out = out + [r ^ bit for r in out]
    return out


def slot_reaches(count):
    order = [0]
    for group in bit_groups(count):
        order = [r ^ o for r in reaches(group) for o in order]
    return order


def hop(sends, group):
    return [x if r == 0 else xor_permute(x, "dp", r) for x, r in zip(sends, reaches(group))]


def scatter_sum(s, groups, to_wire=lambda x: x, from_wire=lambda x: x):
    for group in reversed(groups):
        hops = reaches(group)
        rows = s.shape[0] // len(hops)
        parts = [s[i * rows : (i + 1) * rows] for i in range(len(hops))]
        moved = [xor_permute(to_wire(parts[i]), "dp", r) for i, r in enumerate(hops) if r]
        s = parts[0]
        for piece in moved:
            s = s + from_wire(piece)
    return s


def flip_by(x, index, count):
    for i in range(count.bit_length() - 1):
        bit = 1 << i
        shape = x.shape
        pairs = x.reshape((count // (2 * bit), 2, bit) + shape[1:])
        x = jnp.where((index & bit) != 0, pairs[:, ::-1], pairs).reshape(shape)
    return x


SMEM = pl.BlockSpec(memory_space=pltpu.SMEM)
VMEM = pl.BlockSpec(memory_space=pltpu.VMEM)
ANY = pl.BlockSpec(memory_space=pl.ANY)


def call(kernel, name, in_specs, outs, out_specs, scratch, args, flops, moved):
    return pl.pallas_call(
        kernel,
        name=name,
        in_specs=in_specs,
        out_shape=[jax.ShapeDtypeStruct(s, d) for s, d in outs],
        out_specs=out_specs,
        scratch_shapes=scratch,
        compiler_params=pltpu.CompilerParams(vmem_limit_bytes=VMEM_LIMIT),
        cost_estimate=pl.CostEstimate(flops=flops, bytes_accessed=moved, transcendentals=0),
    )(*args)


def body(
    pictures, captions, tallies, exponent,
    p_gains, p_biases, p_hid, p_wq, p_wp, p_we, p_wr,
    c_gains, c_biases, c_hid, c_wq, c_wp, c_we, c_wr,
):
    t = lax.axis_index("tower")
    d = lax.axis_index("dp")
    chips = lax.axis_size("dp")
    pairs, length, width = captions.shape
    img_len = pictures.shape[1]
    hidden = c_hid.shape[0]
    caps = pairs // 2
    n = caps * length
    total = pairs * chips
    row_blocks = 16
    order = np.array(slot_reaches(chips))
    slot_of = np.zeros(chips, np.int32)
    slot_of[order] = np.arange(chips)
    table = np.stack([slot_of[np.arange(chips) ^ i] for i in range(chips)]).astype(np.int32)
    slots = lax.dynamic_slice_in_dim(jnp.asarray(table), d, 1, 0)[0]
    relative = chips == row_blocks
    row_slots = slots if relative else jnp.arange(row_blocks, dtype=jnp.int32)
    head = jnp.stack([t, d, tallies[0], t]).astype(jnp.int32)
    scal = jnp.concatenate([head, row_slots, slots])

    texts_in = captions.reshape(pairs * length, width)
    c_hid2, p_hid2 = c_hid.reshape(1, hidden), p_hid.reshape(1, hidden)
    blk = (row_blocks, width // row_blocks, n)
    vm = pltpu.VMEM
    sem = pltpu.SemaphoreType.DMA
    half_hid = (n, hidden // 2)
    chunk = width + 2 * LANES
    a_t, qkv, o_t, m, c_t, gp_keep, gp_send, text_send, emb, r = call(
        text_forward_kernel, "text_forward",
        [SMEM, ANY, VMEM, VMEM, VMEM, ANY, ANY, ANY, ANY],
        [(blk, BF16), ((n, 3 * width), BF16), (blk, BF16), ((n, width), F32), (blk, BF16),
         (half_hid, BF16), (half_hid, BF16), ((chips, caps, chunk), BF16),
         ((caps, width), F32), ((caps, LANES), F32)],
        [ANY] * 7 + [VMEM] * 3,
        [vm((n, width), BF16), vm((width, 3 * width), BF16), vm((width, width), BF16),
         vm((width, hidden), BF16), vm((hidden, width), BF16), vm((n, width), BF16),
         vm((n, width), BF16), vm((caps, hidden), F32), vm(blk, BF16), vm((n, 3 * width), BF16),
         vm(blk, BF16), vm((n, width), F32), vm(blk, BF16), vm(half_hid, BF16),
         vm(half_hid, BF16), sem((5,)), sem((7,))],
        (scal, texts_in, c_gains, c_biases, c_hid2, c_wq, c_wp, c_we, c_wr),
        int(2 * n * width * (4 * width + hidden)), 20_000_000,
    )
    c_far = xor_permute(c_t, "tower", 1)
    gp_far = xor_permute(gp_send, "tower", 1)
    text_all = lax.all_to_all(text_send, "dp", 0, 0, tiled=True)

    rows = caps * PAD
    groups = bit_groups(chips)
    (image,) = call(
        image_forward_kernel, "image_forward",
        [SMEM, ANY, VMEM, VMEM, VMEM, ANY, ANY, ANY, ANY],
        [((caps, width), BF16)],
        [VMEM],
        [vm((img_len, pairs, width), BF16), vm((width // LANES, img_len * caps, LANES), F32),
         vm((rows, width), F32), vm((rows, width), BF16),
         vm((rows + 16, 3 * width), BF16), vm((rows, width), F32), vm((caps, width), F32),
         vm((caps, hidden), F32), vm((width, 3 * width), BF16), vm((width, width), BF16),
         vm((width, hidden), BF16), vm((hidden, width), BF16), sem((5,))],
        (scal, jnp.transpose(pictures, (1, 0, 2)), p_gains, p_biases, p_hid2,
         p_wq, p_wp, p_we, p_wr),
        int(2 * rows * width * (4 * width + hidden)), 20_000_000,
    )
    image, text_all = lax.optimization_barrier((image, text_all))
    text_par = xor_permute(text_all, "tower", 1)
    got = hop([image[None]] * len(reaches(groups[0])), groups[0])
    for group in groups[1:]:
        whole = jnp.concatenate(got, axis=0)
        got = hop([whole] * len(reaches(group)), group)
    par_all = xor_permute(jnp.concatenate(got, axis=0), "tower", 1)
    small_slice = total <= 768
    if not small_slice:
        got = [jnp.concatenate(got, axis=0)]

    block = total if small_slice else 96
    held = chips if small_slice else 1
    share = hidden // (2 * chips)
    piece_shape = (width // 2, width)
    (loss, temp, ea, eb, ec, ed, g_all, images_all, texts_all, gall, extra, dc, dy, hid_grad) = call(
        partial(loss_kernel, block, len(got)), "loss",
        [SMEM] + [ANY] * len(got) + [ANY, ANY, ANY, SMEM, VMEM, VMEM] + [ANY] * 6,
        [((1,), F32), ((1,), F32)] + [(piece_shape, BF16)] * 4
        + [((total, total), BF16), ((total, width), BF16), ((total, width), BF16),
           ((total, LANES), BF16), ((total, LANES), F32), ((n, width), F32), ((caps, width), F32),
           ((1, hidden // 2), F32)],
        [SMEM, SMEM] + [ANY] * 10 + [VMEM, VMEM],
        [vm((held, caps, width), BF16), vm((held, caps, width), BF16),
         vm((held, caps, chunk), BF16), vm((held, caps, chunk), BF16),
         vm((total, width), BF16), vm((total, width), BF16), vm((total, LANES), F32),
         vm((total, LANES), BF16), vm((8, total), F32),
         vm((block, total), F32), vm((block, total), BF16), vm((2 * caps, total), BF16),
         vm(half_hid, BF16), vm(half_hid, BF16), vm((2,) + blk, BF16),
         vm((width, hidden // 2), BF16), vm((hidden // 2, width), BF16),
         vm((n, width), F32), vm((2, width, hidden // 4), BF16), sem((16,)), sem((14,))],
        (scal, *got, par_all, text_all, text_par, exponent, emb, r, gp_keep, gp_far,
         c_t, c_far, c_we, c_wr),
        int(3 * n * width * hidden), 20_000_000,
    )

    def widen(x):
        return x.astype(F32)

    def narrow(x):
        return x.astype(BF16)

    e_hops = [xor_permute(ea, "dp", 1), xor_permute(eb, "dp", 2)] if relative else []
    dm, dqkv, vec = call(
        middle_back_kernel, "middle_back",
        [SMEM, ANY, VMEM, ANY, ANY, VMEM] + [ANY] * 4,
        [((n, width), F32), ((n, 3 * width), BF16), ((8, width), F32)],
        [ANY, ANY, VMEM],
        [vm((n, width), F32), vm(half_hid, BF16), vm((n, width), F32),
         vm((width, hidden // 2), BF16), vm((hidden // 2, width), BF16), vm((width, width), BF16),
         vm((n, 3 * width), BF16), vm((n, width), F32), vm((n, width), BF16),
         vm((n, width), BF16), vm((n, 3 * width), BF16), sem((9,))],
        (scal, dc, dy, gp_send, m, c_gains, c_we, c_wr, c_wp, qkv),
        int(2 * n * width * (hidden + 4 * width)), 20_000_000,
    )
    b_shape = (width // 2, width + LANES)
    qa_keep, qb_keep, qa_send, qb_send = call(
        partial(weight_grad_kernel, relative), "weight_grad",
        [SMEM] + [ANY] * 5 + [VMEM] * 4 + [ANY] * len(e_hops),
        [((2,) + piece_shape, BF16), ((2,) + b_shape, BF16)] * 2,
        [ANY] * 4,
        [vm((n, width), F32), vm(blk, BF16), vm(blk, BF16), vm((n, width), BF16),
         vm((n, 3 * width), BF16), vm((row_blocks, width // row_blocks, 3 * width), BF16),
         vm((2, 2) + piece_shape, BF16), vm((2, 2) + b_shape, BF16),
         vm((row_blocks, width // row_blocks, LANES), F32), sem((8 + row_blocks,))],
        (scal, dm, dqkv, a_t, o_t, c_wq, c_gains, c_biases, vec, hid_grad, *e_hops),
        int(2 * n * width * 4 * width), 20_000_000,
    )
    qa_back = xor_permute(qa_send, "tower", 1)
    qb_back = xor_permute(qb_send, "tower", 1)
    cols = width // chips
    q_sums = [
        f(x[i], width) + f(y[i], width)
        for i in range(2)
        for f, x, y in ((from_wire, qa_keep, qa_back), (from_wire, qb_keep, qb_back))
    ]
    if not relative:
        tails = jnp.transpose(hid_grad.reshape(chips, 2, cols), (0, 2, 1)).reshape(width, 2)
        tails = jnp.pad(tails, ((0, 0), (width + 4, 64 - 6)))
        quarter = width // 4
        for i in (1, 3):
            q_sums[i] = q_sums[i] + jnp.concatenate(
                [tails[q * quarter : (q + 1) * quarter] for q in QUARTERS[i]], axis=0
            )
    wire_a, wire_b = to_wire(q_sums[0], width), to_wire(q_sums[1], width)
    q_hops = [xor_permute(wire_a, "dp", 1), xor_permute(wire_b, "dp", 2)] if relative else []
    tok_keep, tok_send = call(
        input_back_kernel, "input_back",
        [SMEM, ANY, ANY, VMEM, ANY, ANY, ANY],
        [((caps, length // 2, width), F32), ((caps, length // 2, width), BF16)],
        [VMEM] * 2,
        [vm((n, width), BF16), vm((width, 3 * width), BF16), vm((n, width), F32),
         vm((n, 3 * width), BF16), vm((n, width), F32), sem((4,))],
        (scal, dm, texts_in, c_gains, dqkv, c_wq, wire_b),
        int(2 * n * width * 3 * width), 9_000_000,
    )
    reduce_grad, rbias = call(
        partial(reduce_grad_kernel, block, length), "reduce_grad",
        [SMEM] + [ANY] * 6,
        [((share, width), F32), ((8, width), F32)],
        [VMEM, VMEM],
        [vm((block, total), BF16), vm((total, width), BF16), vm((block, width), BF16),
         vm((block, LANES), BF16), vm((block, LANES), F32), vm((LANES, width), F32), sem((5,))],
        (exponent, g_all, images_all, texts_all, gall, extra, q_hops[0] if relative else wire_b),
        int(2 * total * total * width), 6_000_000,
    )

    tok_back = widen(xor_permute(tok_send, "tower", 1))
    grad_tokens = jnp.concatenate(
        [jnp.where(t == 0, tok_keep, tok_back), jnp.where(t == 0, tok_back, tok_keep)], axis=0
    )
    half, third = width // 2, width // 4

    def plain(sums):
        sides = []
        for side in range(2):
            at = {}
            for i in (side, side + 2):
                for j, q in enumerate(QUARTERS[i]):
                    at[q] = sums[i][j * third : (j + 1) * third]
            x = jnp.concatenate([at[q] for q in range(4)], axis=0)
            x = flip_by(x.reshape((chips, cols) + x.shape[1:]), d, chips)
            x = x[order].reshape((width,) + x.shape[2:])
            sides.append(
                scatter_sum(x, groups, lambda v: to_wire(v, width), lambda v: from_wire(v, width))
            )
        return sides

    if not relative:
        expand_grad = jnp.concatenate(plain([widen(x) for x in (ea, eb, ec, ed)]), axis=1)
        side_a, side_b = plain(q_sums)
        small = side_b[:, width : width + 8].T
        last = jnp.where(
            t == 0, small[3], lax.dynamic_slice_in_dim(rbias[0], d * cols, cols, 0)
        )
        return (
            loss, temp, grad_tokens, small[0:1], jnp.stack([small[1], small[2], last]),
            small[4:6].reshape(2 * cols),
            jnp.concatenate([side_a[:, half:], side_b[:, :width]], axis=1), side_a[:, :half],
            expand_grad, reduce_grad,
        )

    def second_hops(keep_a, keep_b, hops):
        sum_a = keep_a + widen(hops[0])
        sum_b = keep_b + from_wire(hops[1], width)
        next_a = xor_permute(narrow(sum_a[third:]), "dp", 2)
        next_b = xor_permute(to_wire(sum_b[third:], width), "dp", 1)
        return sum_a[:third], sum_b[:third], next_a, next_b

    def merge(parts, after, name):
        f32_cols = parts[0].shape[1] + parts[1].shape[1]
        bf_cols = parts[2].shape[1] + parts[3].shape[1]
        return call(
            partial(merge_kernel, width), name, [VMEM] * 4 + [ANY] * len(after),
            [((cols, f32_cols), F32)] + [((cols, bf_cols), BF16)] * 3, [VMEM] * 4, [],
            (*parts, *after), 1_000_000, 3_000_000,
        )

    def z_hops(pieces):
        return [xor_permute(x, "dp", r) for x, r in zip(pieces, reaches(groups[0])[1:])]

    e_parts = second_hops(widen(ec), widen(ed), e_hops)
    e_own, *e_far = merge(e_parts, (wire_b,), "merge_expand")
    e_back = z_hops(e_far)
    expand_grad = e_own + sum(widen(x) for x in e_back)
    q_parts = second_hops(q_sums[2], q_sums[3], q_hops)
    q_own, *q_far = merge(q_parts, e_back, "merge_qkv")
    q_in = z_hops(q_far)
    qkv_grad, project_grad, gains_grad, biases_grad, hid_rows = call(
        partial(finish_kernel, width), "finish", [SMEM] + [VMEM] * 5,
        [((cols, 3 * half), F32), ((cols, half), F32), ((1, cols), F32), ((3, cols), F32),
         ((2, cols), F32)],
        [VMEM] * 5, [], (scal, q_own, *q_in, rbias), 1_000_000, 2_000_000,
    )
    return (
        loss, temp, grad_tokens, gains_grad, biases_grad, hid_rows.reshape(2 * cols),
        qkv_grad, project_grad, expand_grad, reduce_grad,
    )


def solution(mesh):
    in_specs = (P("dp", None, None), P("dp", None, None), P("dp")) + (P(),) * 15
    out_specs = (
        P(), P(), P("dp", "tower", None), P("tower", "dp"), P("tower", "dp"),
        P(("tower", "dp")), P("dp", "tower"), P("dp", "tower"), P("dp", "tower"),
        P(("tower", "dp"), None),
    )
    return jax.shard_map(body, mesh=mesh, in_specs=in_specs, out_specs=out_specs, check_vma=False)
```

```python
from functools import partial

import jax
import jax.numpy as jnp
import numpy as np
from jax import lax
from jax.experimental import pallas as pl
from jax.experimental.pallas import tpu as pltpu
from jax.sharding import PartitionSpec as P

F32 = jnp.float32
BF16 = jnp.bfloat16
HEAD_DIM = 64
LANES = 128
EXTRA = 120
norm_eps = 1e-06
embed_eps = 1e-06
NEG = -1000000000.0
VMEM_LIMIT = 60 * 1024 * 1024


def normal_cdf(x):
    return 0.5 + 0.5 * lax.erf(x * 0.7071067811865476)


def load(src, dst, sem):
    copy = pltpu.make_async_copy(src, dst, sem)
    copy.start()
    return copy


def dot(a, b):
    return jnp.dot(a, b, preferred_element_type=F32)


def dot_nt(a, b):
    return lax.dot_general(a, b, (((1,), (1,)), ((), ())), preferred_element_type=F32)


def dot_tn(a, b):
    return lax.dot_general(a, b, (((0,), (0,)), ((), ())), preferred_element_type=F32)


def norm_stats(x):
    mean = jnp.mean(x, axis=-1, keepdims=True)
    centered = x - mean
    rstd = lax.rsqrt(jnp.mean(centered * centered, axis=-1, keepdims=True) + norm_eps)
    return centered * rstd, rstd


def norm_back(dxhat, xhat, rstd):
    return rstd * (
        dxhat
        - jnp.mean(dxhat, axis=-1, keepdims=True)
        - xhat * jnp.mean(dxhat * xhat, axis=-1, keepdims=True)
    )


def row(ref, i):
    return ref[i : i + 1, :].astype(F32)


def head_masks():
    lane = lax.broadcasted_iota(jnp.int32, (1, LANES), 1)
    first = (lane < HEAD_DIM).astype(BF16)
    return first, (1 - first).astype(BF16)


def set_qkv_bias(out, biases):
    width = biases.shape[1]
    out[:, :width] = row(biases, 2)
    out[:, width : 2 * width] = jnp.zeros((1, width), F32)
    out[:, 2 * width :] = row(biases, 3)


def two_heads(x, masks):
    return jnp.concatenate([x * masks[0], x * masks[1]], axis=0)


def softmax_parts(scores, bias):
    keys = scores.shape[1] // 2
    parts = []
    for e in range(2):
        s = scores[:, e * keys : (e + 1) * keys] + bias
        parts.append(jnp.exp(s - jnp.max(s, axis=-1, keepdims=True)))
    return parts


def attend(q2, k2, v2, bias, masks):
    e0, e1 = softmax_parts(dot_nt(q2 * BF16(0.125), two_heads(k2, masks)), bias)
    weights = jnp.concatenate([e0.astype(BF16), e1.astype(BF16)], axis=1)
    ones = jnp.ones((k2.shape[0], LANES), BF16)
    right = jnp.concatenate([two_heads(v2, masks), two_heads(ones, masks)], axis=1)
    out = dot(weights, right)
    return (out[:, :LANES] / out[:, LANES:]).astype(BF16)


def split_dot(x, w):
    hi = x.astype(BF16)
    lo = (x - hi.astype(F32)).astype(BF16)
    n = x.shape[0]
    out = dot(jnp.concatenate([hi, lo], axis=0), w)
    return out[:n] + out[n:]


def text_forward_kernel(
    scal, h_any, gains, biases, hid, wq_any, wp_any, we_any, wr_any,
    a_any, qkv_any, o_any, m_any, c_any, gpk_any, gps_any, send_out, emb_out, r_out,
    h_v, wq, wp, we, wr, qb, av, cv, gsum, a_out, qkv_out, o_out, m_out, c_out, gp_keep, gp_send,
    sems, out_sems,
):
    n, width = m_out.shape
    caps = emb_out.shape[0]
    length = n // caps
    hidden = hid.shape[1]
    t, d = scal[0], scal[1]
    load_h = load(h_any.at[pl.ds(pl.multiple_of(t * n, n), n)], h_v, sems.at[0])
    load_q = load(wq_any, wq, sems.at[1])
    load_h.wait()
    masks = head_masks()

    def put_transposed(out, src):
        count, rows = out.shape[:2]

        def turn(i, carry):
            lanes = pl.ds(pl.multiple_of(i * (width // 2), LANES), width // 2)
            turned = src[:, lanes].astype(F32).T.astype(BF16)
            for e in range(count // 2):
                out[scal[4 + i * (count // 2) + e]] = turned[e * rows : (e + 1) * rows, :]
            return carry

        lax.fori_loop(0, 2, turn, 0, unroll=2)

    h = h_v[...].astype(F32)
    xhat, _ = norm_stats(h)
    a = xhat * row(gains, 0) + row(biases, 0)
    av[...] = a.astype(BF16)
    load_q.wait()
    load_p = load(wp_any, wp, sems.at[2])
    load_e = load(we_any, we, sems.at[3])
    load_r = load(wr_any, wr, sems.at[4])
    set_qkv_bias(qb, biases)

    def to_qkv(j, carry):
        cols = pl.ds(pl.multiple_of(j * 256, 256), 256)
        qkv_out[:, cols] = (dot(av[...], wq[:, cols]) + qb[:, cols]).astype(BF16)
        return carry

    lax.fori_loop(0, 3 * width // 256, to_qkv, 0, unroll=9)
    put_transposed(a_out, av)
    stores = [load(qkv_out, qkv_any, out_sems.at[0]), load(a_out, a_any, out_sems.at[1])]
    same = (
        lax.broadcasted_iota(jnp.int32, (LANES, LANES), 0) // length
        == lax.broadcasted_iota(jnp.int32, (LANES, LANES), 1) // length
    )
    bias = jnp.where(same, 0.0, -1e30)

    def attention(g, carry):
        rows = pl.ds(pl.multiple_of(g * LANES, LANES), LANES)
        for p in range(width // LANES):
            lanes = slice(p * LANES, (p + 1) * LANES)
            q2 = qkv_out[rows, lanes]
            k2 = qkv_out[rows, width + p * LANES : width + (p + 1) * LANES]
            v2 = qkv_out[rows, 2 * width + p * LANES : 2 * width + (p + 1) * LANES]
            av[rows, lanes] = attend(q2, k2, v2, bias, masks)
        return carry

    lax.fori_loop(0, n // LANES, attention, 0)
    load_p.wait()
    m = h_v[...].astype(F32) + dot(av[...], wp[...]) + row(biases, 4)
    m_out[...] = m
    stores.append(load(m_out, m_any, out_sems.at[2]))
    xhat, _ = norm_stats(m)
    c = xhat * row(gains, 1) + row(biases, 1)
    cv[...] = c.astype(BF16)
    put_transposed(c_out, cv)
    put_transposed(o_out, av)
    stores.append(load(c_out, c_any, out_sems.at[3]))
    stores.append(load(o_out, o_any, out_sems.at[4]))
    load_e.wait()
    half = hidden // 512

    def feed(rel, gp_out):
        def step(j, carry):
            local = pl.ds(pl.multiple_of(j * 256, 256), 256)
            at = jnp.bitwise_xor(t, rel) * half + j
            cols = pl.ds(pl.multiple_of(at * 256, 256), 256)
            f = dot(cv[...], we[:, cols]) + hid[:, cols].astype(F32)
            cdf = normal_cdf(f)
            density = jnp.exp(f * f * -0.5) * 0.3989422804014327
            gp_out[:, local] = (cdf + f * density).astype(BF16)
            gsum[:, cols] = jnp.sum((f * cdf).reshape(caps, length, 256), axis=1)
            return carry

        lax.fori_loop(0, half, step, 0, unroll=2)

    feed(1, gp_send)
    stores.append(load(gp_send, gps_any, out_sems.at[5]))
    feed(0, gp_keep)
    stores.append(load(gp_keep, gpk_any, out_sems.at[6]))
    load_r.wait()
    total = gsum[...]
    pooled = (
        jnp.mean(m_out[...].reshape(caps, length, width), axis=1)
        + split_dot(total * (1.0 / length), wr[...])
        + row(biases, 5)
    )
    r = lax.rsqrt(jnp.sum(pooled * pooled, axis=-1, keepdims=True) + embed_eps)
    emb_out[...] = pooled * r
    r_out[...] = jnp.broadcast_to(r, r_out.shape)
    chips = send_out.shape[0]
    share = hidden // (2 * chips)
    scaled = total * r
    hi = r.astype(BF16).astype(F32)
    mid = (r - hi).astype(BF16).astype(F32)
    slot = lax.broadcasted_iota(jnp.int32, (caps, LANES), 0) + t * caps
    lane = lax.broadcasted_iota(jnp.int32, (caps, LANES), 1)
    extra = jnp.where(lane == EXTRA, hi, 0.0)
    extra = jnp.where(lane == EXTRA + 1, mid, extra)
    extra = jnp.where(lane == EXTRA + 2, r - hi - mid, extra)
    extra = jnp.where((lane == EXTRA + 3) & (slot < scal[2]), 1.0, extra)
    for e in range(chips):
        send_out[e, :, :width] = (pooled * r).astype(BF16)
        for half_at in range(2):
            src = (half_at * chips + e) * share
            piece = jnp.concatenate([scaled[:, src : src + share], extra[:, share:]], axis=1)
            to = width + jnp.bitwise_xor(t, half_at) * LANES
            send_out[e, :, pl.ds(pl.multiple_of(to, LANES), LANES)] = piece.astype(BF16)
    for c in stores:
        c.wait()


PAD = 56


def image_forward_kernel(
    scal, x_any, gains, biases, hid, wq_any, wp_any, we_any, wr_any,
    out,
    x_v, xs, hv, av, qkv, mv, msum, gsum, wq, wp, we, wr, qb, pb, sems,
):
    length, both_caps, width = x_v.shape
    caps = both_caps // 2
    n = caps * PAD
    hidden = hid.shape[1]
    t = scal[0]
    load_x = load(x_any, x_v, sems.at[0])
    load_q = load(wq_any, wq, sems.at[1])
    masks = head_masks()
    qkv[n:, :] = jnp.zeros((qkv.shape[0] - n, 3 * width), BF16)
    first = (jnp.zeros((1, 1), jnp.int32) + t) == 0
    load_x.wait()

    def pick(i, carry):
        x = x_v[i].astype(F32)
        x = jnp.where(first, x[:caps], x[caps:])
        for k in range(width // LANES):
            xs[k, pl.ds(pl.multiple_of(i * caps, 8), caps), :] = x[:, k * LANES : (k + 1) * LANES]
        return carry

    lax.fori_loop(0, length, pick, 0, unroll=2)

    def first_norm(j, carry):
        base = pl.multiple_of(j * 2 * PAD, 16)
        for e in range(2):
            x = jnp.concatenate(
                [
                    xs[k, pl.ds(j * 2 + e, length, stride=caps), :]
                    for k in range(width // LANES)
                ],
                axis=1,
            )
            x = jnp.concatenate([x, jnp.zeros((PAD - length, width), F32)], axis=0)
            hv[pl.ds(base + e * PAD, PAD), :] = x
            xhat, _ = norm_stats(x)
            x = xhat * row(gains, 0) + row(biases, 0)
            if e == 0:
                kept = x
        av[pl.ds(base, 2 * PAD), :] = jnp.concatenate([kept, x], axis=0).astype(BF16)
        return carry

    lax.fori_loop(0, caps // 2, first_norm, 0, unroll=4)
    load_q.wait()
    load_p = load(wp_any, wp, sems.at[2])
    load_e = load(we_any, we, sems.at[3])
    load_r = load(wr_any, wr, sems.at[4])
    set_qkv_bias(qb, biases)

    def to_qkv(j, carry):
        cols = pl.ds(pl.multiple_of(j * 256, 256), 256)
        qkv[:n, cols] = (dot(av[...], wq[:, cols]) + qb[:, cols]).astype(BF16)
        return carry

    lax.fori_loop(0, 3 * width // 256, to_qkv, 0, unroll=9)
    q_at = lax.broadcasted_iota(jnp.int32, (2 * PAD, LANES), 0)
    k_at = lax.broadcasted_iota(jnp.int32, (2 * PAD, LANES), 1)
    low = (q_at < PAD) & (k_at < length)
    high = (q_at >= PAD) & (k_at >= PAD) & (k_at < PAD + length)
    bias = jnp.where(low | high, 0.0, -1e30)

    def attention(j, carry):
        base = pl.multiple_of(j * 2 * PAD, 16)
        rows, keys = pl.ds(base, 2 * PAD), pl.ds(base, LANES)
        for p in range(width // LANES):
            lanes = slice(p * LANES, (p + 1) * LANES)
            q2 = qkv[rows, lanes]
            k2 = qkv[keys, width + p * LANES : width + (p + 1) * LANES]
            v2 = qkv[keys, 2 * width + p * LANES : 2 * width + (p + 1) * LANES]
            av[rows, lanes] = attend(q2, k2, v2, bias, masks)
        return carry

    lax.fori_loop(0, caps // 2, attention, 0, unroll=2)
    load_p.wait()
    pb[...] = row(biases, 4)

    def add_attended(j, carry):
        cols = pl.ds(pl.multiple_of(j * 256, 256), 256)
        mv[:, cols] = hv[:, cols] + dot(av[...], wp[:, cols]) + pb[:, cols]
        return carry

    lax.fori_loop(0, width // 256, add_attended, 0, unroll=3)
    group = 8 * PAD
    tail = (lax.broadcasted_iota(jnp.int32, (1, 8, 1), 1) < length - (PAD - 8)).astype(F32)

    def token_sum(x, count):
        tiles = x.reshape(count, PAD // 8, 8, x.shape[1])
        acc = tiles[:, PAD // 8 - 1] * tail
        for i in range(PAD // 8 - 1):
            acc = acc + tiles[:, i]
        return jnp.sum(acc, axis=1)

    def second_norm(j, carry):
        rows = pl.ds(pl.multiple_of(j * group, 16), group)
        m = mv[rows, :]
        xhat, _ = norm_stats(m)
        av[rows, :] = (xhat * row(gains, 1) + row(biases, 1)).astype(BF16)
        msum[pl.ds(pl.multiple_of(j * 8, 8), 8), :] = token_sum(m, 8)
        return carry

    lax.fori_loop(0, caps // 8, second_norm, 0)
    load_e.wait()

    def feed(j, carry):
        cols = pl.ds(pl.multiple_of(j * 256, 256), 256)
        f = dot(av[...], we[:, cols]) + hid[:, cols].astype(F32)
        gsum[:, cols] = token_sum(f * normal_cdf(f), caps)
        return carry

    lax.fori_loop(0, hidden // 256, feed, 0, unroll=2)
    load_r.wait()
    scale = 1.0 / length
    pooled = msum[...] * scale + split_dot(gsum[...] * scale, wr[...]) + row(biases, 5)
    r_img = lax.rsqrt(jnp.sum(pooled * pooled, axis=-1, keepdims=True) + embed_eps)
    out[...] = (pooled * r_img).astype(BF16)


QUARTERS = ((1, 3), (2, 3), (0, 2), (0, 1))


def loss_kernel(
    rows_block, parts, scal, *refs,
):
    own_any, refs = refs[:parts], refs[parts:]
    (par_any, text_any, text_par_any, expo, emb, r, gpk_any, gpr_any, ct_any, ctr_any,
     we_any, wr_any,
     loss_out, temp_out, ea, eb, ec, ed, g_any, images_any, texts_any, gall_any, extra_any,
     dc_any, dy_out, hid_out,
     own_v, par_v, text_v, text_par_v, texts, images, extra, gall, col_flag, sims, grad,
     chip_g, gpk, gpr, ct, we, wr, dc, exp_s, sems, out_sems) = refs
    chips, caps, width = par_any.shape
    staged = own_v.shape[0] == chips
    total = texts.shape[0]
    near_hidden = gpk.shape[1]
    n = dc.shape[0]
    length = n // caps
    t, d = scal[0], scal[1]
    first = (jnp.zeros((1, 1), jnp.int32) + t) == 0
    if staged:
        each = chips // parts
        waits = [
            load(par_any, par_v, sems.at[0]),
            load(text_any, text_v, sems.at[1]),
            load(text_par_any, text_par_v, sems.at[2]),
        ] + [
            load(own_any[i], own_v.at[pl.ds(i * each, each)], sems.at[3 + i]) for i in range(parts)
        ]
        for c in waits:
            c.wait()

    def place(e, carry):
        at, slot = e, scal[4 + 16 + e]
        if not staged:
            waits = [
                load(src.at[pl.ds(i, 1)], dst, sems.at[j])
                for j, (src, i, dst) in enumerate(
                    ((own_any[0], slot, own_v), (par_any, slot, par_v), (text_any, at, text_v),
                     (text_par_any, at, text_par_v))
                )
            ]
            for c in waits:
                c.wait()
            at = slot = 0

        def pair(x0, x1):
            x0, x1 = x0.astype(F32), x1.astype(F32)
            return jnp.concatenate([jnp.where(first, x0, x1), jnp.where(first, x1, x0)], axis=0)

        rows = pl.ds(pl.multiple_of(e * 2 * caps, 16), 2 * caps)
        images[rows, :] = pair(own_v[slot], par_v[slot]).astype(BF16)
        x0, x1 = text_v[at], text_par_v[at]
        texts[rows, :] = pair(x0[:, :width], x1[:, :width]).astype(BF16)
        last = pair(x0[:, width : width + LANES], x1[:, width + LANES :])
        extra[rows, :] = last
        gall[rows, :] = last.astype(BF16)
        return carry

    lax.fori_loop(0, chips, place, 0, unroll=2)
    half = near_hidden // 256
    later = [
        load(src, dst, sems.at[8 + i])
        for i, (src, dst) in enumerate(
            ((wr_any.at[pl.ds(pl.multiple_of(t * near_hidden, 256), near_hidden)], wr),
             (gpk_any, gpk), (gpr_any, gpr),
             (we_any.at[:, pl.ds(pl.multiple_of(t * near_hidden, 256), near_hidden)], we))
        )
    ]
    for i, src in enumerate((ct_any, ctr_any)):
        later.append(load(src, ct.at[i], sems.at[12 + i]))
    stores = [
        load(src, dst, out_sems.at[i])
        for i, (src, dst) in enumerate(
            ((images, images_any), (texts, texts_any), (gall, gall_any), (extra, extra_any))
        )
    ]
    pick = (lax.broadcasted_iota(jnp.int32, (8, LANES), 1) == EXTRA + 3).astype(F32)
    step = min(256, total)

    def flags(j, carry):
        cols = pl.ds(pl.multiple_of(j * step, step), step)
        col_flag[:, cols] = dot_nt(pick, extra[cols, :])
        return carry

    lax.fori_loop(0, total // step, flags, 0)
    scale = jnp.exp(jnp.full((1, 1), expo[0], F32))
    chunk = 48
    blocks = total // rows_block
    per_block = rows_block // chunk
    live = col_flag[0:1, :]

    def similarities(b):
        base = pl.multiple_of(b * rows_block, 16)

        def cols_step(j, carry):
            cols = pl.ds(pl.multiple_of(j * step, step), step)
            sims[:, cols] = scale * dot_nt(texts[pl.ds(base, rows_block), :], images[cols, :])
            return carry

        lax.fori_loop(0, total // step, cols_step, 0)

    def chunk_at(b, i):
        local = pl.ds(pl.multiple_of(i * chunk, 16), chunk)
        whole = pl.ds(pl.multiple_of(b * rows_block + i * chunk, 16), chunk)
        return local, whole

    def column_block(b, acc):
        similarities(b)

        def adding(i, acc):
            local, whole = chunk_at(b, i)
            live_row = extra[whole, EXTRA + 3 : EXTRA + 4]
            part = jnp.exp(sims[local, :]) * live_row
            return acc + jnp.sum(part.reshape(chunk // 8, 8, total), axis=0)

        return lax.fori_loop(0, per_block, adding, acc, unroll=2)

    col_acc = jnp.zeros((8, total), F32)
    if blocks == 1:
        col_acc = column_block(0, col_acc)
    else:
        col_acc = lax.fori_loop(0, blocks, column_block, col_acc)
    col_sum = jnp.sum(col_acc, axis=0, keepdims=True)
    col_part = 0.5 * live / col_sum

    def row_block(b, carry):
        if blocks > 1:
            similarities(b)

        def rows_step(i, acc):
            loss, temp, diag = acc
            local, whole = chunk_at(b, i)
            s = sims[local, :]
            flag = extra[whole, EXTRA + 3 : EXTRA + 4]
            at = lax.broadcasted_iota(jnp.int32, (chunk, total), 0) + (b * rows_block + i * chunk)
            eye = at == lax.broadcasted_iota(jnp.int32, (chunk, total), 1)
            expd = jnp.exp(s)
            rsum = jnp.sum(expd * live, axis=1, keepdims=True)
            g = expd * ((0.5 * flag / rsum) * live + flag * col_part)
            g = g - jnp.where(eye, 0.5 * (flag + live), 0.0)
            grad[local, :] = g.astype(BF16)
            temp = temp + jnp.sum((g * s).reshape(chunk // 8, 8, total), axis=0)
            diag = diag + jnp.sum(
                jnp.where(eye, s * flag, 0.0).reshape(chunk // 8, 8, total), axis=0
            )
            return loss + 0.5 * flag * jnp.log(rsum), temp, diag

        carry = lax.fori_loop(0, per_block, rows_step, carry, unroll=2)
        mine = d * (2 * caps) - b * rows_block

        @pl.when((mine >= 0) & (mine < rows_block))
        def _():
            chip_g[...] = grad[pl.ds(pl.multiple_of(mine, 16), 2 * caps), :]

        if blocks > 1:
            rows = pl.ds(pl.multiple_of(b * rows_block, 16), rows_block)
            load(grad, g_any.at[rows], out_sems.at[4]).wait()
        return carry

    start = (jnp.zeros((chunk, 1), F32), jnp.zeros((8, total), F32), jnp.zeros((8, total), F32))
    if blocks == 1:
        loss, temp, diag = row_block(0, start)
        stores.append(load(grad, g_any, out_sems.at[4]))
    else:
        loss, temp, diag = lax.fori_loop(0, blocks, row_block, start)
    def whole(x):
        return jnp.sum(jnp.sum(x, axis=0, keepdims=True), axis=1, keepdims=True)

    objective = whole(loss) + 0.5 * whole(live * jnp.log(col_sum)) - whole(diag)
    loss_out[...] = objective / whole(live)
    temp_out[...] = whole(temp)

    both_dt = scale * dot(chip_g[...], images[...])
    chip = pl.ds(pl.multiple_of(d * 2 * caps, 16), 2 * caps)
    inv = jnp.sum(extra[chip, EXTRA : EXTRA + 3], axis=1, keepdims=True)
    dt = jnp.where(first, both_dt[:caps], both_dt[caps:])
    dt_far = jnp.where(first, both_dt[caps:], both_dt[:caps])
    both_tx = texts[chip, :].astype(F32)
    tx_far = jnp.where(first, both_tx[caps:], both_tx[:caps])
    inv_far = jnp.where(first, inv[caps:], inv[:caps])

    def pooled_back(tx, dt, inv):
        return inv * (dt - tx * jnp.sum(tx * dt, axis=1, keepdims=True)) * (1.0 / length)

    dy = pooled_back(emb[...], dt, r[:, 0:1])
    dy_out[...] = dy
    dyb = jnp.concatenate([dy, pooled_back(tx_far, dt_far, inv_far)], axis=0).astype(BF16)
    for c in later:
        c.wait()
    dc[...] = jnp.zeros_like(dc)

    def near(j, carry):
        cols = pl.ds(pl.multiple_of(j * 256, 256), 256)
        dg = dot_nt(dyb, wr[cols, :])
        df = (gpk[:, cols].astype(F32).reshape(caps, length, 256) * dg[:caps][:, None, :]).reshape(
            n, 256
        )
        far = (gpr[:, cols].astype(F32).reshape(caps, length, 256) * dg[caps:][:, None, :]).reshape(
            n, 256
        )
        df, far = df.astype(BF16), far.astype(BF16)
        hid_out[0:1, cols] = jnp.sum(df.astype(F32) + far.astype(F32), axis=0, keepdims=True)
        dc[...] += dot_nt(df, we[:, cols])
        side = near_hidden // 512
        local = pl.ds(pl.multiple_of((j % side) * 256, 256), 256)
        exp_s[j // side, :, local] = (
            dot(ct[0].reshape(width, n), df) + dot(ct[1].reshape(width, n), far)
        ).astype(BF16)
        return carry

    lax.fori_loop(0, half, near, 0, unroll=2)
    quarter = width // 4
    for i, out in enumerate((ea, eb, ec, ed)):
        for j, q in enumerate(QUARTERS[i]):
            stores.append(
                load(
                    exp_s.at[i % 2, pl.ds(q * quarter, quarter)],
                    out.at[pl.ds(j * quarter, quarter)],
                    out_sems.at[5 + 2 * i + j],
                )
            )
    stores.append(load(dc, dc_any, out_sems.at[13]))
    for c in stores:
        c.wait()


def middle_back_kernel(
    scal, dc_any, dy, gps_any, m_any, gains, we_any, wr_any, wp_any, qkv_any,
    dm_any, dqkv_any, vec_out,
    dc, gps, mv, we, wr, wp, qkv, dm, dmb, dov, dqkv, sems,
):
    n, width = dm.shape
    caps = dy.shape[0]
    length = n // caps
    far_hidden = gps.shape[1]
    t = scal[0]
    away = pl.ds(pl.multiple_of((1 - t) * far_hidden, 256), far_hidden)
    half = far_hidden // 512
    parts = []
    for i in range(2):
        at = pl.ds(pl.multiple_of(((1 - t) * 2 + i) * half * 256, 256), half * 256)
        here = pl.ds(i * half * 256, half * 256)
        parts.append([
            load(wr_any.at[at], wr.at[here], sems.at[3 * i]),
            load(gps_any.at[:, here], gps.at[:, here], sems.at[3 * i + 1]),
            load(we_any.at[:, at], we.at[:, here], sems.at[3 * i + 2]),
        ])
        if i == 0:
            load_dc = load(dc_any, dc, sems.at[9])
    for c in parts[0]:
        c.wait()
    load_dc.wait()
    load_m = load(m_any, mv, sems.at[10])
    load_p = load(wp_any, wp, sems.at[11])
    load_qkv = load(qkv_any, qkv, sems.at[6])
    dyv = dy[...]
    dyb = dyv.astype(BF16)

    def feed(j, carry):
        cols = pl.ds(pl.multiple_of(j * 256, 256), 256)
        dg = dot_nt(dyb, wr[cols, :])
        df = gps[:, cols].astype(F32).reshape(caps, length, 256) * dg[:, None, :]
        dc[...] += dot_nt(df.reshape(n, 256).astype(BF16), we[:, cols])
        return carry

    lax.fori_loop(0, half, feed, 0, unroll=3)
    for c in parts[1]:
        c.wait()
    lax.fori_loop(half, 2 * half, feed, 0, unroll=3)
    load_m.wait()
    piece = 8 * length

    def norm(i, sums):
        rows = pl.ds(pl.multiple_of(i * piece, piece), piece)
        xhat, rstd = norm_stats(mv[rows, :])
        dcv = dc[rows, :]
        back = norm_back(dcv * row(gains, 1), xhat, rstd)
        dy_rows = dy[pl.ds(pl.multiple_of(i * 8, 8), 8), :]
        out = (back.reshape(piece // length, length, width) + dy_rows[:, None, :]).reshape(
            piece, width
        )
        dm[rows, :] = out
        low = out.astype(BF16)
        dmb[rows, :] = low

        def fold(x):
            return jnp.sum(x.reshape(piece // 8, 8, width), axis=0)

        return sums[0] + fold(dcv * xhat), sums[1] + fold(dcv), sums[2] + fold(low.astype(F32))

    blank = jnp.zeros((8, width), F32)
    sums = lax.fori_loop(0, n // piece, norm, (blank, blank, blank))
    store_dm = load(dm, dm_any, sems.at[7])
    load_p.wait()
    dov[...] = dot_nt(dmb[...], wp[...]).astype(BF16)
    load_qkv.wait()
    masks = head_masks()
    same = (
        lax.broadcasted_iota(jnp.int32, (LANES, LANES), 0) // length
        == lax.broadcasted_iota(jnp.int32, (LANES, LANES), 1) // length
    )
    bias = jnp.where(same, 0.0, -1e30)

    def attention(g, carry):
        rows = pl.ds(pl.multiple_of(g * LANES, LANES), LANES)
        for p in range(width // LANES):
            lanes = slice(p * LANES, (p + 1) * LANES)
            k_lanes = slice(width + p * LANES, width + (p + 1) * LANES)
            v_lanes = slice(2 * width + p * LANES, 2 * width + (p + 1) * LANES)
            q2 = qkv[rows, lanes] * BF16(0.125)
            km = two_heads(qkv[rows, k_lanes], masks)
            vm = two_heads(qkv[rows, v_lanes], masks)
            do2 = dov[rows, lanes]
            parts = softmax_parts(dot_nt(q2, km), bias)
            dp = dot_nt(do2, vm)
            pb, ds = [], []
            for e in range(2):
                prob = parts[e] * (1.0 / jnp.sum(parts[e], axis=-1, keepdims=True))
                dpe = dp[:, e * LANES : (e + 1) * LANES]
                inner = jnp.sum(prob * dpe, axis=-1, keepdims=True)
                pb.append(prob.astype(BF16))
                ds.append((prob * (dpe - inner)).astype(BF16))
            dqkv[rows, lanes] = (dot(jnp.concatenate(ds, axis=1), km) * 0.125).astype(BF16)
            dqkv[rows, k_lanes] = dot_tn(jnp.concatenate(ds, axis=0), two_heads(q2, masks)).astype(
                BF16
            )
            dqkv[rows, v_lanes] = dot_tn(
                jnp.concatenate(pb, axis=0), two_heads(do2, masks)
            ).astype(BF16)
        return carry

    lax.fori_loop(0, n // LANES, attention, 0)
    store = load(dqkv, dqkv_any, sems.at[8])
    for i in range(3):
        vec_out[i : i + 1, :] = jnp.sum(sums[i], axis=0, keepdims=True)
    vec_out[3:4, :] = jnp.sum(dqkv[:, :width].astype(F32), axis=0, keepdims=True)
    vec_out[4:5, :] = jnp.sum(dqkv[:, 2 * width :].astype(F32), axis=0, keepdims=True)
    vec_out[5:8, :] = jnp.zeros((3, width), F32)
    store_dm.wait()
    store.wait()


def weight_grad_kernel(with_hid, scal, dm_any, dqkv_any, at_any, ot_any, wq_any, gains, biases, vec,
                       hid, *rest):
    turn, rest = (rest[:4], rest[4:]) if with_hid else ((), rest)
    keep_a, keep_b, send_a, send_b = rest[:4]
    turned, rest = (rest[4:8], rest[8:]) if with_hid else ((), rest[4:])
    dm, at, ot, dmb, dqkv, wq, grads, tails, inner_v, small, sems, store_sems = rest[:12]
    held, turn_sems = rest[12:16], rest[16:]
    n, width = dm.shape
    t = scal[0]
    load_dm = load(dm_any, dm, sems.at[0])
    load_o = load(ot_any, ot, sems.at[1])
    load_qkv = load(dqkv_any, dqkv, sems.at[2])
    load_a = load(at_any, at, sems.at[3])
    blocks, block = at.shape[:2]
    loads_t = [load(src, dst, turn_sems[0].at[i]) for i, (src, dst) in enumerate(zip(turn, held))]
    load_dm.wait()
    dmb[...] = dm[...].astype(BF16)
    load_o.wait()
    loads_w = [
        load(wq_any.at[pl.ds(e * block, block)], wq.at[scal[4 + e]], sems.at[8 + e])
        for e in range(blocks)
    ]
    half, quarter = width // 2, width // 4

    def project(hh, carry):
        cols = pl.ds(pl.multiple_of(hh * half, LANES), half)
        grads[hh, 0] = dot(ot[...].reshape(width, n), dmb[:, cols]).astype(BF16)
        return carry

    lax.fori_loop(0, 2, project, 0)
    for c in loads_t:
        c.wait()
    for side in range(len(turned) // 2):
        total = held[2 * side][...].astype(F32) + held[2 * side + 1][...].astype(F32)
        turned[side][...] = total[:quarter]
        turned[2 + side][...] = total[quarter:].astype(BF16)
    load_qkv.wait()
    load_a.wait()
    for c in loads_w:
        c.wait()
    inner_v[...] = jnp.zeros_like(inner_v)

    def attend_in(c, carry):
        cols = pl.ds(pl.multiple_of(c * half, LANES), half)
        value = dot(at[...].reshape(width, n), dqkv[:, cols])
        grads[c // 3, 1 + c % 3] = value.astype(BF16)
        prod = value * wq[:, :, cols].reshape(width, half).astype(F32)
        acc = inner_v[...]
        for k in range(half // LANES):
            acc = acc + prod[:, k * LANES : (k + 1) * LANES]
        inner_v[...] = acc
        return carry

    lax.fori_loop(0, 6, attend_in, 0)

    def move(src, out, side, lanes, slot):
        return [
            load(
                src.at[pl.ds(q * quarter, quarter)],
                out.at[i, pl.ds(j * quarter, quarter), pl.ds(lanes, src.shape[1])],
                store_sems.at[slot + 2 * i + j],
            )
            for i in range(2)
            for j, q in enumerate(QUARTERS[side + 2 * i])
        ]

    stores = []
    for k, (hh, out_a, out_b) in enumerate(((1 - t, send_a, send_b), (t, keep_a, keep_b))):
        for part in range(4):
            out = (out_a, out_b)[part // 2]
            stores += move(grads.at[hh, part], out, part // 2, (part % 2) * half, 20 * k + 4 * part)
    inner = inner_v[...]
    inner = jnp.sum(inner, axis=1, keepdims=True)
    sums = jnp.sum(dqkv[...].astype(F32), axis=0, keepdims=True)
    hi = sums.astype(BF16)
    lo = (sums - hi.astype(F32)).astype(BF16)
    both = jnp.concatenate([hi, lo, jnp.zeros((14, 3 * width), BF16)], axis=0)
    shift1 = dot_nt(wq[...].reshape(width, 3 * width), both)
    shift1 = shift1[:, 0:1] + shift1[:, 1:2]
    first = (jnp.zeros((1, 1), jnp.int32) + t) == 0
    zero = jnp.zeros((1, width), F32)
    for_zero = jnp.concatenate([zero, zero, vec[1:2, :], vec[3:4, :], zero, zero], axis=0)
    for_one = jnp.concatenate([vec[0:1, :], vec[4:5, :], vec[2:3, :], zero, zero, zero], axis=0)
    ends = jnp.concatenate([1.0 / row(gains, 0), row(biases, 0)], axis=0)
    lines = jnp.concatenate([for_zero, ends, for_one, ends], axis=0).T
    lane = lax.broadcasted_iota(jnp.int32, (1, 8), 1)
    if with_hid:
        columns = jnp.broadcast_to(hid[...], (8, hid.shape[1])).T
    for e in range(blocks):
        at_block = slice(e * block, (e + 1) * block)
        if with_hid:
            pick = columns[2 * e * block : (2 * e + 1) * block] * (lane == 4).astype(F32)
            pick = pick + columns[(2 * e + 1) * block : (2 * e + 2) * block] * (lane == 5).astype(F32)
        else:
            pick = jnp.zeros((block, 8), F32)
        small[scal[4 + e]] = jnp.concatenate(
            [lines[at_block, :8], lines[at_block, 8:], pick,
             jnp.zeros((block, LANES - 24), F32)], axis=1
        )
    sv = small[...].reshape(width, LANES)
    zeros_set, ones_set, own = sv[:, :8], sv[:, 8:16], sv[:, 16:24]
    gain1 = zeros_set[:, 6:7] * (inner - zeros_set[:, 7:8] * shift1)
    zeros_set = zeros_set + gain1 * (lane == 0).astype(F32) + shift1 * (lane == 1).astype(F32)
    used = (lane < 4).astype(F32)
    zeros_set, ones_set = zeros_set * used, ones_set * used
    keep_set = jnp.where(first, zeros_set, ones_set) + own
    send_set = jnp.where(first, ones_set, zeros_set)
    for hh in range(2):
        value = jnp.where((jnp.zeros((1, 1), jnp.int32) + t) == hh, keep_set, send_set)
        hi = value.astype(BF16).astype(F32)
        fill = jnp.zeros((width, LANES // 2 - 8), F32)
        tails[hh] = jnp.concatenate([hi, fill, value - hi, fill], axis=1).astype(BF16)
    stores += move(tails.at[1 - t], send_b, 1, width, 16)
    stores += move(tails.at[t], keep_b, 1, width, 36)
    for c in stores:
        c.wait()


def input_back_kernel(
    scal, dm_any, h_any, gains, dqkv_any, wq_any, order_any,
    tok_keep, tok_send,
    h_v, wq, dm, dqkv, da, sems,
):
    n, width = dm.shape
    caps, half_len, _ = tok_keep.shape
    t = scal[0]
    loads = [
        load(src, dst, sems.at[i])
        for i, (src, dst) in enumerate(
            ((dqkv_any, dqkv), (wq_any, wq),
             (h_any.at[pl.ds(pl.multiple_of(t * n, n), n)], h_v), (dm_any, dm))
        )
    ]
    loads[0].wait()
    loads[1].wait()

    def back(j, carry):
        rows = pl.ds(pl.multiple_of(j * 256, 256), 256)
        da[:, rows] = dot_nt(dqkv[...], wq[rows, :])
        return carry

    lax.fori_loop(0, width // 256, back, 0, unroll=3)
    loads[2].wait()
    loads[3].wait()
    piece = 8 * 2 * half_len
    first = (jnp.zeros((1, 1, 1), jnp.int32) + t) == 0

    def norm(i, carry):
        rows = pl.ds(pl.multiple_of(i * piece, piece), piece)
        xhat, rstd = norm_stats(h_v[rows, :].astype(F32))
        grad = dm[rows, :] + norm_back(da[rows, :] * row(gains, 0), xhat, rstd)
        halves = grad.reshape(8, 2, half_len, width)
        at = pl.ds(pl.multiple_of(i * 8, 8), 8)
        tok_keep[at] = jnp.where(first, halves[:, 0], halves[:, 1])
        tok_send[at] = jnp.where(first, halves[:, 1], halves[:, 0]).astype(BF16)
        return carry

    lax.fori_loop(0, n // piece, norm, 0)


def reduce_grad_kernel(
    rows_block, length, expo, g_any, images_any, texts_any, gall_any, extra_any, order_any,
    red_out, bias_out,
    g_v, images, texts, gall, extra, acc, sems,
):
    total, width = images.shape
    blocks = total // rows_block
    share = red_out.shape[0]
    whole = load(images_any, images, sems.at[0])
    scale = jnp.exp(jnp.full((1, 1), expo[0], F32))
    acc[...] = jnp.zeros_like(acc)
    whole.wait()

    def block(b, rb):
        rows = pl.ds(pl.multiple_of(b * rows_block, 16), rows_block)
        waits = [
            load(src.at[rows], dst, sems.at[1 + i])
            for i, (src, dst) in enumerate(
                ((g_any, g_v), (texts_any, texts), (gall_any, gall), (extra_any, extra))
            )
        ]
        for c in waits:
            c.wait()
        def project(i, rb):
            at = pl.ds(pl.multiple_of(i * 96, 96), 96)
            dt = scale * dot(g_v[at, :], images[...])
            tx = texts[at, :].astype(F32)
            part = (dt - tx * jnp.sum(tx * dt, axis=1, keepdims=True)) * (1.0 / length)
            part = part.astype(BF16)
            texts[at, :] = part
            inv = jnp.sum(extra[at, EXTRA : EXTRA + 3], axis=1, keepdims=True)
            return rb + jnp.sum(part.astype(F32) * inv, axis=0, keepdims=True)

        rb = lax.fori_loop(0, rows_block // 96, project, rb)
        acc[...] += dot_tn(gall[...], texts[...])
        return rb

    rb = lax.fori_loop(0, blocks, block, jnp.zeros((1, width), F32))
    red_out[...] = acc[:share, :]
    bias_out[...] = jnp.broadcast_to(rb * float(length), bias_out.shape)


def to_wire(x, width):
    low = x.astype(BF16)
    if x.shape[1] == width:
        return low
    rest = x[:, width:] - low[:, width:].astype(F32)
    return jnp.concatenate([low, rest.astype(BF16)], axis=1)


def from_wire(x, width):
    y = x.astype(F32)
    if x.shape[1] == width:
        return y
    return jnp.concatenate([y[:, :width], y[:, width : width + 64] + y[:, width + 64 :]], axis=1)


def wire_kernel(width, qa, qa_back, qb, qb_back, far_a, far_b, wire_a, wire_b, a0, a1, b0, b1,
                sems):
    loads = [
        load(src.at[0], dst, sems.at[i])
        for i, (src, dst) in enumerate(((qa, a0), (qa_back, a1), (qb, b0), (qb_back, b1)))
    ]
    loads[0].wait()
    loads[1].wait()
    wire_a[...] = (a0[...].astype(F32) + a1[...].astype(F32)).astype(BF16)
    loads[2].wait()
    loads[3].wait()
    wire_b[...] = to_wire(from_wire(b0[...], width) + from_wire(b1[...], width), width)


def turn_kernel(width, stacked, count, *refs):
    ins, (kept_a, kept_b, next_a, next_b) = refs[: 2 * count], refs[2 * count : 2 * count + 4]
    scratch, sems = refs[2 * count + 4 : -1], refs[-1]
    loads = [
        load(src.at[1] if i % count < stacked else src, dst, sems.at[i])
        for i, (src, dst) in enumerate(zip(ins, scratch))
    ]
    half = kept_a.shape[0]
    for side, (kept, moved) in enumerate(((kept_a, next_a), (kept_b, next_b))):
        at = range(side * count, (side + 1) * count)
        for i in at:
            loads[i].wait()
        total = from_wire(scratch[at[0]][...], width)
        for i in at[1:]:
            total = total + from_wire(scratch[i][...], width)
        kept[...] = total[:half]
        moved[...] = to_wire(total[half:], width)


def merge_kernel(width, sum_a, sum_b, hop_a, hop_b, *rest):
    outs = rest[-4:]
    for i, out in enumerate(outs):
        rows = out.shape[0]
        at = slice(i * rows, (i + 1) * rows)
        a = sum_a[at, :] + hop_a[at, :].astype(F32)
        b = sum_b[at, :] + from_wire(hop_b[at, :], width)
        if i == 0:
            out[:, :width] = a
            out[:, width:] = b
        else:
            out[:, :width] = a.astype(BF16)
            out[:, width:] = to_wire(b, width)


def finish_kernel(width, scal, total, hop_1, hop_2, hop_3, rbias,
                  qkv_out, project_out, gains_out, biases_out, hid_out):
    half = width // 2
    rows, cols = project_out.shape[0], width
    t, d = scal[0], scal[1]
    acc = total[...]
    for hop in (hop_1, hop_2, hop_3):
        x = hop[...]
        acc = acc + jnp.concatenate(
            [x[:, :width].astype(F32), from_wire(x[:, width:], width)], axis=1
        )
    project_out[...] = acc[:, :half]
    qkv_out[...] = acc[:, half : 2 * width]
    small = acc[:, 2 * width : 2 * width + 8].T
    lane = lax.broadcasted_iota(jnp.int32, (rows, cols), 1)
    mine = lax.broadcasted_iota(jnp.int32, (rows, cols), 0) + d * rows
    last = jnp.sum(jnp.where(lane == mine, rbias[0:1, :], 0.0), axis=1, keepdims=True)
    last = jnp.broadcast_to(last, (rows, 8)).T
    first = (jnp.zeros((1, 1), jnp.int32) + t) == 0
    gains_out[...] = small[0:1]
    biases_out[...] = jnp.concatenate(
        [small[1:3], jnp.where(first, small[3:4], last[0:1])], axis=0
    )
    hid_out[...] = jnp.concatenate([small[4:5], small[5:6]], axis=1)


def xor_permute(x, axis, bit):
    return lax.ppermute(x, axis, [(i, i ^ bit) for i in range(lax.axis_size(axis))])


def bit_groups(count):
    bits = [1 << i for i in range(count.bit_length() - 1)]
    groups = [tuple(bits[i : i + 2]) for i in range(0, len(bits), 2)]
    return groups[::-1]


def reaches(group):
    out = [0]
    for bit in group:
        out = out + [r ^ bit for r in out]
    return out


def slot_reaches(count):
    order = [0]
    for group in bit_groups(count):
        order = [r ^ o for r in reaches(group) for o in order]
    return order


def hop(sends, group):
    return [x if r == 0 else xor_permute(x, "dp", r) for x, r in zip(sends, reaches(group))]


def scatter_sum(s, groups, to_wire=lambda x: x, from_wire=lambda x: x):
    for group in reversed(groups):
        hops = reaches(group)
        rows = s.shape[0] // len(hops)
        parts = [s[i * rows : (i + 1) * rows] for i in range(len(hops))]
        moved = [xor_permute(to_wire(parts[i]), "dp", r) for i, r in enumerate(hops) if r]
        s = parts[0]
        for piece in moved:
            s = s + from_wire(piece)
    return s


def flip_by(x, index, count):
    for i in range(count.bit_length() - 1):
        bit = 1 << i
        shape = x.shape
        pairs = x.reshape((count // (2 * bit), 2, bit) + shape[1:])
        x = jnp.where((index & bit) != 0, pairs[:, ::-1], pairs).reshape(shape)
    return x


SMEM = pl.BlockSpec(memory_space=pltpu.SMEM)
VMEM = pl.BlockSpec(memory_space=pltpu.VMEM)
ANY = pl.BlockSpec(memory_space=pl.ANY)


def call(kernel, name, in_specs, outs, out_specs, scratch, args, flops, moved):
    return pl.pallas_call(
        kernel,
        name=name,
        in_specs=in_specs,
        out_shape=[jax.ShapeDtypeStruct(s, d) for s, d in outs],
        out_specs=out_specs,
        scratch_shapes=scratch,
        compiler_params=pltpu.CompilerParams(vmem_limit_bytes=VMEM_LIMIT),
        cost_estimate=pl.CostEstimate(flops=flops, bytes_accessed=moved, transcendentals=0),
    )(*args)


def body(
    pictures, captions, tallies, exponent,
    p_gains, p_biases, p_hid, p_wq, p_wp, p_we, p_wr,
    c_gains, c_biases, c_hid, c_wq, c_wp, c_we, c_wr,
):
    t = lax.axis_index("tower")
    d = lax.axis_index("dp")
    chips = lax.axis_size("dp")
    pairs, length, width = captions.shape
    img_len = pictures.shape[1]
    hidden = c_hid.shape[0]
    caps = pairs // 2
    n = caps * length
    total = pairs * chips
    row_blocks = 16
    order = np.array(slot_reaches(chips))
    slot_of = np.zeros(chips, np.int32)
    slot_of[order] = np.arange(chips)
    table = np.stack([slot_of[np.arange(chips) ^ i] for i in range(chips)]).astype(np.int32)
    slots = lax.dynamic_slice_in_dim(jnp.asarray(table), d, 1, 0)[0]
    relative = chips == row_blocks
    row_slots = slots if relative else jnp.arange(row_blocks, dtype=jnp.int32)
    head = jnp.stack([t, d, tallies[0], t]).astype(jnp.int32)
    scal = jnp.concatenate([head, row_slots, slots])

    texts_in = captions.reshape(pairs * length, width)
    c_hid2, p_hid2 = c_hid.reshape(1, hidden), p_hid.reshape(1, hidden)
    blk = (row_blocks, width // row_blocks, n)
    vm = pltpu.VMEM
    sem = pltpu.SemaphoreType.DMA
    half_hid = (n, hidden // 2)
    chunk = width + 2 * LANES
    a_t, qkv, o_t, m, c_t, gp_keep, gp_send, text_send, emb, r = call(
        text_forward_kernel, "text_forward",
        [SMEM, ANY, VMEM, VMEM, VMEM, ANY, ANY, ANY, ANY],
        [(blk, BF16), ((n, 3 * width), BF16), (blk, BF16), ((n, width), F32), (blk, BF16),
         (half_hid, BF16), (half_hid, BF16), ((chips, caps, chunk), BF16),
         ((caps, width), F32), ((caps, LANES), F32)],
        [ANY] * 7 + [VMEM] * 3,
        [vm((n, width), BF16), vm((width, 3 * width), BF16), vm((width, width), BF16),
         vm((width, hidden), BF16), vm((hidden, width), BF16), vm((1, 3 * width), F32),
         vm((n, width), BF16), vm((n, width), BF16), vm((caps, hidden), F32), vm(blk, BF16), vm((n, 3 * width), BF16),
         vm(blk, BF16), vm((n, width), F32), vm(blk, BF16), vm(half_hid, BF16),
         vm(half_hid, BF16), sem((5,)), sem((7,))],
        (scal, texts_in, c_gains, c_biases, c_hid2, c_wq, c_wp, c_we, c_wr),
        int(2 * n * width * (4 * width + hidden)), 20_000_000,
    )
    c_far = xor_permute(c_t, "tower", 1)
    gp_far = xor_permute(gp_send, "tower", 1)
    text_all = lax.all_to_all(text_send, "dp", 0, 0, tiled=True)

    rows = caps * PAD
    groups = bit_groups(chips)
    (image,) = call(
        image_forward_kernel, "image_forward",
        [SMEM, ANY, VMEM, VMEM, VMEM, ANY, ANY, ANY, ANY],
        [((caps, width), BF16)],
        [VMEM],
        [vm((img_len, pairs, width), BF16), vm((width // LANES, img_len * caps, LANES), F32),
         vm((rows, width), F32), vm((rows, width), BF16),
         vm((rows + 16, 3 * width), BF16), vm((rows, width), F32), vm((caps, width), F32),
         vm((caps, hidden), F32), vm((width, 3 * width), BF16), vm((width, width), BF16),
         vm((width, hidden), BF16), vm((hidden, width), BF16), vm((1, 3 * width), F32),
         vm((1, width), F32), sem((5,))],
        (scal, jnp.transpose(pictures, (1, 0, 2)), p_gains, p_biases, p_hid2,
         p_wq, p_wp, p_we, p_wr),
        int(2 * rows * width * (4 * width + hidden)), 20_000_000,
    )
    image, text_all = lax.optimization_barrier((image, text_all))
    text_par = xor_permute(text_all, "tower", 1)
    got = hop([image[None]] * len(reaches(groups[0])), groups[0])
    for group in groups[1:]:
        whole = jnp.concatenate(got, axis=0)
        got = hop([whole] * len(reaches(group)), group)
    par_all = xor_permute(jnp.concatenate(got, axis=0), "tower", 1)
    small_slice = total <= 768
    if not small_slice:
        got = [jnp.concatenate(got, axis=0)]

    block = total if small_slice else 96
    held = chips if small_slice else 1
    share = hidden // (2 * chips)
    piece_shape = (width // 2, width)
    (loss, temp, ea, eb, ec, ed, g_all, images_all, texts_all, gall, extra, dc, dy, hid_grad) = call(
        partial(loss_kernel, block, len(got)), "loss",
        [SMEM] + [ANY] * len(got) + [ANY, ANY, ANY, SMEM, VMEM, VMEM] + [ANY] * 6,
        [((1, 1), F32), ((1, 1), F32)] + [(piece_shape, BF16)] * 4
        + [((total, total), BF16), ((total, width), BF16), ((total, width), BF16),
           ((total, LANES), BF16), ((total, LANES), F32), ((n, width), F32), ((caps, width), F32),
           ((1, hidden // 2), F32)],
        [VMEM, VMEM] + [ANY] * 10 + [VMEM, VMEM],
        [vm((held, caps, width), BF16), vm((held, caps, width), BF16),
         vm((held, caps, chunk), BF16), vm((held, caps, chunk), BF16),
         vm((total, width), BF16), vm((total, width), BF16), vm((total, LANES), F32),
         vm((total, LANES), BF16), vm((8, total), F32),
         vm((block, total), F32), vm((block, total), BF16), vm((2 * caps, total), BF16),
         vm(half_hid, BF16), vm(half_hid, BF16), vm((2,) + blk, BF16),
         vm((width, hidden // 2), BF16), vm((hidden // 2, width), BF16),
         vm((n, width), F32), vm((2, width, hidden // 4), BF16), sem((16,)), sem((14,))],
        (scal, *got, par_all, text_all, text_par, exponent, emb, r, gp_keep, gp_far,
         c_t, c_far, c_we, c_wr),
        int(3 * n * width * hidden), 20_000_000,
    )

    def widen(x):
        return x.astype(F32)

    def narrow(x):
        return x.astype(BF16)

    e_hops = [xor_permute(ea, "dp", 1), xor_permute(eb, "dp", 2)] if relative else []
    dm, dqkv, vec = call(
        middle_back_kernel, "middle_back",
        [SMEM, ANY, VMEM, ANY, ANY, VMEM] + [ANY] * 4,
        [((n, width), F32), ((n, 3 * width), BF16), ((8, width), F32)],
        [ANY, ANY, VMEM],
        [vm((n, width), F32), vm(half_hid, BF16), vm((n, width), F32),
         vm((width, hidden // 2), BF16), vm((hidden // 2, width), BF16), vm((width, width), BF16),
         vm((n, 3 * width), BF16), vm((n, width), F32), vm((n, width), BF16),
         vm((n, width), BF16), vm((n, 3 * width), BF16), sem((12,))],
        (scal, dc, dy, gp_send, m, c_gains, c_we, c_wr, c_wp, qkv),
        int(2 * n * width * (hidden + 4 * width)), 20_000_000,
    )
    b_shape = (width // 2, width + LANES)
    quarter_shape = (width // 4, width)
    qa_keep, qb_keep, qa_send, qb_send, *turned = call(
        partial(weight_grad_kernel, relative), "weight_grad",
        [SMEM] + [ANY] * 5 + [VMEM] * 4 + [ANY] * (4 if relative else 0),
        [((2,) + piece_shape, BF16), ((2,) + b_shape, BF16)] * 2
        + ([(quarter_shape, F32)] * 2 + [(quarter_shape, BF16)] * 2 if relative else []),
        [ANY] * 4 + [VMEM] * (4 if relative else 0),
        [vm((n, width), F32), vm(blk, BF16), vm(blk, BF16), vm((n, width), BF16),
         vm((n, 3 * width), BF16), vm((row_blocks, width // row_blocks, 3 * width), BF16),
         vm((2, 4, width, width // 2), BF16), vm((2, width, LANES), BF16), vm((width, LANES), F32),
         vm((row_blocks, width // row_blocks, LANES), F32), sem((8 + row_blocks,)), sem((40,))]
        + ([vm(piece_shape, BF16)] * 4 + [sem((4,))] if relative else []),
        (scal, dm, dqkv, a_t, o_t, c_wq, c_gains, c_biases, vec, hid_grad)
        + ((ec, e_hops[0], ed, e_hops[1]) if relative else ()),
        int(2 * n * width * 4 * width), 20_000_000,
    )
    qa_back = xor_permute(qa_send, "tower", 1)
    qb_back = xor_permute(qb_send, "tower", 1)
    cols = width // chips
    if relative:
        e_parts = (
            turned[0], turned[1], xor_permute(turned[2], "dp", 2), xor_permute(turned[3], "dp", 1)
        )
        wire_a, wire_b = call(
            partial(wire_kernel, width), "wire", [ANY] * 6,
            [(piece_shape, BF16), (b_shape, BF16)], [VMEM] * 2,
            [vm(piece_shape, BF16)] * 2 + [vm(b_shape, BF16)] * 2 + [sem((4,))],
            (qa_keep, qa_back, qb_keep, qb_back, *e_parts[2:]), 1_000_000, 4_000_000,
        )
        q_hops = [xor_permute(wire_a, "dp", 1), xor_permute(wire_b, "dp", 2)]
    else:
        q_sums = [
            from_wire(x[i], width) + from_wire(y[i], width)
            for i in range(2)
            for x, y in ((qa_keep, qa_back), (qb_keep, qb_back))
        ]
        tails = jnp.transpose(hid_grad.reshape(chips, 2, cols), (0, 2, 1)).reshape(width, 2)
        tails = jnp.pad(tails, ((0, 0), (width + 4, 64 - 6)))
        quarter = width // 4
        for i in (1, 3):
            q_sums[i] = q_sums[i] + jnp.concatenate(
                [tails[q * quarter : (q + 1) * quarter] for q in QUARTERS[i]], axis=0
            )
        wire_b = qb_back
        q_hops = []
    tok_keep, tok_send = call(
        input_back_kernel, "input_back",
        [SMEM, ANY, ANY, VMEM, ANY, ANY, ANY],
        [((caps, length // 2, width), F32), ((caps, length // 2, width), BF16)],
        [VMEM] * 2,
        [vm((n, width), BF16), vm((width, 3 * width), BF16), vm((n, width), F32),
         vm((n, 3 * width), BF16), vm((n, width), F32), sem((4,))],
        (scal, dm, texts_in, c_gains, dqkv, c_wq, wire_b),
        int(2 * n * width * 3 * width), 9_000_000,
    )
    reduce_grad, rbias = call(
        partial(reduce_grad_kernel, block, length), "reduce_grad",
        [SMEM] + [ANY] * 6,
        [((share, width), F32), ((8, width), F32)],
        [VMEM, VMEM],
        [vm((block, total), BF16), vm((total, width), BF16), vm((block, width), BF16),
         vm((block, LANES), BF16), vm((block, LANES), F32), vm((LANES, width), F32), sem((5,))],
        (exponent, g_all, images_all, texts_all, gall, extra, q_hops[0] if relative else wire_b),
        int(2 * total * total * width), 6_000_000,
    )

    tok_back = widen(xor_permute(tok_send, "tower", 1))
    grad_tokens = jnp.concatenate(
        [jnp.where(t == 0, tok_keep, tok_back), jnp.where(t == 0, tok_back, tok_keep)], axis=0
    )
    half, third = width // 2, width // 4

    def plain(sums):
        sides = []
        for side in range(2):
            at = {}
            for i in (side, side + 2):
                for j, q in enumerate(QUARTERS[i]):
                    at[q] = sums[i][j * third : (j + 1) * third]
            x = jnp.concatenate([at[q] for q in range(4)], axis=0)
            x = flip_by(x.reshape((chips, cols) + x.shape[1:]), d, chips)
            x = x[order].reshape((width,) + x.shape[2:])
            sides.append(
                scatter_sum(x, groups, lambda v: to_wire(v, width), lambda v: from_wire(v, width))
            )
        return sides

    if not relative:
        expand_grad = jnp.concatenate(plain([widen(x) for x in (ea, eb, ec, ed)]), axis=1)
        side_a, side_b = plain(q_sums)
        small = side_b[:, width : width + 8].T
        last = jnp.where(
            t == 0, small[3], lax.dynamic_slice_in_dim(rbias[0], d * cols, cols, 0)
        )
        return (
            loss.reshape(1), temp.reshape(1), grad_tokens, small[0:1], jnp.stack([small[1], small[2], last]),
            small[4:6].reshape(2 * cols),
            jnp.concatenate([side_a[:, half:], side_b[:, :width]], axis=1), side_a[:, :half],
            expand_grad, reduce_grad,
        )

    def second_hops(side_a, side_b, stacked, name):
        count = len(side_a)
        shapes = [x.shape[-2:] for x in (*side_a, *side_b)]
        small = shapes[-1][1] - width
        kept_a, kept_b, next_a, next_b = call(
            partial(turn_kernel, width, stacked, count), name, [ANY] * (2 * count),
            [((third, width), F32), ((third, width + small // 2), F32),
             ((third, width), BF16), ((third, width + small), BF16)],
            [VMEM] * 4, [vm(x, BF16) for x in shapes] + [sem((2 * count,))],
            (*side_a, *side_b), 1_000_000, 4_000_000,
        )
        return kept_a, kept_b, xor_permute(next_a, "dp", 2), xor_permute(next_b, "dp", 1)

    def merge(parts, after, name):
        f32_cols = parts[0].shape[1] + parts[1].shape[1]
        bf_cols = parts[2].shape[1] + parts[3].shape[1]
        return call(
            partial(merge_kernel, width), name, [VMEM] * 4 + [ANY] * len(after),
            [((cols, f32_cols), F32)] + [((cols, bf_cols), BF16)] * 3, [VMEM] * 4, [],
            (*parts, *after), 1_000_000, 3_000_000,
        )

    def z_hops(pieces):
        return [xor_permute(x, "dp", r) for x, r in zip(pieces, reaches(groups[0])[1:])]

    e_own, *e_far = merge(e_parts, (wire_b,), "merge_expand")
    e_back = z_hops(e_far)
    expand_grad = e_own + sum(widen(x) for x in e_back)
    q_parts = second_hops(
        (qa_keep, qa_back, q_hops[0]), (qb_keep, qb_back, q_hops[1]), 2, "turn_qkv"
    )
    q_own, *q_far = merge(q_parts, e_back, "merge_qkv")
    q_in = z_hops(q_far)
    qkv_grad, project_grad, gains_grad, biases_grad, hid_rows = call(
        partial(finish_kernel, width), "finish", [SMEM] + [VMEM] * 5,
        [((cols, 3 * half), F32), ((cols, half), F32), ((1, cols), F32), ((3, cols), F32),
         ((1, 2 * cols), F32)],
        [VMEM] * 5, [], (scal, q_own, *q_in, rbias), 1_000_000, 2_000_000,
    )
    return (
        loss.reshape(1), temp.reshape(1), grad_tokens, gains_grad, biases_grad, hid_rows.reshape(2 * cols),
        qkv_grad, project_grad, expand_grad, reduce_grad,
    )


def solution(mesh):
    in_specs = (P("dp", None, None), P("dp", None, None), P("dp")) + (P(),) * 15
    out_specs = (
        P(), P(), P("dp", "tower", None), P("tower", "dp"), P("tower", "dp"),
        P(("tower", "dp")), P("dp", "tower"), P("dp", "tower"), P("dp", "tower"),
        P(("tower", "dp"), None),
    )
    return jax.shard_map(body, mesh=mesh, in_specs=in_specs, out_specs=out_specs, check_vma=False)
```

```python
import math
from functools import partial

import jax
import jax.numpy as jnp
import numpy as np
from jax import lax
from jax.experimental import pallas as pl
from jax.experimental.pallas import tpu as pltpu
from jax.sharding import PartitionSpec as P

F32 = jnp.float32
BF16 = jnp.bfloat16
HEAD_DIM = 64
LANES = 128
EXTRA = 120
norm_eps = 1e-06
embed_eps = 1e-06
NEG = -1000000000.0
VMEM_LIMIT = 60 * 1024 * 1024
MARGIN = 8 * 1024 * 1024
SMALL = ("merge_expand", "merge_qkv", "finish", "reduce_grad")


def normal_cdf(x):
    return 0.5 + 0.5 * lax.erf(x * 0.7071067811865476)


def load(src, dst, sem):
    copy = pltpu.make_async_copy(src, dst, sem)
    copy.start()
    return copy


def dot(a, b):
    return jnp.dot(a, b, preferred_element_type=F32)


def dot_nt(a, b):
    return lax.dot_general(a, b, (((1,), (1,)), ((), ())), preferred_element_type=F32)


def dot_tn(a, b):
    return lax.dot_general(a, b, (((0,), (0,)), ((), ())), preferred_element_type=F32)


def norm_stats(x):
    mean = jnp.mean(x, axis=-1, keepdims=True)
    centered = x - mean
    rstd = lax.rsqrt(jnp.mean(centered * centered, axis=-1, keepdims=True) + norm_eps)
    return centered * rstd, rstd


def norm_back(dxhat, xhat, rstd):
    return rstd * (
        dxhat
        - jnp.mean(dxhat, axis=-1, keepdims=True)
        - xhat * jnp.mean(dxhat * xhat, axis=-1, keepdims=True)
    )


def row(ref, i):
    return ref[i : i + 1, :].astype(F32)


def head_masks():
    lane = lax.broadcasted_iota(jnp.int32, (1, LANES), 1)
    first = (lane < HEAD_DIM).astype(BF16)
    return first, (1 - first).astype(BF16)


def set_qkv_bias(out, biases):
    width = biases.shape[1]
    out[:, :width] = row(biases, 2)
    out[:, width : 2 * width] = jnp.zeros((1, width), F32)
    out[:, 2 * width :] = row(biases, 3)


def set_hidden_bias(out, hid):
    lines = hid[...].astype(F32)
    for i in range(hid.shape[0]):
        out[:, i * LANES : (i + 1) * LANES] = lines[i : i + 1]


def two_heads(x, masks):
    return jnp.concatenate([x * masks[0], x * masks[1]], axis=0)


def softmax_parts(scores, bias):
    keys = scores.shape[1] // 2
    parts = []
    for e in range(2):
        s = scores[:, e * keys : (e + 1) * keys] + bias
        parts.append(jnp.exp(s - jnp.max(s, axis=-1, keepdims=True)))
    return parts


def attend(q2, k2, v2, bias, masks):
    e0, e1 = softmax_parts(dot_nt(q2 * BF16(0.125), two_heads(k2, masks)), bias)
    weights = jnp.concatenate([e0.astype(BF16), e1.astype(BF16)], axis=1)
    ones = jnp.ones((k2.shape[0], LANES), BF16)
    right = jnp.concatenate([two_heads(v2, masks), two_heads(ones, masks)], axis=1)
    out = dot(weights, right)
    return (out[:, :LANES] / out[:, LANES:]).astype(BF16)


def split_dot(x, w):
    hi = x.astype(BF16)
    lo = (x - hi.astype(F32)).astype(BF16)
    n = x.shape[0]
    out = dot(jnp.concatenate([hi, lo], axis=0), w)
    return out[:n] + out[n:]


def text_forward_kernel(
    scal, h_any, gains, biases, hid, wq_any, wp_any, we_any, wr_any,
    a_any, qkv_any, o_any, m_any, c_any, gpk_any, gps_any, send_out, emb_out, r_out,
    h_v, wq, wp, we, wr, qb, hb, av, cv, gsum, a_out, qkv_out, o_out, m_out, c_out, gp_keep, gp_send,
    sems, out_sems,
):
    n, width = m_out.shape
    caps = emb_out.shape[0]
    length = n // caps
    hidden = hid.shape[0] * LANES
    t, d = scal[0], scal[1]
    load_h = load(h_any.at[pl.ds(pl.multiple_of(t * n, n), n)], h_v, sems.at[0])
    load_q = load(wq_any, wq, sems.at[1])
    load_h.wait()
    masks = head_masks()

    def put_transposed(out, src):
        count, rows = out.shape[:2]

        def turn(i, carry):
            lanes = pl.ds(pl.multiple_of(i * (width // 2), LANES), width // 2)
            turned = src[:, lanes].astype(F32).T.astype(BF16)
            for e in range(count // 2):
                out[scal[4 + i * (count // 2) + e]] = turned[e * rows : (e + 1) * rows, :]
            return carry

        lax.fori_loop(0, 2, turn, 0, unroll=2)

    h = h_v[...].astype(F32)
    xhat, _ = norm_stats(h)
    a = xhat * row(gains, 0) + row(biases, 0)
    av[...] = a.astype(BF16)
    load_q.wait()
    load_p = load(wp_any, wp, sems.at[2])
    load_e = load(we_any, we, sems.at[3])
    load_r = load(wr_any, wr, sems.at[4])
    set_qkv_bias(qb, biases)
    set_hidden_bias(hb, hid)

    def to_qkv(j, carry):
        cols = pl.ds(pl.multiple_of(j * 256, 256), 256)
        qkv_out[:, cols] = (dot(av[...], wq[:, cols]) + qb[:, cols]).astype(BF16)
        return carry

    lax.fori_loop(0, 3 * width // 256, to_qkv, 0, unroll=9)
    put_transposed(a_out, av)
    stores = [load(qkv_out, qkv_any, out_sems.at[0]), load(a_out, a_any, out_sems.at[1])]
    same = (
        lax.broadcasted_iota(jnp.int32, (LANES, LANES), 0) // length
        == lax.broadcasted_iota(jnp.int32, (LANES, LANES), 1) // length
    )
    bias = jnp.where(same, 0.0, -1e30)

    def attention(g, carry):
        rows = pl.ds(pl.multiple_of(g * LANES, LANES), LANES)
        for p in range(width // LANES):
            lanes = slice(p * LANES, (p + 1) * LANES)
            q2 = qkv_out[rows, lanes]
            k2 = qkv_out[rows, width + p * LANES : width + (p + 1) * LANES]
            v2 = qkv_out[rows, 2 * width + p * LANES : 2 * width + (p + 1) * LANES]
            av[rows, lanes] = attend(q2, k2, v2, bias, masks)
        return carry

    lax.fori_loop(0, n // LANES, attention, 0)
    load_p.wait()
    m = h_v[...].astype(F32) + dot(av[...], wp[...]) + row(biases, 4)
    m_out[...] = m
    stores.append(load(m_out, m_any, out_sems.at[2]))
    xhat, _ = norm_stats(m)
    c = xhat * row(gains, 1) + row(biases, 1)
    cv[...] = c.astype(BF16)
    put_transposed(c_out, cv)
    put_transposed(o_out, av)
    stores.append(load(c_out, c_any, out_sems.at[3]))
    stores.append(load(o_out, o_any, out_sems.at[4]))
    load_e.wait()
    half = hidden // 512

    def feed(rel, gp_out):
        def step(j, carry):
            local = pl.ds(pl.multiple_of(j * 256, 256), 256)
            at = jnp.bitwise_xor(t, rel) * half + j
            cols = pl.ds(pl.multiple_of(at * 256, 256), 256)
            f = dot(cv[...], we[:, cols]) + hb[:, cols]
            cdf = normal_cdf(f)
            density = jnp.exp(f * f * -0.5) * 0.3989422804014327
            gp_out[:, local] = (cdf + f * density).astype(BF16)
            gsum[:, cols] = jnp.sum((f * cdf).reshape(caps, length, 256), axis=1)
            return carry

        lax.fori_loop(0, half, step, 0, unroll=2)

    feed(1, gp_send)
    stores.append(load(gp_send, gps_any, out_sems.at[5]))
    feed(0, gp_keep)
    stores.append(load(gp_keep, gpk_any, out_sems.at[6]))
    load_r.wait()
    total = gsum[...]
    pooled = (
        jnp.mean(m_out[...].reshape(caps, length, width), axis=1)
        + split_dot(total * (1.0 / length), wr[...])
        + row(biases, 5)
    )
    r = lax.rsqrt(jnp.sum(pooled * pooled, axis=-1, keepdims=True) + embed_eps)
    emb_out[...] = pooled * r
    r_out[...] = jnp.broadcast_to(r, r_out.shape)
    chips = send_out.shape[0]
    share = hidden // (2 * chips)
    scaled = total * r
    hi = r.astype(BF16).astype(F32)
    mid = (r - hi).astype(BF16).astype(F32)
    slot = lax.broadcasted_iota(jnp.int32, (caps, LANES), 0) + t * caps
    lane = lax.broadcasted_iota(jnp.int32, (caps, LANES), 1)
    extra = jnp.where(lane == EXTRA, hi, 0.0)
    extra = jnp.where(lane == EXTRA + 1, mid, extra)
    extra = jnp.where(lane == EXTRA + 2, r - hi - mid, extra)
    extra = jnp.where((lane == EXTRA + 3) & (slot < scal[2]), 1.0, extra)
    for e in range(chips):
        send_out[e, :, :width] = (pooled * r).astype(BF16)
        for half_at in range(2):
            src = (half_at * chips + e) * share
            piece = jnp.concatenate([scaled[:, src : src + share], extra[:, share:]], axis=1)
            to = width + jnp.bitwise_xor(t, half_at) * LANES
            send_out[e, :, pl.ds(pl.multiple_of(to, LANES), LANES)] = piece.astype(BF16)
    for c in stores:
        c.wait()


PAD = 56


def image_forward_kernel(
    scal, x_any, gains, biases, hid, wq_any, wp_any, we_any, wr_any,
    out,
    x_v, xs, hv, av, qkv, mv, msum, gsum, wq, wp, we, wr, qb, hb, pb, sems,
):
    length, both_caps, width = x_v.shape
    caps = both_caps // 2
    n = caps * PAD
    hidden = hid.shape[0] * LANES
    t = scal[0]
    load_x = load(x_any, x_v, sems.at[0])
    load_q = load(wq_any, wq, sems.at[1])
    masks = head_masks()
    qkv[n:, :] = jnp.zeros((qkv.shape[0] - n, 3 * width), BF16)
    first = (jnp.zeros((1, 1), jnp.int32) + t) == 0
    load_x.wait()

    def pick(i, carry):
        x = x_v[i].astype(F32)
        x = jnp.where(first, x[:caps], x[caps:])
        for k in range(width // LANES):
            xs[k, pl.ds(pl.multiple_of(i * caps, 8), caps), :] = x[:, k * LANES : (k + 1) * LANES]
        return carry

    lax.fori_loop(0, length, pick, 0, unroll=2)

    def first_norm(j, carry):
        base = pl.multiple_of(j * 2 * PAD, 16)
        for e in range(2):
            x = jnp.concatenate(
                [
                    xs[k, pl.ds(j * 2 + e, length, stride=caps), :]
                    for k in range(width // LANES)
                ],
                axis=1,
            )
            x = jnp.concatenate([x, jnp.zeros((PAD - length, width), F32)], axis=0)
            hv[pl.ds(base + e * PAD, PAD), :] = x
            xhat, _ = norm_stats(x)
            x = xhat * row(gains, 0) + row(biases, 0)
            if e == 0:
                kept = x
        av[pl.ds(base, 2 * PAD), :] = jnp.concatenate([kept, x], axis=0).astype(BF16)
        return carry

    lax.fori_loop(0, caps // 2, first_norm, 0, unroll=4)
    load_q.wait()
    load_p = load(wp_any, wp, sems.at[2])
    load_e = load(we_any, we, sems.at[3])
    load_r = load(wr_any, wr, sems.at[4])
    set_qkv_bias(qb, biases)
    set_hidden_bias(hb, hid)

    def to_qkv(j, carry):
        cols = pl.ds(pl.multiple_of(j * 256, 256), 256)
        qkv[:n, cols] = (dot(av[...], wq[:, cols]) + qb[:, cols]).astype(BF16)
        return carry

    lax.fori_loop(0, 3 * width // 256, to_qkv, 0, unroll=9)
    q_at = lax.broadcasted_iota(jnp.int32, (2 * PAD, LANES), 0)
    k_at = lax.broadcasted_iota(jnp.int32, (2 * PAD, LANES), 1)
    low = (q_at < PAD) & (k_at < length)
    high = (q_at >= PAD) & (k_at >= PAD) & (k_at < PAD + length)
    bias = jnp.where(low | high, 0.0, -1e30)

    def attention(j, carry):
        base = pl.multiple_of(j * 2 * PAD, 16)
        rows, keys = pl.ds(base, 2 * PAD), pl.ds(base, LANES)
        for p in range(width // LANES):
            lanes = slice(p * LANES, (p + 1) * LANES)
            q2 = qkv[rows, lanes]
            k2 = qkv[keys, width + p * LANES : width + (p + 1) * LANES]
            v2 = qkv[keys, 2 * width + p * LANES : 2 * width + (p + 1) * LANES]
            av[rows, lanes] = attend(q2, k2, v2, bias, masks)
        return carry

    lax.fori_loop(0, caps // 2, attention, 0, unroll=2)
    load_p.wait()
    pb[...] = row(biases, 4)

    def add_attended(j, carry):
        cols = pl.ds(pl.multiple_of(j * 256, 256), 256)
        mv[:, cols] = hv[:, cols] + dot(av[...], wp[:, cols]) + pb[:, cols]
        return carry

    lax.fori_loop(0, width // 256, add_attended, 0, unroll=3)
    group = 8 * PAD
    tail = (lax.broadcasted_iota(jnp.int32, (1, 8, 1), 1) < length - (PAD - 8)).astype(F32)

    def token_sum(x, count):
        tiles = x.reshape(count, PAD // 8, 8, x.shape[1])
        acc = tiles[:, PAD // 8 - 1] * tail
        for i in range(PAD // 8 - 1):
            acc = acc + tiles[:, i]
        return jnp.sum(acc, axis=1)

    def second_norm(j, carry):
        rows = pl.ds(pl.multiple_of(j * group, 16), group)
        m = mv[rows, :]
        xhat, _ = norm_stats(m)
        av[rows, :] = (xhat * row(gains, 1) + row(biases, 1)).astype(BF16)
        msum[pl.ds(pl.multiple_of(j * 8, 8), 8), :] = token_sum(m, 8)
        return carry

    lax.fori_loop(0, caps // 8, second_norm, 0)
    load_e.wait()

    def feed(j, carry):
        cols = pl.ds(pl.multiple_of(j * 256, 256), 256)
        f = dot(av[...], we[:, cols]) + hb[:, cols]
        gsum[:, cols] = token_sum(f * normal_cdf(f), caps)
        return carry

    lax.fori_loop(0, hidden // 256, feed, 0, unroll=2)
    load_r.wait()
    scale = 1.0 / length
    pooled = msum[...] * scale + split_dot(gsum[...] * scale, wr[...]) + row(biases, 5)
    r_img = lax.rsqrt(jnp.sum(pooled * pooled, axis=-1, keepdims=True) + embed_eps)
    out[...] = (pooled * r_img).astype(BF16)


QUARTERS = ((1, 3), (2, 3), (0, 2), (0, 1))


def loss_kernel(
    rows_block, parts, scal, *refs,
):
    own_any, refs = refs[:parts], refs[parts:]
    (par_any, text_any, text_par_any, expo, emb, r, gpk_any, gpr_any, ct_any, ctr_any,
     we_any, wr_any,
     loss_out, temp_out, ea, eb, ec, ed, g_any, images_any, texts_any, gall_any, extra_any,
     dc_any, dy_out, hid_out,
     own_v, par_v, text_v, text_par_v, texts, images, extra, gall, col_flag, sims, grad,
     chip_g, gpk, gpr, ct, we, wr, dc, exp_s, sems, out_sems) = refs
    chips, caps, width = par_any.shape
    staged = own_v.shape[0] == chips
    total = texts.shape[0]
    near_hidden = gpk.shape[1]
    n = dc.shape[0]
    length = n // caps
    t, d = scal[0], scal[1]
    first = (jnp.zeros((1, 1), jnp.int32) + t) == 0
    if staged:
        each = chips // parts
        waits = [
            load(par_any, par_v, sems.at[0]),
            load(text_any, text_v, sems.at[1]),
            load(text_par_any, text_par_v, sems.at[2]),
        ] + [
            load(own_any[i], own_v.at[pl.ds(i * each, each)], sems.at[3 + i]) for i in range(parts)
        ]
        for c in waits:
            c.wait()

    def place(e, carry):
        at, slot = e, scal[4 + 16 + e]
        if not staged:
            waits = [
                load(src.at[pl.ds(i, 1)], dst, sems.at[j])
                for j, (src, i, dst) in enumerate(
                    ((own_any[0], slot, own_v), (par_any, slot, par_v), (text_any, at, text_v),
                     (text_par_any, at, text_par_v))
                )
            ]
            for c in waits:
                c.wait()
            at = slot = 0

        def pair(x0, x1):
            x0, x1 = x0.astype(F32), x1.astype(F32)
            return jnp.concatenate([jnp.where(first, x0, x1), jnp.where(first, x1, x0)], axis=0)

        rows = pl.ds(pl.multiple_of(e * 2 * caps, 16), 2 * caps)
        images[rows, :] = pair(own_v[slot], par_v[slot]).astype(BF16)
        x0, x1 = text_v[at], text_par_v[at]
        texts[rows, :] = pair(x0[:, :width], x1[:, :width]).astype(BF16)
        last = pair(x0[:, width : width + LANES], x1[:, width + LANES :])
        extra[rows, :] = last
        gall[rows, :] = last.astype(BF16)
        return carry

    lax.fori_loop(0, chips, place, 0, unroll=2)
    half = near_hidden // 256
    later = [
        load(src, dst, sems.at[8 + i])
        for i, (src, dst) in enumerate(
            ((wr_any.at[pl.ds(pl.multiple_of(t * near_hidden, 256), near_hidden)], wr),
             (gpk_any, gpk), (gpr_any, gpr),
             (we_any.at[:, pl.ds(pl.multiple_of(t * near_hidden, 256), near_hidden)], we))
        )
    ]
    for i, src in enumerate((ct_any, ctr_any)):
        later.append(load(src, ct.at[i], sems.at[12 + i]))
    stores = [
        load(src, dst, out_sems.at[i])
        for i, (src, dst) in enumerate(
            ((images, images_any), (texts, texts_any), (gall, gall_any), (extra, extra_any))
        )
    ]
    pick = (lax.broadcasted_iota(jnp.int32, (8, LANES), 1) == EXTRA + 3).astype(F32)
    step = min(256, total)

    def flags(j, carry):
        cols = pl.ds(pl.multiple_of(j * step, step), step)
        col_flag[:, cols] = dot_nt(pick, extra[cols, :])
        return carry

    lax.fori_loop(0, total // step, flags, 0)
    scale = jnp.exp(jnp.full((1, 1), expo[0], F32))
    chunk = 48
    blocks = total // rows_block
    per_block = rows_block // chunk
    live = col_flag[0:1, :]

    def similarities(b):
        base = pl.multiple_of(b * rows_block, 16)

        def cols_step(j, carry):
            cols = pl.ds(pl.multiple_of(j * step, step), step)
            sims[:, cols] = scale * dot_nt(texts[pl.ds(base, rows_block), :], images[cols, :])
            return carry

        lax.fori_loop(0, total // step, cols_step, 0)

    def chunk_at(b, i):
        local = pl.ds(pl.multiple_of(i * chunk, 16), chunk)
        whole = pl.ds(pl.multiple_of(b * rows_block + i * chunk, 16), chunk)
        return local, whole

    def column_block(b, acc):
        similarities(b)

        def adding(i, acc):
            local, whole = chunk_at(b, i)
            live_row = extra[whole, EXTRA + 3 : EXTRA + 4]
            part = jnp.exp(sims[local, :]) * live_row
            return acc + jnp.sum(part.reshape(chunk // 8, 8, total), axis=0)

        return lax.fori_loop(0, per_block, adding, acc, unroll=2)

    col_acc = jnp.zeros((8, total), F32)
    if blocks == 1:
        col_acc = column_block(0, col_acc)
    else:
        col_acc = lax.fori_loop(0, blocks, column_block, col_acc)
    col_sum = jnp.sum(col_acc, axis=0, keepdims=True)
    col_part = 0.5 * live / col_sum

    def row_block(b, carry):
        if blocks > 1:
            similarities(b)

        def rows_step(i, acc):
            loss, temp, diag = acc
            local, whole = chunk_at(b, i)
            s = sims[local, :]
            flag = extra[whole, EXTRA + 3 : EXTRA + 4]
            at = lax.broadcasted_iota(jnp.int32, (chunk, total), 0) + (b * rows_block + i * chunk)
            eye = at == lax.broadcasted_iota(jnp.int32, (chunk, total), 1)
            expd = jnp.exp(s)
            rsum = jnp.sum(expd * live, axis=1, keepdims=True)
            g = expd * ((0.5 * flag / rsum) * live + flag * col_part)
            g = g - jnp.where(eye, 0.5 * (flag + live), 0.0)
            grad[local, :] = g.astype(BF16)
            temp = temp + jnp.sum((g * s).reshape(chunk // 8, 8, total), axis=0)
            diag = diag + jnp.sum(
                jnp.where(eye, s * flag, 0.0).reshape(chunk // 8, 8, total), axis=0
            )
            return loss + 0.5 * flag * jnp.log(rsum), temp, diag

        carry = lax.fori_loop(0, per_block, rows_step, carry, unroll=2)
        mine = d * (2 * caps) - b * rows_block

        @pl.when((mine >= 0) & (mine < rows_block))
        def _():
            chip_g[...] = grad[pl.ds(pl.multiple_of(mine, 16), 2 * caps), :]

        if blocks > 1:
            rows = pl.ds(pl.multiple_of(b * rows_block, 16), rows_block)
            load(grad, g_any.at[rows], out_sems.at[4]).wait()
        return carry

    start = (jnp.zeros((chunk, 1), F32), jnp.zeros((8, total), F32), jnp.zeros((8, total), F32))
    if blocks == 1:
        loss, temp, diag = row_block(0, start)
        stores.append(load(grad, g_any, out_sems.at[4]))
    else:
        loss, temp, diag = lax.fori_loop(0, blocks, row_block, start)
    def whole(x):
        return jnp.sum(jnp.sum(x, axis=0, keepdims=True), axis=1, keepdims=True)

    objective = whole(loss) + 0.5 * whole(live * jnp.log(col_sum)) - whole(diag)
    loss_out[...] = objective / whole(live)
    temp_out[...] = whole(temp)

    both_dt = scale * dot(chip_g[...], images[...])
    chip = pl.ds(pl.multiple_of(d * 2 * caps, 16), 2 * caps)
    inv = jnp.sum(extra[chip, EXTRA : EXTRA + 3], axis=1, keepdims=True)
    dt = jnp.where(first, both_dt[:caps], both_dt[caps:])
    dt_far = jnp.where(first, both_dt[caps:], both_dt[:caps])
    both_tx = texts[chip, :].astype(F32)
    tx_far = jnp.where(first, both_tx[caps:], both_tx[:caps])
    inv_far = jnp.where(first, inv[caps:], inv[:caps])

    def pooled_back(tx, dt, inv):
        return inv * (dt - tx * jnp.sum(tx * dt, axis=1, keepdims=True)) * (1.0 / length)

    dy = pooled_back(emb[...], dt, r[:, 0:1])
    dy_out[...] = dy
    dyb = jnp.concatenate([dy, pooled_back(tx_far, dt_far, inv_far)], axis=0).astype(BF16)
    for c in later:
        c.wait()
    dc[...] = jnp.zeros_like(dc)

    def near(j, carry):
        cols = pl.ds(pl.multiple_of(j * 256, 256), 256)
        dg = dot_nt(dyb, wr[cols, :])
        df = (gpk[:, cols].astype(F32).reshape(caps, length, 256) * dg[:caps][:, None, :]).reshape(
            n, 256
        )
        far = (gpr[:, cols].astype(F32).reshape(caps, length, 256) * dg[caps:][:, None, :]).reshape(
            n, 256
        )
        df, far = df.astype(BF16), far.astype(BF16)
        hid_out[0:1, cols] = jnp.sum(df.astype(F32) + far.astype(F32), axis=0, keepdims=True)
        dc[...] += dot_nt(df, we[:, cols])
        side = near_hidden // 512
        local = pl.ds(pl.multiple_of((j % side) * 256, 256), 256)
        exp_s[j // side, :, local] = (
            dot(ct[0].reshape(width, n), df) + dot(ct[1].reshape(width, n), far)
        ).astype(BF16)
        return carry

    lax.fori_loop(0, half, near, 0, unroll=2)
    quarter = width // 4
    for i, out in enumerate((ea, eb, ec, ed)):
        for j, q in enumerate(QUARTERS[i]):
            stores.append(
                load(
                    exp_s.at[i % 2, pl.ds(q * quarter, quarter)],
                    out.at[pl.ds(j * quarter, quarter)],
                    out_sems.at[5 + 2 * i + j],
                )
            )
    stores.append(load(dc, dc_any, out_sems.at[13]))
    for c in stores:
        c.wait()


def middle_back_kernel(
    scal, dc_any, dy, gps_any, m_any, gains, we_any, wr_any, wp_any, qkv_any,
    dm_any, dqkv_any, vec_out,
    dc, gps, mv, we, wr, wp, qkv, dm, dmb, dov, dqkv, sems,
):
    n, width = dm.shape
    caps = dy.shape[0]
    length = n // caps
    far_hidden = gps.shape[1]
    t = scal[0]
    away = pl.ds(pl.multiple_of((1 - t) * far_hidden, 256), far_hidden)
    half = far_hidden // 512
    parts = []
    for i in range(2):
        at = pl.ds(pl.multiple_of(((1 - t) * 2 + i) * half * 256, 256), half * 256)
        here = pl.ds(i * half * 256, half * 256)
        parts.append([
            load(wr_any.at[at], wr.at[here], sems.at[3 * i]),
            load(gps_any.at[:, here], gps.at[:, here], sems.at[3 * i + 1]),
            load(we_any.at[:, at], we.at[:, here], sems.at[3 * i + 2]),
        ])
        if i == 0:
            load_dc = load(dc_any, dc, sems.at[9])
    for c in parts[0]:
        c.wait()
    load_dc.wait()
    load_m = load(m_any, mv, sems.at[10])
    load_p = load(wp_any, wp, sems.at[11])
    load_qkv = load(qkv_any, qkv, sems.at[6])
    dyv = dy[...]
    dyb = dyv.astype(BF16)

    def feed(j, carry):
        cols = pl.ds(pl.multiple_of(j * 256, 256), 256)
        dg = dot_nt(dyb, wr[cols, :])
        df = gps[:, cols].astype(F32).reshape(caps, length, 256) * dg[:, None, :]
        dc[...] += dot_nt(df.reshape(n, 256).astype(BF16), we[:, cols])
        return carry

    lax.fori_loop(0, half, feed, 0, unroll=3)
    for c in parts[1]:
        c.wait()
    lax.fori_loop(half, 2 * half, feed, 0, unroll=3)
    load_m.wait()
    piece = 8 * length

    def norm(i, sums):
        rows = pl.ds(pl.multiple_of(i * piece, piece), piece)
        xhat, rstd = norm_stats(mv[rows, :])
        dcv = dc[rows, :]
        back = norm_back(dcv * row(gains, 1), xhat, rstd)
        dy_rows = dy[pl.ds(pl.multiple_of(i * 8, 8), 8), :]
        out = (back.reshape(piece // length, length, width) + dy_rows[:, None, :]).reshape(
            piece, width
        )
        dm[rows, :] = out
        low = out.astype(BF16)
        dmb[rows, :] = low

        def fold(x):
            return jnp.sum(x.reshape(piece // 8, 8, width), axis=0)

        return sums[0] + fold(dcv * xhat), sums[1] + fold(dcv), sums[2] + fold(low.astype(F32))

    blank = jnp.zeros((8, width), F32)
    sums = lax.fori_loop(0, n // piece, norm, (blank, blank, blank))
    store_dm = load(dm, dm_any, sems.at[7])
    load_p.wait()
    dov[...] = dot_nt(dmb[...], wp[...]).astype(BF16)
    load_qkv.wait()
    masks = head_masks()
    same = (
        lax.broadcasted_iota(jnp.int32, (LANES, LANES), 0) // length
        == lax.broadcasted_iota(jnp.int32, (LANES, LANES), 1) // length
    )
    bias = jnp.where(same, 0.0, -1e30)

    def attention(g, carry):
        rows = pl.ds(pl.multiple_of(g * LANES, LANES), LANES)
        for p in range(width // LANES):
            lanes = slice(p * LANES, (p + 1) * LANES)
            k_lanes = slice(width + p * LANES, width + (p + 1) * LANES)
            v_lanes = slice(2 * width + p * LANES, 2 * width + (p + 1) * LANES)
            q2 = qkv[rows, lanes] * BF16(0.125)
            km = two_heads(qkv[rows, k_lanes], masks)
            vm = two_heads(qkv[rows, v_lanes], masks)
            do2 = dov[rows, lanes]
            parts = softmax_parts(dot_nt(q2, km), bias)
            dp = dot_nt(do2, vm)
            pb, ds = [], []
            for e in range(2):
                prob = parts[e] * (1.0 / jnp.sum(parts[e], axis=-1, keepdims=True))
                dpe = dp[:, e * LANES : (e + 1) * LANES]
                inner = jnp.sum(prob * dpe, axis=-1, keepdims=True)
                pb.append(prob.astype(BF16))
                ds.append((prob * (dpe - inner)).astype(BF16))
            dqkv[rows, lanes] = (dot(jnp.concatenate(ds, axis=1), km) * 0.125).astype(BF16)
            dqkv[rows, k_lanes] = dot_tn(jnp.concatenate(ds, axis=0), two_heads(q2, masks)).astype(
                BF16
            )
            dqkv[rows, v_lanes] = dot_tn(
                jnp.concatenate(pb, axis=0), two_heads(do2, masks)
            ).astype(BF16)
        return carry

    lax.fori_loop(0, n // LANES, attention, 0)
    store = load(dqkv, dqkv_any, sems.at[8])
    for i in range(3):
        vec_out[i : i + 1, :] = jnp.sum(sums[i], axis=0, keepdims=True)
    vec_out[3:4, :] = jnp.sum(dqkv[:, :width].astype(F32), axis=0, keepdims=True)
    vec_out[4:5, :] = jnp.sum(dqkv[:, 2 * width :].astype(F32), axis=0, keepdims=True)
    vec_out[5:8, :] = jnp.zeros((3, width), F32)
    store_dm.wait()
    store.wait()


def weight_grad_kernel(with_hid, scal, dm_any, dqkv_any, at_any, ot_any, wq_any, gains, biases, vec,
                       hid, *rest):
    turn, rest = (rest[:4], rest[4:]) if with_hid else ((), rest)
    keep_a, keep_b, send_a, send_b = rest[:4]
    turned, rest = (rest[4:8], rest[8:]) if with_hid else ((), rest[4:])
    dm, at, ot, dmb, dqkv, wq, grads, tails, inner_v, small, sems, store_sems = rest[:12]
    held, turn_sems = rest[12:16], rest[16:]
    n, width = dm.shape
    t = scal[0]
    load_dm = load(dm_any, dm, sems.at[0])
    load_o = load(ot_any, ot, sems.at[1])
    load_qkv = load(dqkv_any, dqkv, sems.at[2])
    load_a = load(at_any, at, sems.at[3])
    blocks, block = at.shape[:2]
    loads_t = [load(src, dst, turn_sems[0].at[i]) for i, (src, dst) in enumerate(zip(turn, held))]
    load_dm.wait()
    dmb[...] = dm[...].astype(BF16)
    load_o.wait()
    loads_w = [
        load(wq_any.at[pl.ds(e * block, block)], wq.at[scal[4 + e]], sems.at[8 + e])
        for e in range(blocks)
    ]
    half, quarter = width // 2, width // 4

    def project(hh, carry):
        cols = pl.ds(pl.multiple_of(hh * half, LANES), half)
        grads[hh, 0] = dot(ot[...].reshape(width, n), dmb[:, cols]).astype(BF16)
        return carry

    lax.fori_loop(0, 2, project, 0)
    for c in loads_t:
        c.wait()
    for side in range(len(turned) // 2):
        total = held[2 * side][...].astype(F32) + held[2 * side + 1][...].astype(F32)
        turned[side][...] = total[:quarter]
        turned[2 + side][...] = total[quarter:].astype(BF16)
    load_qkv.wait()
    load_a.wait()
    for c in loads_w:
        c.wait()
    inner_v[...] = jnp.zeros_like(inner_v)

    def attend_in(c, carry):
        cols = pl.ds(pl.multiple_of(c * half, LANES), half)
        value = dot(at[...].reshape(width, n), dqkv[:, cols])
        grads[c // 3, 1 + c % 3] = value.astype(BF16)
        prod = value * wq[:, :, cols].reshape(width, half).astype(F32)
        acc = inner_v[...]
        for k in range(half // LANES):
            acc = acc + prod[:, k * LANES : (k + 1) * LANES]
        inner_v[...] = acc
        return carry

    lax.fori_loop(0, 6, attend_in, 0)

    def move(src, out, side, lanes, slot):
        return [
            load(
                src.at[pl.ds(q * quarter, quarter)],
                out.at[i, pl.ds(j * quarter, quarter), pl.ds(lanes, src.shape[1])],
                store_sems.at[slot + 2 * i + j],
            )
            for i in range(2)
            for j, q in enumerate(QUARTERS[side + 2 * i])
        ]

    stores = []
    for k, (hh, out_a, out_b) in enumerate(((1 - t, send_a, send_b), (t, keep_a, keep_b))):
        for part in range(4):
            out = (out_a, out_b)[part // 2]
            stores += move(grads.at[hh, part], out, part // 2, (part % 2) * half, 20 * k + 4 * part)
    inner = inner_v[...]
    inner = jnp.sum(inner, axis=1, keepdims=True)
    sums = jnp.sum(dqkv[...].astype(F32), axis=0, keepdims=True)
    hi = sums.astype(BF16)
    lo = (sums - hi.astype(F32)).astype(BF16)
    both = jnp.concatenate([hi, lo, jnp.zeros((14, 3 * width), BF16)], axis=0)
    shift1 = dot_nt(wq[...].reshape(width, 3 * width), both)
    shift1 = shift1[:, 0:1] + shift1[:, 1:2]
    first = (jnp.zeros((1, 1), jnp.int32) + t) == 0
    zero = jnp.zeros((1, width), F32)
    for_zero = jnp.concatenate([zero, zero, vec[1:2, :], vec[3:4, :], zero, zero], axis=0)
    for_one = jnp.concatenate([vec[0:1, :], vec[4:5, :], vec[2:3, :], zero, zero, zero], axis=0)
    ends = jnp.concatenate([1.0 / row(gains, 0), row(biases, 0)], axis=0)
    lines = jnp.concatenate([for_zero, ends, for_one, ends], axis=0).T
    lane = lax.broadcasted_iota(jnp.int32, (1, 8), 1)
    if with_hid:
        columns = jnp.broadcast_to(hid[...], (8, hid.shape[1])).T
    for e in range(blocks):
        at_block = slice(e * block, (e + 1) * block)
        if with_hid:
            pick = columns[2 * e * block : (2 * e + 1) * block] * (lane == 4).astype(F32)
            pick = pick + columns[(2 * e + 1) * block : (2 * e + 2) * block] * (lane == 5).astype(F32)
        else:
            pick = jnp.zeros((block, 8), F32)
        small[scal[4 + e]] = jnp.concatenate(
            [lines[at_block, :8], lines[at_block, 8:], pick,
             jnp.zeros((block, LANES - 24), F32)], axis=1
        )
    sv = small[...].reshape(width, LANES)
    zeros_set, ones_set, own = sv[:, :8], sv[:, 8:16], sv[:, 16:24]
    gain1 = zeros_set[:, 6:7] * (inner - zeros_set[:, 7:8] * shift1)
    zeros_set = zeros_set + gain1 * (lane == 0).astype(F32) + shift1 * (lane == 1).astype(F32)
    used = (lane < 4).astype(F32)
    zeros_set, ones_set = zeros_set * used, ones_set * used
    keep_set = jnp.where(first, zeros_set, ones_set) + own
    send_set = jnp.where(first, ones_set, zeros_set)
    for hh in range(2):
        value = jnp.where((jnp.zeros((1, 1), jnp.int32) + t) == hh, keep_set, send_set)
        hi = value.astype(BF16).astype(F32)
        fill = jnp.zeros((width, LANES // 2 - 8), F32)
        tails[hh] = jnp.concatenate([hi, fill, value - hi, fill], axis=1).astype(BF16)
    stores += move(tails.at[1 - t], send_b, 1, width, 16)
    stores += move(tails.at[t], keep_b, 1, width, 36)
    for c in stores:
        c.wait()


def input_back_kernel(
    scal, dm_any, h_any, gains, dqkv_any, wq_any, order_any,
    tok_keep, tok_send,
    h_v, wq, dm, dqkv, da, sems,
):
    n, width = dm.shape
    caps, half_len, _ = tok_keep.shape
    t = scal[0]
    loads = [
        load(src, dst, sems.at[i])
        for i, (src, dst) in enumerate(
            ((dqkv_any, dqkv), (wq_any, wq),
             (h_any.at[pl.ds(pl.multiple_of(t * n, n), n)], h_v), (dm_any, dm))
        )
    ]
    loads[0].wait()
    loads[1].wait()

    def back(j, carry):
        rows = pl.ds(pl.multiple_of(j * 256, 256), 256)
        da[:, rows] = dot_nt(dqkv[...], wq[rows, :])
        return carry

    lax.fori_loop(0, width // 256, back, 0, unroll=3)
    loads[2].wait()
    loads[3].wait()
    piece = 8 * 2 * half_len
    first = (jnp.zeros((1, 1, 1), jnp.int32) + t) == 0

    def norm(i, carry):
        rows = pl.ds(pl.multiple_of(i * piece, piece), piece)
        xhat, rstd = norm_stats(h_v[rows, :].astype(F32))
        grad = dm[rows, :] + norm_back(da[rows, :] * row(gains, 0), xhat, rstd)
        halves = grad.reshape(8, 2, half_len, width)
        at = pl.ds(pl.multiple_of(i * 8, 8), 8)
        tok_keep[at] = jnp.where(first, halves[:, 0], halves[:, 1])
        tok_send[at] = jnp.where(first, halves[:, 1], halves[:, 0]).astype(BF16)
        return carry

    lax.fori_loop(0, n // piece, norm, 0)


def reduce_grad_kernel(
    rows_block, length, expo, g_any, images_any, texts_any, gall_any, extra_any, order_any,
    red_out, bias_out,
    g_v, images, texts, gall, extra, acc, sems,
):
    total, width = images.shape
    blocks = total // rows_block
    share = red_out.shape[0]
    whole = load(images_any, images, sems.at[0])
    scale = jnp.exp(jnp.full((1, 1), expo[0], F32))
    acc[...] = jnp.zeros_like(acc)
    whole.wait()

    def block(b, rb):
        rows = pl.ds(pl.multiple_of(b * rows_block, 16), rows_block)
        waits = [
            load(src.at[rows], dst, sems.at[1 + i])
            for i, (src, dst) in enumerate(
                ((g_any, g_v), (texts_any, texts), (gall_any, gall), (extra_any, extra))
            )
        ]
        for c in waits:
            c.wait()
        def project(i, rb):
            at = pl.ds(pl.multiple_of(i * 96, 96), 96)
            dt = scale * dot(g_v[at, :], images[...])
            tx = texts[at, :].astype(F32)
            part = (dt - tx * jnp.sum(tx * dt, axis=1, keepdims=True)) * (1.0 / length)
            part = part.astype(BF16)
            texts[at, :] = part
            inv = jnp.sum(extra[at, EXTRA : EXTRA + 3], axis=1, keepdims=True)
            return rb + jnp.sum(part.astype(F32) * inv, axis=0, keepdims=True)

        rb = lax.fori_loop(0, rows_block // 96, project, rb)
        acc[...] += dot_tn(gall[...], texts[...])
        return rb

    rb = lax.fori_loop(0, blocks, block, jnp.zeros((1, width), F32))
    red_out[...] = acc[:share, :]
    bias_out[...] = jnp.broadcast_to(rb * float(length), bias_out.shape)


def to_wire(x, width):
    low = x.astype(BF16)
    if x.shape[1] == width:
        return low
    rest = x[:, width:] - low[:, width:].astype(F32)
    return jnp.concatenate([low, rest.astype(BF16)], axis=1)


def from_wire(x, width):
    y = x.astype(F32)
    if x.shape[1] == width:
        return y
    return jnp.concatenate([y[:, :width], y[:, width : width + 64] + y[:, width + 64 :]], axis=1)


def wire_kernel(width, qa, qa_back, qb, qb_back, far_a, far_b, wire_a, wire_b, a0, a1, b0, b1,
                sems):
    loads = [
        load(src.at[0], dst, sems.at[i])
        for i, (src, dst) in enumerate(((qa, a0), (qa_back, a1), (qb, b0), (qb_back, b1)))
    ]
    loads[0].wait()
    loads[1].wait()
    wire_a[...] = (a0[...].astype(F32) + a1[...].astype(F32)).astype(BF16)
    loads[2].wait()
    loads[3].wait()
    wire_b[...] = to_wire(from_wire(b0[...], width) + from_wire(b1[...], width), width)


def turn_kernel(width, stacked, count, *refs):
    ins, (kept_a, kept_b, next_a, next_b) = refs[: 2 * count], refs[2 * count : 2 * count + 4]
    scratch, sems = refs[2 * count + 4 : -1], refs[-1]
    loads = [
        load(src.at[1] if i % count < stacked else src, dst, sems.at[i])
        for i, (src, dst) in enumerate(zip(ins, scratch))
    ]
    half = kept_a.shape[0]
    for side, (kept, moved) in enumerate(((kept_a, next_a), (kept_b, next_b))):
        at = range(side * count, (side + 1) * count)
        for i in at:
            loads[i].wait()
        total = from_wire(scratch[at[0]][...], width)
        for i in at[1:]:
            total = total + from_wire(scratch[i][...], width)
        kept[...] = total[:half]
        moved[...] = to_wire(total[half:], width)


def merge_kernel(width, sum_a, sum_b, hop_a, hop_b, *rest):
    outs = rest[-4:]
    for i, out in enumerate(outs):
        rows = out.shape[0]
        at = slice(i * rows, (i + 1) * rows)
        a = sum_a[at, :] + hop_a[at, :].astype(F32)
        b = sum_b[at, :] + from_wire(hop_b[at, :], width)
        if i == 0:
            out[:, :width] = a
            out[:, width:] = b
        else:
            out[:, :width] = a.astype(BF16)
            out[:, width:] = to_wire(b, width)


def finish_kernel(width, scal, total, hop_1, hop_2, hop_3, rbias,
                  qkv_out, project_out, gains_out, biases_out, hid_out):
    half = width // 2
    rows, cols = project_out.shape[0], width
    t, d = scal[0], scal[1]
    acc = total[...]
    for hop in (hop_1, hop_2, hop_3):
        x = hop[...]
        acc = acc + jnp.concatenate(
            [x[:, :width].astype(F32), from_wire(x[:, width:], width)], axis=1
        )
    project_out[...] = acc[:, :half]
    qkv_out[...] = acc[:, half : 2 * width]
    small = acc[:, 2 * width : 2 * width + 8].T
    lane = lax.broadcasted_iota(jnp.int32, (rows, cols), 1)
    mine = lax.broadcasted_iota(jnp.int32, (rows, cols), 0) + d * rows
    last = jnp.sum(jnp.where(lane == mine, rbias[0:1, :], 0.0), axis=1, keepdims=True)
    last = jnp.broadcast_to(last, (rows, 8)).T
    first = (jnp.zeros((1, 1), jnp.int32) + t) == 0
    gains_out[...] = small[0:1]
    biases_out[...] = jnp.concatenate(
        [small[1:3], jnp.where(first, small[3:4], last[0:1])], axis=0
    )
    hid_out[...] = jnp.concatenate([small[4:5], small[5:6]], axis=1)


def xor_permute(x, axis, bit):
    return lax.ppermute(x, axis, [(i, i ^ bit) for i in range(lax.axis_size(axis))])


def bit_groups(count):
    bits = [1 << i for i in range(count.bit_length() - 1)]
    groups = [tuple(bits[i : i + 2]) for i in range(0, len(bits), 2)]
    return groups[::-1]


def reaches(group):
    out = [0]
    for bit in group:
        out = out + [r ^ bit for r in out]
    return out


def slot_reaches(count):
    order = [0]
    for group in bit_groups(count):
        order = [r ^ o for r in reaches(group) for o in order]
    return order


def hop(sends, group):
    return [x if r == 0 else xor_permute(x, "dp", r) for x, r in zip(sends, reaches(group))]


def scatter_sum(s, groups, to_wire=lambda x: x, from_wire=lambda x: x):
    for group in reversed(groups):
        hops = reaches(group)
        rows = s.shape[0] // len(hops)
        parts = [s[i * rows : (i + 1) * rows] for i in range(len(hops))]
        moved = [xor_permute(to_wire(parts[i]), "dp", r) for i, r in enumerate(hops) if r]
        s = parts[0]
        for piece in moved:
            s = s + from_wire(piece)
    return s


def flip_by(x, index, count):
    for i in range(count.bit_length() - 1):
        bit = 1 << i
        shape = x.shape
        pairs = x.reshape((count // (2 * bit), 2, bit) + shape[1:])
        x = jnp.where((index & bit) != 0, pairs[:, ::-1], pairs).reshape(shape)
    return x


SMEM = pl.BlockSpec(memory_space=pltpu.SMEM)
VMEM = pl.BlockSpec(memory_space=pltpu.VMEM)
ANY = pl.BlockSpec(memory_space=pl.ANY)


def padded_bytes(shape, dtype):
    size = jnp.dtype(dtype).itemsize
    shape = (1,) * (2 - len(shape)) + tuple(shape)
    rows = -(-shape[-2] // 16) * 16
    return math.prod(shape[:-2]) * rows * (-(-shape[-1] // LANES) * LANES) * size


def call(kernel, name, in_specs, outs, out_specs, scratch, args, flops, moved):
    held = [(x.shape, x.dtype) for x in scratch if jnp.issubdtype(x.dtype, jnp.floating)]
    held += [(a.shape, a.dtype) for a, spec in zip(args, in_specs) if spec is VMEM]
    held += [o for o, spec in zip(outs, out_specs) if spec is VMEM]
    limit = VMEM_LIMIT
    if name in SMALL:
        limit = min(limit, sum(padded_bytes(*x) for x in held) + MARGIN)
    return pl.pallas_call(
        kernel,
        name=name,
        in_specs=in_specs,
        out_shape=[jax.ShapeDtypeStruct(s, d) for s, d in outs],
        out_specs=out_specs,
        scratch_shapes=scratch,
        compiler_params=pltpu.CompilerParams(vmem_limit_bytes=limit),
        cost_estimate=pl.CostEstimate(flops=flops, bytes_accessed=moved, transcendentals=0),
    )(*args)


def body(
    pictures, captions, tallies, exponent,
    p_gains, p_biases, p_hid, p_wq, p_wp, p_we, p_wr,
    c_gains, c_biases, c_hid, c_wq, c_wp, c_we, c_wr,
):
    t = lax.axis_index("tower")
    d = lax.axis_index("dp")
    chips = lax.axis_size("dp")
    pairs, length, width = captions.shape
    img_len = pictures.shape[1]
    hidden = c_hid.shape[0]
    caps = pairs // 2
    n = caps * length
    total = pairs * chips
    row_blocks = 16
    order = np.array(slot_reaches(chips))
    slot_of = np.zeros(chips, np.int32)
    slot_of[order] = np.arange(chips)
    table = np.stack([slot_of[np.arange(chips) ^ i] for i in range(chips)]).astype(np.int32)
    slots = lax.dynamic_slice_in_dim(jnp.asarray(table), d, 1, 0)[0]
    relative = chips == row_blocks
    row_slots = slots if relative else jnp.arange(row_blocks, dtype=jnp.int32)
    head = jnp.stack([t, d, tallies[0], t]).astype(jnp.int32)
    scal = jnp.concatenate([head, row_slots, slots])

    texts_in = captions.reshape(pairs * length, width)
    c_hid2, p_hid2 = c_hid.reshape(hidden // LANES, LANES), p_hid.reshape(hidden // LANES, LANES)
    blk = (row_blocks, width // row_blocks, n)
    vm = pltpu.VMEM
    sem = pltpu.SemaphoreType.DMA
    half_hid = (n, hidden // 2)
    chunk = width + 2 * LANES
    a_t, qkv, o_t, m, c_t, gp_keep, gp_send, text_send, emb, r = call(
        text_forward_kernel, "text_forward",
        [SMEM, ANY, VMEM, VMEM, VMEM, ANY, ANY, ANY, ANY],
        [(blk, BF16), ((n, 3 * width), BF16), (blk, BF16), ((n, width), F32), (blk, BF16),
         (half_hid, BF16), (half_hid, BF16), ((chips, caps, chunk), BF16),
         ((caps, width), F32), ((caps, LANES), F32)],
        [ANY] * 7 + [VMEM] * 3,
        [vm((n, width), BF16), vm((width, 3 * width), BF16), vm((width, width), BF16),
         vm((width, hidden), BF16), vm((hidden, width), BF16), vm((1, 3 * width), F32),
         vm((1, hidden), F32),
         vm((n, width), BF16), vm((n, width), BF16), vm((caps, hidden), F32), vm(blk, BF16), vm((n, 3 * width), BF16),
         vm(blk, BF16), vm((n, width), F32), vm(blk, BF16), vm(half_hid, BF16),
         vm(half_hid, BF16), sem((5,)), sem((7,))],
        (scal, texts_in, c_gains, c_biases, c_hid2, c_wq, c_wp, c_we, c_wr),
        int(2 * n * width * (4 * width + hidden)), 20_000_000,
    )
    c_far = xor_permute(c_t, "tower", 1)
    gp_far = xor_permute(gp_send, "tower", 1)
    text_all = lax.all_to_all(text_send, "dp", 0, 0, tiled=True)

    rows = caps * PAD
    groups = bit_groups(chips)
    (image,) = call(
        image_forward_kernel, "image_forward",
        [SMEM, ANY, VMEM, VMEM, VMEM, ANY, ANY, ANY, ANY],
        [((caps, width), BF16)],
        [VMEM],
        [vm((img_len, pairs, width), BF16), vm((width // LANES, img_len * caps, LANES), F32),
         vm((rows, width), F32), vm((rows, width), BF16),
         vm((rows + 16, 3 * width), BF16), vm((rows, width), F32), vm((caps, width), F32),
         vm((caps, hidden), F32), vm((width, 3 * width), BF16), vm((width, width), BF16),
         vm((width, hidden), BF16), vm((hidden, width), BF16), vm((1, 3 * width), F32),
         vm((1, hidden), F32),
         vm((1, width), F32), sem((5,))],
        (scal, jnp.transpose(pictures, (1, 0, 2)), p_gains, p_biases, p_hid2,
         p_wq, p_wp, p_we, p_wr),
        int(2 * rows * width * (4 * width + hidden)), 20_000_000,
    )
    image, text_all = lax.optimization_barrier((image, text_all))
    text_par = xor_permute(text_all, "tower", 1)
    got = hop([image[None]] * len(reaches(groups[0])), groups[0])
    for group in groups[1:]:
        whole = jnp.concatenate(got, axis=0)
        got = hop([whole] * len(reaches(group)), group)
    par_all = xor_permute(jnp.concatenate(got, axis=0), "tower", 1)
    small_slice = total <= 768
    if not small_slice:
        got = [jnp.concatenate(got, axis=0)]

    block = total if small_slice else 96
    held = chips if small_slice else 1
    share = hidden // (2 * chips)
    piece_shape = (width // 2, width)
    (loss, temp, ea, eb, ec, ed, g_all, images_all, texts_all, gall, extra, dc, dy, hid_grad) = call(
        partial(loss_kernel, block, len(got)), "loss",
        [SMEM] + [ANY] * len(got) + [ANY, ANY, ANY, SMEM, VMEM, VMEM] + [ANY] * 6,
        [((1, 1), F32), ((1, 1), F32)] + [(piece_shape, BF16)] * 4
        + [((total, total), BF16), ((total, width), BF16), ((total, width), BF16),
           ((total, LANES), BF16), ((total, LANES), F32), ((n, width), F32), ((caps, width), F32),
           ((1, hidden // 2), F32)],
        [VMEM, VMEM] + [ANY] * 10 + [VMEM, VMEM],
        [vm((held, caps, width), BF16), vm((held, caps, width), BF16),
         vm((held, caps, chunk), BF16), vm((held, caps, chunk), BF16),
         vm((total, width), BF16), vm((total, width), BF16), vm((total, LANES), F32),
         vm((total, LANES), BF16), vm((8, total), F32),
         vm((block, total), F32), vm((block, total), BF16), vm((2 * caps, total), BF16),
         vm(half_hid, BF16), vm(half_hid, BF16), vm((2,) + blk, BF16),
         vm((width, hidden // 2), BF16), vm((hidden // 2, width), BF16),
         vm((n, width), F32), vm((2, width, hidden // 4), BF16), sem((16,)), sem((14,))],
        (scal, *got, par_all, text_all, text_par, exponent, emb, r, gp_keep, gp_far,
         c_t, c_far, c_we, c_wr),
        int(3 * n * width * hidden), 20_000_000,
    )

    def widen(x):
        return x.astype(F32)

    def narrow(x):
        return x.astype(BF16)

    e_hops = [xor_permute(ea, "dp", 1), xor_permute(eb, "dp", 2)] if relative else []
    dm, dqkv, vec = call(
        middle_back_kernel, "middle_back",
        [SMEM, ANY, VMEM, ANY, ANY, VMEM] + [ANY] * 4,
        [((n, width), F32), ((n, 3 * width), BF16), ((8, width), F32)],
        [ANY, ANY, VMEM],
        [vm((n, width), F32), vm(half_hid, BF16), vm((n, width), F32),
         vm((width, hidden // 2), BF16), vm((hidden // 2, width), BF16), vm((width, width), BF16),
         vm((n, 3 * width), BF16), vm((n, width), F32), vm((n, width), BF16),
         vm((n, width), BF16), vm((n, 3 * width), BF16), sem((12,))],
        (scal, dc, dy, gp_send, m, c_gains, c_we, c_wr, c_wp, qkv),
        int(2 * n * width * (hidden + 4 * width)), 20_000_000,
    )
    b_shape = (width // 2, width + LANES)
    quarter_shape = (width // 4, width)
    qa_keep, qb_keep, qa_send, qb_send, *turned = call(
        partial(weight_grad_kernel, relative), "weight_grad",
        [SMEM] + [ANY] * 5 + [VMEM] * 4 + [ANY] * (4 if relative else 0),
        [((2,) + piece_shape, BF16), ((2,) + b_shape, BF16)] * 2
        + ([(quarter_shape, F32)] * 2 + [(quarter_shape, BF16)] * 2 if relative else []),
        [ANY] * 4 + [VMEM] * (4 if relative else 0),
        [vm((n, width), F32), vm(blk, BF16), vm(blk, BF16), vm((n, width), BF16),
         vm((n, 3 * width), BF16), vm((row_blocks, width // row_blocks, 3 * width), BF16),
         vm((2, 4, width, width // 2), BF16), vm((2, width, LANES), BF16), vm((width, LANES), F32),
         vm((row_blocks, width // row_blocks, LANES), F32), sem((8 + row_blocks,)), sem((40,))]
        + ([vm(piece_shape, BF16)] * 4 + [sem((4,))] if relative else []),
        (scal, dm, dqkv, a_t, o_t, c_wq, c_gains, c_biases, vec, hid_grad)
        + ((ec, e_hops[0], ed, e_hops[1]) if relative else ()),
        int(2 * n * width * 4 * width), 20_000_000,
    )
    qa_back = xor_permute(qa_send, "tower", 1)
    qb_back = xor_permute(qb_send, "tower", 1)
    cols = width // chips
    if relative:
        e_parts = (
            turned[0], turned[1], xor_permute(turned[2], "dp", 2), xor_permute(turned[3], "dp", 1)
        )
        wire_a, wire_b = call(
            partial(wire_kernel, width), "wire", [ANY] * 6,
            [(piece_shape, BF16), (b_shape, BF16)], [VMEM] * 2,
            [vm(piece_shape, BF16)] * 2 + [vm(b_shape, BF16)] * 2 + [sem((4,))],
            (qa_keep, qa_back, qb_keep, qb_back, *e_parts[2:]), 1_000_000, 4_000_000,
        )
        q_hops = [xor_permute(wire_a, "dp", 1), xor_permute(wire_b, "dp", 2)]
    else:
        q_sums = [
            from_wire(x[i], width) + from_wire(y[i], width)
            for i in range(2)
            for x, y in ((qa_keep, qa_back), (qb_keep, qb_back))
        ]
        tails = jnp.transpose(hid_grad.reshape(chips, 2, cols), (0, 2, 1)).reshape(width, 2)
        tails = jnp.pad(tails, ((0, 0), (width + 4, 64 - 6)))
        quarter = width // 4
        for i in (1, 3):
            q_sums[i] = q_sums[i] + jnp.concatenate(
                [tails[q * quarter : (q + 1) * quarter] for q in QUARTERS[i]], axis=0
            )
        wire_b = qb_back
        q_hops = []
    tok_keep, tok_send = call(
        input_back_kernel, "input_back",
        [SMEM, ANY, ANY, VMEM, ANY, ANY, ANY],
        [((caps, length // 2, width), F32), ((caps, length // 2, width), BF16)],
        [VMEM] * 2,
        [vm((n, width), BF16), vm((width, 3 * width), BF16), vm((n, width), F32),
         vm((n, 3 * width), BF16), vm((n, width), F32), sem((4,))],
        (scal, dm, texts_in, c_gains, dqkv, c_wq, wire_b),
        int(2 * n * width * 3 * width), 9_000_000,
    )
    reduce_grad, rbias = call(
        partial(reduce_grad_kernel, block, length), "reduce_grad",
        [SMEM] + [ANY] * 6,
        [((share, width), F32), ((8, width), F32)],
        [VMEM, VMEM],
        [vm((block, total), BF16), vm((total, width), BF16), vm((block, width), BF16),
         vm((block, LANES), BF16), vm((block, LANES), F32), vm((LANES, width), F32), sem((5,))],
        (exponent, g_all, images_all, texts_all, gall, extra, q_hops[0] if relative else wire_b),
        int(2 * total * total * width), 6_000_000,
    )

    tok_back = widen(xor_permute(tok_send, "tower", 1))
    grad_tokens = jnp.concatenate(
        [jnp.where(t == 0, tok_keep, tok_back), jnp.where(t == 0, tok_back, tok_keep)], axis=0
    )
    half, third = width // 2, width // 4

    def plain(sums):
        sides = []
        for side in range(2):
            at = {}
            for i in (side, side + 2):
                for j, q in enumerate(QUARTERS[i]):
                    at[q] = sums[i][j * third : (j + 1) * third]
            x = jnp.concatenate([at[q] for q in range(4)], axis=0)
            x = flip_by(x.reshape((chips, cols) + x.shape[1:]), d, chips)
            x = x[order].reshape((width,) + x.shape[2:])
            sides.append(
                scatter_sum(x, groups, lambda v: to_wire(v, width), lambda v: from_wire(v, width))
            )
        return sides

    if not relative:
        expand_grad = jnp.concatenate(plain([widen(x) for x in (ea, eb, ec, ed)]), axis=1)
        side_a, side_b = plain(q_sums)
        small = side_b[:, width : width + 8].T
        last = jnp.where(
            t == 0, small[3], lax.dynamic_slice_in_dim(rbias[0], d * cols, cols, 0)
        )
        return (
            loss.reshape(1), temp.reshape(1), grad_tokens, small[0:1], jnp.stack([small[1], small[2], last]),
            small[4:6].reshape(2 * cols),
            jnp.concatenate([side_a[:, half:], side_b[:, :width]], axis=1), side_a[:, :half],
            expand_grad, reduce_grad,
        )

    def second_hops(side_a, side_b, stacked, name):
        count = len(side_a)
        shapes = [x.shape[-2:] for x in (*side_a, *side_b)]
        small = shapes[-1][1] - width
        kept_a, kept_b, next_a, next_b = call(
            partial(turn_kernel, width, stacked, count), name, [ANY] * (2 * count),
            [((third, width), F32), ((third, width + small // 2), F32),
             ((third, width), BF16), ((third, width + small), BF16)],
            [VMEM] * 4, [vm(x, BF16) for x in shapes] + [sem((2 * count,))],
            (*side_a, *side_b), 1_000_000, 4_000_000,
        )
        return kept_a, kept_b, xor_permute(next_a, "dp", 2), xor_permute(next_b, "dp", 1)

    def merge(parts, after, name):
        f32_cols = parts[0].shape[1] + parts[1].shape[1]
        bf_cols = parts[2].shape[1] + parts[3].shape[1]
        return call(
            partial(merge_kernel, width), name, [VMEM] * 4 + [ANY] * len(after),
            [((cols, f32_cols), F32)] + [((cols, bf_cols), BF16)] * 3, [VMEM] * 4, [],
            (*parts, *after), 1_000_000, 3_000_000,
        )

    def z_hops(pieces):
        return [xor_permute(x, "dp", r) for x, r in zip(pieces, reaches(groups[0])[1:])]

    e_own, *e_far = merge(e_parts, (wire_b,), "merge_expand")
    e_back = z_hops(e_far)
    expand_grad = e_own + sum(widen(x) for x in e_back)
    q_parts = second_hops(
        (qa_keep, qa_back, q_hops[0]), (qb_keep, qb_back, q_hops[1]), 2, "turn_qkv"
    )
    q_own, *q_far = merge(q_parts, e_back, "merge_qkv")
    q_in = z_hops(q_far)
    qkv_grad, project_grad, gains_grad, biases_grad, hid_rows = call(
        partial(finish_kernel, width), "finish", [SMEM] + [VMEM] * 5,
        [((cols, 3 * half), F32), ((cols, half), F32), ((1, cols), F32), ((3, cols), F32),
         ((1, 2 * cols), F32)],
        [VMEM] * 5, [], (scal, q_own, *q_in, rbias), 1_000_000, 2_000_000,
    )
    return (
        loss.reshape(1), temp.reshape(1), grad_tokens, gains_grad, biases_grad, hid_rows.reshape(2 * cols),
        qkv_grad, project_grad, expand_grad, reduce_grad,
    )


def solution(mesh):
    in_specs = (P("dp", None, None), P("dp", None, None), P("dp")) + (P(),) * 15
    out_specs = (
        P(), P(), P("dp", "tower", None), P("tower", "dp"), P("tower", "dp"),
        P(("tower", "dp")), P("dp", "tower"), P("dp", "tower"), P("dp", "tower"),
        P(("tower", "dp"), None),
    )
    return jax.shard_map(body, mesh=mesh, in_specs=in_specs, out_specs=out_specs, check_vma=False)
```

```python
import math
from functools import partial

import jax
import jax.numpy as jnp
import numpy as np
from jax import lax
from jax.experimental import pallas as pl
from jax.experimental.pallas import tpu as pltpu
from jax.sharding import PartitionSpec as P

F32 = jnp.float32
BF16 = jnp.bfloat16
HEAD_DIM = 64
LANES = 128
EXTRA = 120
norm_eps = 1e-06
embed_eps = 1e-06
NEG = -1000000000.0
VMEM_LIMIT = 60 * 1024 * 1024
MARGIN = 8 * 1024 * 1024
SMALL = ("merge_expand", "merge_qkv", "finish", "reduce_grad")


def normal_cdf(x):
    return 0.5 + 0.5 * lax.erf(x * 0.7071067811865476)


def load(src, dst, sem):
    copy = pltpu.make_async_copy(src, dst, sem)
    copy.start()
    return copy


def dot(a, b):
    return jnp.dot(a, b, preferred_element_type=F32)


def dot_nt(a, b):
    return lax.dot_general(a, b, (((1,), (1,)), ((), ())), preferred_element_type=F32)


def dot_tn(a, b):
    return lax.dot_general(a, b, (((0,), (0,)), ((), ())), preferred_element_type=F32)


def norm_stats(x):
    mean = jnp.mean(x, axis=-1, keepdims=True)
    centered = x - mean
    rstd = lax.rsqrt(jnp.mean(centered * centered, axis=-1, keepdims=True) + norm_eps)
    return centered * rstd, rstd


def norm_back(dxhat, xhat, rstd):
    return rstd * (
        dxhat
        - jnp.mean(dxhat, axis=-1, keepdims=True)
        - xhat * jnp.mean(dxhat * xhat, axis=-1, keepdims=True)
    )


def row(ref, i):
    return ref[i : i + 1, :].astype(F32)


def head_masks():
    lane = lax.broadcasted_iota(jnp.int32, (1, LANES), 1)
    first = (lane < HEAD_DIM).astype(BF16)
    return first, (1 - first).astype(BF16)


def set_qkv_bias(out, biases):
    width = biases.shape[1]
    out[:, :width] = row(biases, 2)
    out[:, width : 2 * width] = jnp.zeros((1, width), F32)
    out[:, 2 * width :] = row(biases, 3)


def set_hidden_bias(out, hid):
    lines = hid[...].astype(F32)
    for i in range(hid.shape[0]):
        out[:, i * LANES : (i + 1) * LANES] = lines[i : i + 1]


def two_heads(x, masks):
    return jnp.concatenate([x * masks[0], x * masks[1]], axis=0)


def softmax_parts(scores, bias):
    keys = scores.shape[1] // 2
    parts = []
    for e in range(2):
        s = scores[:, e * keys : (e + 1) * keys] + bias
        parts.append(jnp.exp(s - jnp.max(s, axis=-1, keepdims=True)))
    return parts


def attend(q2, k2, v2, bias, masks):
    e0, e1 = softmax_parts(dot_nt(q2 * BF16(0.125), two_heads(k2, masks)), bias)
    weights = jnp.concatenate([e0.astype(BF16), e1.astype(BF16)], axis=1)
    ones = jnp.ones((k2.shape[0], LANES), BF16)
    right = jnp.concatenate([two_heads(v2, masks), two_heads(ones, masks)], axis=1)
    out = dot(weights, right)
    return (out[:, :LANES] / out[:, LANES:]).astype(BF16)


def split_dot(x, w):
    hi = x.astype(BF16)
    lo = (x - hi.astype(F32)).astype(BF16)
    n = x.shape[0]
    out = dot(jnp.concatenate([hi, lo], axis=0), w)
    return out[:n] + out[n:]


def text_forward_kernel(
    scal, h_any, gains, biases, hid, wq_any, wp_any, we_any, wr_any,
    a_any, qkv_any, o_any, m_any, c_any, gpk_any, gps_any, send_out, emb_out, r_out,
    h_v, wq, wp, we, wr, qb, hb, av, cv, gsum, a_out, qkv_out, o_out, m_out, c_out, gp_keep, gp_send,
    sems, out_sems,
):
    n, width = m_out.shape
    caps = emb_out.shape[0]
    length = n // caps
    hidden = hid.shape[0] * LANES
    t, d = scal[0], scal[1]
    load_h = load(h_any.at[pl.ds(pl.multiple_of(t * n, n), n)], h_v, sems.at[0])
    load_q = load(wq_any, wq, sems.at[1])
    load_h.wait()
    masks = head_masks()

    def put_transposed(out, src):
        count, rows = out.shape[:2]

        def turn(i, carry):
            lanes = pl.ds(pl.multiple_of(i * (width // 2), LANES), width // 2)
            turned = src[:, lanes].astype(F32).T.astype(BF16)
            for e in range(count // 2):
                out[scal[4 + i * (count // 2) + e]] = turned[e * rows : (e + 1) * rows, :]
            return carry

        lax.fori_loop(0, 2, turn, 0, unroll=2)

    h = h_v[...].astype(F32)
    xhat, _ = norm_stats(h)
    a = xhat * row(gains, 0) + row(biases, 0)
    av[...] = a.astype(BF16)
    load_q.wait()
    load_p = load(wp_any, wp, sems.at[2])
    load_e = load(we_any, we, sems.at[3])
    load_r = load(wr_any, wr, sems.at[4])
    set_qkv_bias(qb, biases)
    set_hidden_bias(hb, hid)

    def to_qkv(j, carry):
        cols = pl.ds(pl.multiple_of(j * 256, 256), 256)
        qkv_out[:, cols] = (dot(av[...], wq[:, cols]) + qb[:, cols]).astype(BF16)
        return carry

    lax.fori_loop(0, 3 * width // 256, to_qkv, 0, unroll=9)
    put_transposed(a_out, av)
    stores = [load(qkv_out, qkv_any, out_sems.at[0]), load(a_out, a_any, out_sems.at[1])]
    same = (
        lax.broadcasted_iota(jnp.int32, (LANES, LANES), 0) // length
        == lax.broadcasted_iota(jnp.int32, (LANES, LANES), 1) // length
    )
    bias = jnp.where(same, 0.0, -1e30)

    def attention(g, carry):
        rows = pl.ds(pl.multiple_of(g * LANES, LANES), LANES)
        for p in range(width // LANES):
            lanes = slice(p * LANES, (p + 1) * LANES)
            q2 = qkv_out[rows, lanes]
            k2 = qkv_out[rows, width + p * LANES : width + (p + 1) * LANES]
            v2 = qkv_out[rows, 2 * width + p * LANES : 2 * width + (p + 1) * LANES]
            av[rows, lanes] = attend(q2, k2, v2, bias, masks)
        return carry

    lax.fori_loop(0, n // LANES, attention, 0)
    load_p.wait()
    m = h_v[...].astype(F32) + dot(av[...], wp[...]) + row(biases, 4)
    m_out[...] = m
    stores.append(load(m_out, m_any, out_sems.at[2]))
    xhat, _ = norm_stats(m)
    c = xhat * row(gains, 1) + row(biases, 1)
    cv[...] = c.astype(BF16)
    put_transposed(c_out, cv)
    put_transposed(o_out, av)
    stores.append(load(c_out, c_any, out_sems.at[3]))
    stores.append(load(o_out, o_any, out_sems.at[4]))
    load_e.wait()
    half = hidden // 512

    def feed(rel, gp_out):
        def step(j, carry):
            local = pl.ds(pl.multiple_of(j * 256, 256), 256)
            at = jnp.bitwise_xor(t, rel) * half + j
            cols = pl.ds(pl.multiple_of(at * 256, 256), 256)
            f = dot(cv[...], we[:, cols]) + hb[:, cols]
            cdf = normal_cdf(f)
            density = jnp.exp(f * f * -0.5) * 0.3989422804014327
            gp_out[:, local] = (cdf + f * density).astype(BF16)
            gsum[:, cols] = jnp.sum((f * cdf).reshape(caps, length, 256), axis=1)
            return carry

        lax.fori_loop(0, half, step, 0, unroll=2)

    feed(1, gp_send)
    stores.append(load(gp_send, gps_any, out_sems.at[5]))
    feed(0, gp_keep)
    stores.append(load(gp_keep, gpk_any, out_sems.at[6]))
    load_r.wait()
    total = gsum[...]
    pooled = (
        jnp.mean(m_out[...].reshape(caps, length, width), axis=1)
        + split_dot(total * (1.0 / length), wr[...])
        + row(biases, 5)
    )
    r = lax.rsqrt(jnp.sum(pooled * pooled, axis=-1, keepdims=True) + embed_eps)
    emb_out[...] = pooled * r
    r_out[...] = jnp.broadcast_to(r, r_out.shape)
    chips = send_out.shape[0]
    share = hidden // (2 * chips)
    scaled = total * r
    hi = r.astype(BF16).astype(F32)
    mid = (r - hi).astype(BF16).astype(F32)
    slot = lax.broadcasted_iota(jnp.int32, (caps, LANES), 0) + t * caps
    lane = lax.broadcasted_iota(jnp.int32, (caps, LANES), 1)
    extra = jnp.where(lane == EXTRA, hi, 0.0)
    extra = jnp.where(lane == EXTRA + 1, mid, extra)
    extra = jnp.where(lane == EXTRA + 2, r - hi - mid, extra)
    extra = jnp.where((lane == EXTRA + 3) & (slot < scal[2]), 1.0, extra)
    for e in range(chips):
        send_out[e, :, :width] = (pooled * r).astype(BF16)
        for half_at in range(2):
            src = (half_at * chips + e) * share
            piece = jnp.concatenate([scaled[:, src : src + share], extra[:, share:]], axis=1)
            to = width + jnp.bitwise_xor(t, half_at) * LANES
            send_out[e, :, pl.ds(pl.multiple_of(to, LANES), LANES)] = piece.astype(BF16)
    for c in stores:
        c.wait()


PAD = 56


def image_forward_kernel(
    scal, x_any, gains, biases, hid, wq_any, wp_any, we_any, wr_any,
    out,
    x_v, xs, hv, av, qkv, mv, msum, gsum, wq, wp, we, wr, qb, hb, pb, sems,
):
    length, both_caps, width = x_v.shape
    caps = both_caps // 2
    n = caps * PAD
    hidden = hid.shape[0] * LANES
    t = scal[0]
    load_x = load(x_any, x_v, sems.at[0])
    load_q = load(wq_any, wq, sems.at[1])
    masks = head_masks()
    qkv[n:, :] = jnp.zeros((qkv.shape[0] - n, 3 * width), BF16)
    first = (jnp.zeros((1, 1), jnp.int32) + t) == 0
    load_x.wait()

    def pick(i, carry):
        x = x_v[i].astype(F32)
        x = jnp.where(first, x[:caps], x[caps:])
        for k in range(width // LANES):
            xs[k, pl.ds(pl.multiple_of(i * caps, 8), caps), :] = x[:, k * LANES : (k + 1) * LANES]
        return carry

    lax.fori_loop(0, length, pick, 0, unroll=2)

    def first_norm(j, carry):
        base = pl.multiple_of(j * 2 * PAD, 16)
        for e in range(2):
            x = jnp.concatenate(
                [
                    xs[k, pl.ds(j * 2 + e, length, stride=caps), :]
                    for k in range(width // LANES)
                ],
                axis=1,
            )
            x = jnp.concatenate([x, jnp.zeros((PAD - length, width), F32)], axis=0)
            hv[pl.ds(base + e * PAD, PAD), :] = x
            xhat, _ = norm_stats(x)
            x = xhat * row(gains, 0) + row(biases, 0)
            if e == 0:
                kept = x
        av[pl.ds(base, 2 * PAD), :] = jnp.concatenate([kept, x], axis=0).astype(BF16)
        return carry

    lax.fori_loop(0, caps // 2, first_norm, 0, unroll=4)
    load_q.wait()
    load_p = load(wp_any, wp, sems.at[2])
    load_e = load(we_any, we, sems.at[3])
    load_r = load(wr_any, wr, sems.at[4])
    set_qkv_bias(qb, biases)
    set_hidden_bias(hb, hid)

    def to_qkv(j, carry):
        cols = pl.ds(pl.multiple_of(j * 256, 256), 256)
        qkv[:n, cols] = (dot(av[...], wq[:, cols]) + qb[:, cols]).astype(BF16)
        return carry

    lax.fori_loop(0, 3 * width // 256, to_qkv, 0, unroll=9)
    q_at = lax.broadcasted_iota(jnp.int32, (2 * PAD, LANES), 0)
    k_at = lax.broadcasted_iota(jnp.int32, (2 * PAD, LANES), 1)
    low = (q_at < PAD) & (k_at < length)
    high = (q_at >= PAD) & (k_at >= PAD) & (k_at < PAD + length)
    bias = jnp.where(low | high, 0.0, -1e30)

    def attention(j, carry):
        base = pl.multiple_of(j * 2 * PAD, 16)
        rows, keys = pl.ds(base, 2 * PAD), pl.ds(base, LANES)
        for p in range(width // LANES):
            lanes = slice(p * LANES, (p + 1) * LANES)
            q2 = qkv[rows, lanes]
            k2 = qkv[keys, width + p * LANES : width + (p + 1) * LANES]
            v2 = qkv[keys, 2 * width + p * LANES : 2 * width + (p + 1) * LANES]
            av[rows, lanes] = attend(q2, k2, v2, bias, masks)
        return carry

    lax.fori_loop(0, caps // 2, attention, 0, unroll=4)
    load_p.wait()
    pb[...] = row(biases, 4)

    def add_attended(j, carry):
        cols = pl.ds(pl.multiple_of(j * 256, 256), 256)
        mv[:, cols] = hv[:, cols] + dot(av[...], wp[:, cols]) + pb[:, cols]
        return carry

    lax.fori_loop(0, width // 256, add_attended, 0, unroll=3)
    group = 8 * PAD
    tail = (lax.broadcasted_iota(jnp.int32, (1, 8, 1), 1) < length - (PAD - 8)).astype(F32)

    def token_sum(x, count):
        tiles = x.reshape(count, PAD // 8, 8, x.shape[1])
        acc = tiles[:, PAD // 8 - 1] * tail
        for i in range(PAD // 8 - 1):
            acc = acc + tiles[:, i]
        return jnp.sum(acc, axis=1)

    def second_norm(j, carry):
        rows = pl.ds(pl.multiple_of(j * group, 16), group)
        m = mv[rows, :]
        xhat, _ = norm_stats(m)
        av[rows, :] = (xhat * row(gains, 1) + row(biases, 1)).astype(BF16)
        msum[pl.ds(pl.multiple_of(j * 8, 8), 8), :] = token_sum(m, 8)
        return carry

    lax.fori_loop(0, caps // 8, second_norm, 0, unroll=3)
    load_e.wait()

    def feed(j, carry):
        cols = pl.ds(pl.multiple_of(j * 256, 256), 256)
        f = dot(av[...], we[:, cols]) + hb[:, cols]
        gsum[:, cols] = token_sum(f * normal_cdf(f), caps)
        return carry

    lax.fori_loop(0, hidden // 256, feed, 0, unroll=3)
    load_r.wait()
    scale = 1.0 / length
    pooled = msum[...] * scale + split_dot(gsum[...] * scale, wr[...]) + row(biases, 5)
    r_img = lax.rsqrt(jnp.sum(pooled * pooled, axis=-1, keepdims=True) + embed_eps)
    out[...] = (pooled * r_img).astype(BF16)


QUARTERS = ((1, 3), (2, 3), (0, 2), (0, 1))


def loss_kernel(
    rows_block, parts, scal, *refs,
):
    own_any, refs = refs[:parts], refs[parts:]
    (par_any, text_any, text_par_any, expo, emb, r, gpk_any, gpr_any, ct_any, ctr_any,
     we_any, wr_any,
     loss_out, temp_out, ea, eb, ec, ed, g_any, images_any, texts_any, gall_any, extra_any,
     dc_any, dy_out, hid_out,
     own_v, par_v, text_v, text_par_v, texts, images, extra, gall, col_flag, sims, grad,
     chip_g, gpk, gpr, ct, we, wr, dc, exp_s, sems, out_sems) = refs
    chips, caps, width = par_any.shape
    staged = own_v.shape[0] == chips
    total = texts.shape[0]
    near_hidden = gpk.shape[1]
    n = dc.shape[0]
    length = n // caps
    t, d = scal[0], scal[1]
    first = (jnp.zeros((1, 1), jnp.int32) + t) == 0
    if staged:
        each = chips // parts
        waits = [
            load(par_any, par_v, sems.at[0]),
            load(text_any, text_v, sems.at[1]),
            load(text_par_any, text_par_v, sems.at[2]),
        ] + [
            load(own_any[i], own_v.at[pl.ds(i * each, each)], sems.at[3 + i]) for i in range(parts)
        ]
        for c in waits:
            c.wait()

    def place(e, carry):
        at, slot = e, scal[4 + 16 + e]
        if not staged:
            waits = [
                load(src.at[pl.ds(i, 1)], dst, sems.at[j])
                for j, (src, i, dst) in enumerate(
                    ((own_any[0], slot, own_v), (par_any, slot, par_v), (text_any, at, text_v),
                     (text_par_any, at, text_par_v))
                )
            ]
            for c in waits:
                c.wait()
            at = slot = 0

        def pair(x0, x1):
            x0, x1 = x0.astype(F32), x1.astype(F32)
            return jnp.concatenate([jnp.where(first, x0, x1), jnp.where(first, x1, x0)], axis=0)

        rows = pl.ds(pl.multiple_of(e * 2 * caps, 16), 2 * caps)
        images[rows, :] = pair(own_v[slot], par_v[slot]).astype(BF16)
        x0, x1 = text_v[at], text_par_v[at]
        texts[rows, :] = pair(x0[:, :width], x1[:, :width]).astype(BF16)
        last = pair(x0[:, width : width + LANES], x1[:, width + LANES :])
        extra[rows, :] = last
        gall[rows, :] = last.astype(BF16)
        return carry

    lax.fori_loop(0, chips, place, 0, unroll=2)
    half = near_hidden // 256
    later = [
        load(src, dst, sems.at[8 + i])
        for i, (src, dst) in enumerate(
            ((wr_any.at[pl.ds(pl.multiple_of(t * near_hidden, 256), near_hidden)], wr),
             (gpk_any, gpk), (gpr_any, gpr),
             (we_any.at[:, pl.ds(pl.multiple_of(t * near_hidden, 256), near_hidden)], we))
        )
    ]
    for i, src in enumerate((ct_any, ctr_any)):
        later.append(load(src, ct.at[i], sems.at[12 + i]))
    stores = [
        load(src, dst, out_sems.at[i])
        for i, (src, dst) in enumerate(
            ((images, images_any), (texts, texts_any), (gall, gall_any), (extra, extra_any))
        )
    ]
    pick = (lax.broadcasted_iota(jnp.int32, (8, LANES), 1) == EXTRA + 3).astype(F32)
    step = min(256, total)

    def flags(j, carry):
        cols = pl.ds(pl.multiple_of(j * step, step), step)
        col_flag[:, cols] = dot_nt(pick, extra[cols, :])
        return carry

    lax.fori_loop(0, total // step, flags, 0)
    scale = jnp.exp(jnp.full((1, 1), expo[0], F32))
    chunk = 48
    blocks = total // rows_block
    per_block = rows_block // chunk
    live = col_flag[0:1, :]

    def similarities(b):
        base = pl.multiple_of(b * rows_block, 16)

        def cols_step(j, carry):
            cols = pl.ds(pl.multiple_of(j * step, step), step)
            sims[:, cols] = scale * dot_nt(texts[pl.ds(base, rows_block), :], images[cols, :])
            return carry

        lax.fori_loop(0, total // step, cols_step, 0)

    def chunk_at(b, i):
        local = pl.ds(pl.multiple_of(i * chunk, 16), chunk)
        whole = pl.ds(pl.multiple_of(b * rows_block + i * chunk, 16), chunk)
        return local, whole

    def column_block(b, acc):
        similarities(b)

        def adding(i, acc):
            local, whole = chunk_at(b, i)
            live_row = extra[whole, EXTRA + 3 : EXTRA + 4]
            part = jnp.exp(sims[local, :]) * live_row
            return acc + jnp.sum(part.reshape(chunk // 8, 8, total), axis=0)

        return lax.fori_loop(0, per_block, adding, acc, unroll=2)

    col_acc = jnp.zeros((8, total), F32)
    if blocks == 1:
        col_acc = column_block(0, col_acc)
    else:
        col_acc = lax.fori_loop(0, blocks, column_block, col_acc)
    col_sum = jnp.sum(col_acc, axis=0, keepdims=True)
    col_part = 0.5 * live / col_sum

    def row_block(b, carry):
        if blocks > 1:
            similarities(b)

        def rows_step(i, acc):
            loss, temp, diag = acc
            local, whole = chunk_at(b, i)
            s = sims[local, :]
            flag = extra[whole, EXTRA + 3 : EXTRA + 4]
            at = lax.broadcasted_iota(jnp.int32, (chunk, total), 0) + (b * rows_block + i * chunk)
            eye = at == lax.broadcasted_iota(jnp.int32, (chunk, total), 1)
            expd = jnp.exp(s)
            rsum = jnp.sum(expd * live, axis=1, keepdims=True)
            g = expd * ((0.5 * flag / rsum) * live + flag * col_part)
            g = g - jnp.where(eye, 0.5 * (flag + live), 0.0)
            grad[local, :] = g.astype(BF16)
            temp = temp + jnp.sum((g * s).reshape(chunk // 8, 8, total), axis=0)
            diag = diag + jnp.sum(
                jnp.where(eye, s * flag, 0.0).reshape(chunk // 8, 8, total), axis=0
            )
            return loss + 0.5 * flag * jnp.log(rsum), temp, diag

        carry = lax.fori_loop(0, per_block, rows_step, carry, unroll=2)
        mine = d * (2 * caps) - b * rows_block

        @pl.when((mine >= 0) & (mine < rows_block))
        def _():
            chip_g[...] = grad[pl.ds(pl.multiple_of(mine, 16), 2 * caps), :]

        if blocks > 1:
            rows = pl.ds(pl.multiple_of(b * rows_block, 16), rows_block)
            load(grad, g_any.at[rows], out_sems.at[4]).wait()
        return carry

    start = (jnp.zeros((chunk, 1), F32), jnp.zeros((8, total), F32), jnp.zeros((8, total), F32))
    if blocks == 1:
        loss, temp, diag = row_block(0, start)
        stores.append(load(grad, g_any, out_sems.at[4]))
    else:
        loss, temp, diag = lax.fori_loop(0, blocks, row_block, start)
    def whole(x):
        return jnp.sum(jnp.sum(x, axis=0, keepdims=True), axis=1, keepdims=True)

    objective = whole(loss) + 0.5 * whole(live * jnp.log(col_sum)) - whole(diag)
    loss_out[...] = objective / whole(live)
    temp_out[...] = whole(temp)

    both_dt = scale * dot(chip_g[...], images[...])
    chip = pl.ds(pl.multiple_of(d * 2 * caps, 16), 2 * caps)
    inv = jnp.sum(extra[chip, EXTRA : EXTRA + 3], axis=1, keepdims=True)
    dt = jnp.where(first, both_dt[:caps], both_dt[caps:])
    dt_far = jnp.where(first, both_dt[caps:], both_dt[:caps])
    both_tx = texts[chip, :].astype(F32)
    tx_far = jnp.where(first, both_tx[caps:], both_tx[:caps])
    inv_far = jnp.where(first, inv[caps:], inv[:caps])

    def pooled_back(tx, dt, inv):
        return inv * (dt - tx * jnp.sum(tx * dt, axis=1, keepdims=True)) * (1.0 / length)

    dy = pooled_back(emb[...], dt, r[:, 0:1])
    dy_out[...] = dy
    dyb = jnp.concatenate([dy, pooled_back(tx_far, dt_far, inv_far)], axis=0).astype(BF16)
    for c in later:
        c.wait()
    dc[...] = jnp.zeros_like(dc)

    def near(j, carry):
        cols = pl.ds(pl.multiple_of(j * 256, 256), 256)
        dg = dot_nt(dyb, wr[cols, :])
        df = (gpk[:, cols].astype(F32).reshape(caps, length, 256) * dg[:caps][:, None, :]).reshape(
            n, 256
        )
        far = (gpr[:, cols].astype(F32).reshape(caps, length, 256) * dg[caps:][:, None, :]).reshape(
            n, 256
        )
        df, far = df.astype(BF16), far.astype(BF16)
        hid_out[0:1, cols] = jnp.sum(df.astype(F32) + far.astype(F32), axis=0, keepdims=True)
        dc[...] += dot_nt(df, we[:, cols])
        side = near_hidden // 512
        local = pl.ds(pl.multiple_of((j % side) * 256, 256), 256)
        exp_s[j // side, :, local] = (
            dot(ct[0].reshape(width, n), df) + dot(ct[1].reshape(width, n), far)
        ).astype(BF16)
        return carry

    lax.fori_loop(0, half, near, 0, unroll=2)
    quarter = width // 4
    for i, out in enumerate((ea, eb, ec, ed)):
        for j, q in enumerate(QUARTERS[i]):
            stores.append(
                load(
                    exp_s.at[i % 2, pl.ds(q * quarter, quarter)],
                    out.at[pl.ds(j * quarter, quarter)],
                    out_sems.at[5 + 2 * i + j],
                )
            )
    stores.append(load(dc, dc_any, out_sems.at[13]))
    for c in stores:
        c.wait()


def middle_back_kernel(
    scal, dc_any, dy, gps_any, m_any, gains, we_any, wr_any, wp_any, qkv_any,
    dm_any, dqkv_any, vec_out,
    dc, gps, mv, we, wr, wp, qkv, dm, dmb, dov, dqkv, sems,
):
    n, width = dm.shape
    caps = dy.shape[0]
    length = n // caps
    far_hidden = gps.shape[1]
    t = scal[0]
    away = pl.ds(pl.multiple_of((1 - t) * far_hidden, 256), far_hidden)
    half = far_hidden // 512
    parts = []
    for i in range(2):
        at = pl.ds(pl.multiple_of(((1 - t) * 2 + i) * half * 256, 256), half * 256)
        here = pl.ds(i * half * 256, half * 256)
        parts.append([
            load(wr_any.at[at], wr.at[here], sems.at[3 * i]),
            load(gps_any.at[:, here], gps.at[:, here], sems.at[3 * i + 1]),
            load(we_any.at[:, at], we.at[:, here], sems.at[3 * i + 2]),
        ])
        if i == 0:
            load_dc = load(dc_any, dc, sems.at[9])
    for c in parts[0]:
        c.wait()
    load_dc.wait()
    load_m = load(m_any, mv, sems.at[10])
    load_p = load(wp_any, wp, sems.at[11])
    load_qkv = load(qkv_any, qkv, sems.at[6])
    dyv = dy[...]
    dyb = dyv.astype(BF16)

    def feed(j, carry):
        cols = pl.ds(pl.multiple_of(j * 256, 256), 256)
        dg = dot_nt(dyb, wr[cols, :])
        df = gps[:, cols].astype(F32).reshape(caps, length, 256) * dg[:, None, :]
        dc[...] += dot_nt(df.reshape(n, 256).astype(BF16), we[:, cols])
        return carry

    lax.fori_loop(0, half, feed, 0, unroll=3)
    for c in parts[1]:
        c.wait()
    lax.fori_loop(half, 2 * half, feed, 0, unroll=3)
    load_m.wait()
    piece = 8 * length

    def norm(i, sums):
        rows = pl.ds(pl.multiple_of(i * piece, piece), piece)
        xhat, rstd = norm_stats(mv[rows, :])
        dcv = dc[rows, :]
        back = norm_back(dcv * row(gains, 1), xhat, rstd)
        dy_rows = dy[pl.ds(pl.multiple_of(i * 8, 8), 8), :]
        out = (back.reshape(piece // length, length, width) + dy_rows[:, None, :]).reshape(
            piece, width
        )
        dm[rows, :] = out
        low = out.astype(BF16)
        dmb[rows, :] = low

        def fold(x):
            return jnp.sum(x.reshape(piece // 8, 8, width), axis=0)

        return sums[0] + fold(dcv * xhat), sums[1] + fold(dcv), sums[2] + fold(low.astype(F32))

    blank = jnp.zeros((8, width), F32)
    sums = lax.fori_loop(0, n // piece, norm, (blank, blank, blank))
    store_dm = load(dm, dm_any, sems.at[7])
    load_p.wait()
    dov[...] = dot_nt(dmb[...], wp[...]).astype(BF16)
    load_qkv.wait()
    masks = head_masks()
    same = (
        lax.broadcasted_iota(jnp.int32, (LANES, LANES), 0) // length
        == lax.broadcasted_iota(jnp.int32, (LANES, LANES), 1) // length
    )
    bias = jnp.where(same, 0.0, -1e30)

    def attention(g, carry):
        rows = pl.ds(pl.multiple_of(g * LANES, LANES), LANES)
        for p in range(width // LANES):
            lanes = slice(p * LANES, (p + 1) * LANES)
            k_lanes = slice(width + p * LANES, width + (p + 1) * LANES)
            v_lanes = slice(2 * width + p * LANES, 2 * width + (p + 1) * LANES)
            q2 = qkv[rows, lanes] * BF16(0.125)
            km = two_heads(qkv[rows, k_lanes], masks)
            vm = two_heads(qkv[rows, v_lanes], masks)
            do2 = dov[rows, lanes]
            parts = softmax_parts(dot_nt(q2, km), bias)
            dp = dot_nt(do2, vm)
            pb, ds = [], []
            for e in range(2):
                prob = parts[e] * (1.0 / jnp.sum(parts[e], axis=-1, keepdims=True))
                dpe = dp[:, e * LANES : (e + 1) * LANES]
                inner = jnp.sum(prob * dpe, axis=-1, keepdims=True)
                pb.append(prob.astype(BF16))
                ds.append((prob * (dpe - inner)).astype(BF16))
            dqkv[rows, lanes] = (dot(jnp.concatenate(ds, axis=1), km) * 0.125).astype(BF16)
            dqkv[rows, k_lanes] = dot_tn(jnp.concatenate(ds, axis=0), two_heads(q2, masks)).astype(
                BF16
            )
            dqkv[rows, v_lanes] = dot_tn(
                jnp.concatenate(pb, axis=0), two_heads(do2, masks)
            ).astype(BF16)
        return carry

    lax.fori_loop(0, n // LANES, attention, 0)
    store = load(dqkv, dqkv_any, sems.at[8])
    for i in range(3):
        vec_out[i : i + 1, :] = jnp.sum(sums[i], axis=0, keepdims=True)
    vec_out[3:4, :] = jnp.sum(dqkv[:, :width].astype(F32), axis=0, keepdims=True)
    vec_out[4:5, :] = jnp.sum(dqkv[:, 2 * width :].astype(F32), axis=0, keepdims=True)
    vec_out[5:8, :] = jnp.zeros((3, width), F32)
    store_dm.wait()
    store.wait()


def weight_grad_kernel(with_hid, scal, dm_any, dqkv_any, at_any, ot_any, wq_any, gains, biases, vec,
                       hid, *rest):
    turn, rest = (rest[:4], rest[4:]) if with_hid else ((), rest)
    keep_a, keep_b, send_a, send_b = rest[:4]
    turned, rest = (rest[4:8], rest[8:]) if with_hid else ((), rest[4:])
    dm, at, ot, dmb, dqkv, wq, grads, tails, inner_v, small, sems, store_sems = rest[:12]
    held, turn_sems = rest[12:16], rest[16:]
    n, width = dm.shape
    t = scal[0]
    load_dm = load(dm_any, dm, sems.at[0])
    load_o = load(ot_any, ot, sems.at[1])
    load_qkv = load(dqkv_any, dqkv, sems.at[2])
    load_a = load(at_any, at, sems.at[3])
    blocks, block = at.shape[:2]
    loads_t = [load(src, dst, turn_sems[0].at[i]) for i, (src, dst) in enumerate(zip(turn, held))]
    load_dm.wait()
    dmb[...] = dm[...].astype(BF16)
    load_o.wait()
    loads_w = [
        load(wq_any.at[pl.ds(e * block, block)], wq.at[scal[4 + e]], sems.at[8 + e])
        for e in range(blocks)
    ]
    half, quarter = width // 2, width // 4

    def project(hh, carry):
        cols = pl.ds(pl.multiple_of(hh * half, LANES), half)
        grads[hh, 0] = dot(ot[...].reshape(width, n), dmb[:, cols]).astype(BF16)
        return carry

    lax.fori_loop(0, 2, project, 0)
    for c in loads_t:
        c.wait()
    for side in range(len(turned) // 2):
        total = held[2 * side][...].astype(F32) + held[2 * side + 1][...].astype(F32)
        turned[side][...] = total[:quarter]
        turned[2 + side][...] = total[quarter:].astype(BF16)
    load_qkv.wait()
    load_a.wait()
    for c in loads_w:
        c.wait()
    inner_v[...] = jnp.zeros_like(inner_v)

    def attend_in(c, carry):
        cols = pl.ds(pl.multiple_of(c * half, LANES), half)
        value = dot(at[...].reshape(width, n), dqkv[:, cols])
        grads[c // 3, 1 + c % 3] = value.astype(BF16)
        prod = value * wq[:, :, cols].reshape(width, half).astype(F32)
        acc = inner_v[...]
        for k in range(half // LANES):
            acc = acc + prod[:, k * LANES : (k + 1) * LANES]
        inner_v[...] = acc
        return carry

    lax.fori_loop(0, 6, attend_in, 0)

    def move(src, out, side, lanes, slot):
        return [
            load(
                src.at[pl.ds(q * quarter, quarter)],
                out.at[i, pl.ds(j * quarter, quarter), pl.ds(lanes, src.shape[1])],
                store_sems.at[slot + 2 * i + j],
            )
            for i in range(2)
            for j, q in enumerate(QUARTERS[side + 2 * i])
        ]

    stores = []
    for k, (hh, out_a, out_b) in enumerate(((1 - t, send_a, send_b), (t, keep_a, keep_b))):
        for part in range(4):
            out = (out_a, out_b)[part // 2]
            stores += move(grads.at[hh, part], out, part // 2, (part % 2) * half, 20 * k + 4 * part)
    inner = inner_v[...]
    inner = jnp.sum(inner, axis=1, keepdims=True)
    sums = jnp.sum(dqkv[...].astype(F32), axis=0, keepdims=True)
    hi = sums.astype(BF16)
    lo = (sums - hi.astype(F32)).astype(BF16)
    both = jnp.concatenate([hi, lo, jnp.zeros((14, 3 * width), BF16)], axis=0)
    shift1 = dot_nt(wq[...].reshape(width, 3 * width), both)
    shift1 = shift1[:, 0:1] + shift1[:, 1:2]
    first = (jnp.zeros((1, 1), jnp.int32) + t) == 0
    zero = jnp.zeros((1, width), F32)
    for_zero = jnp.concatenate([zero, zero, vec[1:2, :], vec[3:4, :], zero, zero], axis=0)
    for_one = jnp.concatenate([vec[0:1, :], vec[4:5, :], vec[2:3, :], zero, zero, zero], axis=0)
    ends = jnp.concatenate([1.0 / row(gains, 0), row(biases, 0)], axis=0)
    lines = jnp.concatenate([for_zero, ends, for_one, ends], axis=0).T
    lane = lax.broadcasted_iota(jnp.int32, (1, 8), 1)
    if with_hid:
        columns = jnp.broadcast_to(hid[...], (8, hid.shape[1])).T
    for e in range(blocks):
        at_block = slice(e * block, (e + 1) * block)
        if with_hid:
            pick = columns[2 * e * block : (2 * e + 1) * block] * (lane == 4).astype(F32)
            pick = pick + columns[(2 * e + 1) * block : (2 * e + 2) * block] * (lane == 5).astype(F32)
        else:
            pick = jnp.zeros((block, 8), F32)
        small[scal[4 + e]] = jnp.concatenate(
            [lines[at_block, :8], lines[at_block, 8:], pick,
             jnp.zeros((block, LANES - 24), F32)], axis=1
        )
    sv = small[...].reshape(width, LANES)
    zeros_set, ones_set, own = sv[:, :8], sv[:, 8:16], sv[:, 16:24]
    gain1 = zeros_set[:, 6:7] * (inner - zeros_set[:, 7:8] * shift1)
    zeros_set = zeros_set + gain1 * (lane == 0).astype(F32) + shift1 * (lane == 1).astype(F32)
    used = (lane < 4).astype(F32)
    zeros_set, ones_set = zeros_set * used, ones_set * used
    keep_set = jnp.where(first, zeros_set, ones_set) + own
    send_set = jnp.where(first, ones_set, zeros_set)
    for hh in range(2):
        value = jnp.where((jnp.zeros((1, 1), jnp.int32) + t) == hh, keep_set, send_set)
        hi = value.astype(BF16).astype(F32)
        fill = jnp.zeros((width, LANES // 2 - 8), F32)
        tails[hh] = jnp.concatenate([hi, fill, value - hi, fill], axis=1).astype(BF16)
    stores += move(tails.at[1 - t], send_b, 1, width, 16)
    stores += move(tails.at[t], keep_b, 1, width, 36)
    for c in stores:
        c.wait()


def input_back_kernel(
    scal, dm_any, h_any, gains, dqkv_any, wq_any, order_any,
    tok_keep, tok_send,
    h_v, wq, dm, dqkv, da, sems,
):
    n, width = dm.shape
    caps, half_len, _ = tok_keep.shape
    t = scal[0]
    loads = [
        load(src, dst, sems.at[i])
        for i, (src, dst) in enumerate(
            ((dqkv_any, dqkv), (wq_any, wq),
             (h_any.at[pl.ds(pl.multiple_of(t * n, n), n)], h_v), (dm_any, dm))
        )
    ]
    loads[0].wait()
    loads[1].wait()

    def back(j, carry):
        rows = pl.ds(pl.multiple_of(j * 256, 256), 256)
        da[:, rows] = dot_nt(dqkv[...], wq[rows, :])
        return carry

    lax.fori_loop(0, width // 256, back, 0, unroll=3)
    loads[2].wait()
    loads[3].wait()
    piece = 8 * 2 * half_len
    first = (jnp.zeros((1, 1, 1), jnp.int32) + t) == 0

    def norm(i, carry):
        rows = pl.ds(pl.multiple_of(i * piece, piece), piece)
        xhat, rstd = norm_stats(h_v[rows, :].astype(F32))
        grad = dm[rows, :] + norm_back(da[rows, :] * row(gains, 0), xhat, rstd)
        halves = grad.reshape(8, 2, half_len, width)
        at = pl.ds(pl.multiple_of(i * 8, 8), 8)
        tok_keep[at] = jnp.where(first, halves[:, 0], halves[:, 1])
        tok_send[at] = jnp.where(first, halves[:, 1], halves[:, 0]).astype(BF16)
        return carry

    lax.fori_loop(0, n // piece, norm, 0)


def reduce_grad_kernel(
    rows_block, length, expo, g_any, images_any, texts_any, gall_any, extra_any, order_any,
    red_out, bias_out,
    g_v, images, texts, gall, extra, acc, sems,
):
    total, width = images.shape
    blocks = total // rows_block
    share = red_out.shape[0]
    whole = load(images_any, images, sems.at[0])
    scale = jnp.exp(jnp.full((1, 1), expo[0], F32))
    acc[...] = jnp.zeros_like(acc)
    whole.wait()

    def block(b, rb):
        rows = pl.ds(pl.multiple_of(b * rows_block, 16), rows_block)
        waits = [
            load(src.at[rows], dst, sems.at[1 + i])
            for i, (src, dst) in enumerate(
                ((g_any, g_v), (texts_any, texts), (gall_any, gall), (extra_any, extra))
            )
        ]
        for c in waits:
            c.wait()
        def project(i, rb):
            at = pl.ds(pl.multiple_of(i * 96, 96), 96)
            dt = scale * dot(g_v[at, :], images[...])
            tx = texts[at, :].astype(F32)
            part = (dt - tx * jnp.sum(tx * dt, axis=1, keepdims=True)) * (1.0 / length)
            part = part.astype(BF16)
            texts[at, :] = part
            inv = jnp.sum(extra[at, EXTRA : EXTRA + 3], axis=1, keepdims=True)
            return rb + jnp.sum(part.astype(F32) * inv, axis=0, keepdims=True)

        rb = lax.fori_loop(0, rows_block // 96, project, rb)
        acc[...] += dot_tn(gall[...], texts[...])
        return rb

    rb = lax.fori_loop(0, blocks, block, jnp.zeros((1, width), F32))
    red_out[...] = acc[:share, :]
    bias_out[...] = jnp.broadcast_to(rb * float(length), bias_out.shape)


def to_wire(x, width):
    low = x.astype(BF16)
    if x.shape[1] == width:
        return low
    rest = x[:, width:] - low[:, width:].astype(F32)
    return jnp.concatenate([low, rest.astype(BF16)], axis=1)


def from_wire(x, width):
    y = x.astype(F32)
    if x.shape[1] == width:
        return y
    return jnp.concatenate([y[:, :width], y[:, width : width + 64] + y[:, width + 64 :]], axis=1)


def wire_kernel(width, qa, qa_back, qb, qb_back, far_a, far_b, wire_a, wire_b, a0, a1, b0, b1,
                sems):
    loads = [
        load(src.at[0], dst, sems.at[i])
        for i, (src, dst) in enumerate(((qa, a0), (qa_back, a1), (qb, b0), (qb_back, b1)))
    ]
    loads[0].wait()
    loads[1].wait()
    wire_a[...] = (a0[...].astype(F32) + a1[...].astype(F32)).astype(BF16)
    loads[2].wait()
    loads[3].wait()
    wire_b[...] = to_wire(from_wire(b0[...], width) + from_wire(b1[...], width), width)


def turn_kernel(width, stacked, count, *refs):
    ins, (kept_a, kept_b, next_a, next_b) = refs[: 2 * count], refs[2 * count : 2 * count + 4]
    scratch, sems = refs[2 * count + 4 : -1], refs[-1]
    loads = [
        load(src.at[1] if i % count < stacked else src, dst, sems.at[i])
        for i, (src, dst) in enumerate(zip(ins, scratch))
    ]
    half = kept_a.shape[0]
    for side, (kept, moved) in enumerate(((kept_a, next_a), (kept_b, next_b))):
        at = range(side * count, (side + 1) * count)
        for i in at:
            loads[i].wait()
        total = from_wire(scratch[at[0]][...], width)
        for i in at[1:]:
            total = total + from_wire(scratch[i][...], width)
        kept[...] = total[:half]
        moved[...] = to_wire(total[half:], width)


def merge_kernel(width, sum_a, sum_b, hop_a, hop_b, *rest):
    outs = rest[-4:]
    for i, out in enumerate(outs):
        rows = out.shape[0]
        at = slice(i * rows, (i + 1) * rows)
        a = sum_a[at, :] + hop_a[at, :].astype(F32)
        b = sum_b[at, :] + from_wire(hop_b[at, :], width)
        if i == 0:
            out[:, :width] = a
            out[:, width:] = b
        else:
            out[:, :width] = a.astype(BF16)
            out[:, width:] = to_wire(b, width)


def finish_kernel(width, scal, total, hop_1, hop_2, hop_3, rbias,
                  qkv_out, project_out, gains_out, biases_out, hid_out):
    half = width // 2
    rows, cols = project_out.shape[0], width
    t, d = scal[0], scal[1]
    acc = total[...]
    for hop in (hop_1, hop_2, hop_3):
        x = hop[...]
        acc = acc + jnp.concatenate(
            [x[:, :width].astype(F32), from_wire(x[:, width:], width)], axis=1
        )
    project_out[...] = acc[:, :half]
    qkv_out[...] = acc[:, half : 2 * width]
    small = acc[:, 2 * width : 2 * width + 8].T
    lane = lax.broadcasted_iota(jnp.int32, (rows, cols), 1)
    mine = lax.broadcasted_iota(jnp.int32, (rows, cols), 0) + d * rows
    last = jnp.sum(jnp.where(lane == mine, rbias[0:1, :], 0.0), axis=1, keepdims=True)
    last = jnp.broadcast_to(last, (rows, 8)).T
    first = (jnp.zeros((1, 1), jnp.int32) + t) == 0
    gains_out[...] = small[0:1]
    biases_out[...] = jnp.concatenate(
        [small[1:3], jnp.where(first, small[3:4], last[0:1])], axis=0
    )
    hid_out[...] = jnp.concatenate([small[4:5], small[5:6]], axis=1)


def xor_permute(x, axis, bit):
    return lax.ppermute(x, axis, [(i, i ^ bit) for i in range(lax.axis_size(axis))])


def bit_groups(count):
    bits = [1 << i for i in range(count.bit_length() - 1)]
    groups = [tuple(bits[i : i + 2]) for i in range(0, len(bits), 2)]
    return groups[::-1]


def reaches(group):
    out = [0]
    for bit in group:
        out = out + [r ^ bit for r in out]
    return out


def slot_reaches(count):
    order = [0]
    for group in bit_groups(count):
        order = [r ^ o for r in reaches(group) for o in order]
    return order


def hop(sends, group):
    return [x if r == 0 else xor_permute(x, "dp", r) for x, r in zip(sends, reaches(group))]


def scatter_sum(s, groups, to_wire=lambda x: x, from_wire=lambda x: x):
    for group in reversed(groups):
        hops = reaches(group)
        rows = s.shape[0] // len(hops)
        parts = [s[i * rows : (i + 1) * rows] for i in range(len(hops))]
        moved = [xor_permute(to_wire(parts[i]), "dp", r) for i, r in enumerate(hops) if r]
        s = parts[0]
        for piece in moved:
            s = s + from_wire(piece)
    return s


def flip_by(x, index, count):
    for i in range(count.bit_length() - 1):
        bit = 1 << i
        shape = x.shape
        pairs = x.reshape((count // (2 * bit), 2, bit) + shape[1:])
        x = jnp.where((index & bit) != 0, pairs[:, ::-1], pairs).reshape(shape)
    return x


SMEM = pl.BlockSpec(memory_space=pltpu.SMEM)
VMEM = pl.BlockSpec(memory_space=pltpu.VMEM)
ANY = pl.BlockSpec(memory_space=pl.ANY)


def padded_bytes(shape, dtype):
    size = jnp.dtype(dtype).itemsize
    shape = (1,) * (2 - len(shape)) + tuple(shape)
    rows = -(-shape[-2] // 16) * 16
    return math.prod(shape[:-2]) * rows * (-(-shape[-1] // LANES) * LANES) * size


def call(kernel, name, in_specs, outs, out_specs, scratch, args, flops, moved):
    held = [(x.shape, x.dtype) for x in scratch if jnp.issubdtype(x.dtype, jnp.floating)]
    held += [(a.shape, a.dtype) for a, spec in zip(args, in_specs) if spec is VMEM]
    held += [o for o, spec in zip(outs, out_specs) if spec is VMEM]
    limit = VMEM_LIMIT
    if name in SMALL:
        limit = min(limit, sum(padded_bytes(*x) for x in held) + MARGIN)
    return pl.pallas_call(
        kernel,
        name=name,
        in_specs=in_specs,
        out_shape=[jax.ShapeDtypeStruct(s, d) for s, d in outs],
        out_specs=out_specs,
        scratch_shapes=scratch,
        compiler_params=pltpu.CompilerParams(vmem_limit_bytes=limit),
        cost_estimate=pl.CostEstimate(flops=flops, bytes_accessed=moved, transcendentals=0),
    )(*args)


def body(
    pictures, captions, tallies, exponent,
    p_gains, p_biases, p_hid, p_wq, p_wp, p_we, p_wr,
    c_gains, c_biases, c_hid, c_wq, c_wp, c_we, c_wr,
):
    t = lax.axis_index("tower")
    d = lax.axis_index("dp")
    chips = lax.axis_size("dp")
    pairs, length, width = captions.shape
    img_len = pictures.shape[1]
    hidden = c_hid.shape[0]
    caps = pairs // 2
    n = caps * length
    total = pairs * chips
    row_blocks = 16
    order = np.array(slot_reaches(chips))
    away = jnp.arange(chips, dtype=jnp.int32) ^ d
    slots, stride = jnp.zeros(chips, jnp.int32), 1
    for group in bit_groups(chips):
        slots = slots + ((away >> (group[0].bit_length() - 1)) & (len(reaches(group)) - 1)) * stride
        stride *= len(reaches(group))
    relative = chips == row_blocks
    row_slots = slots if relative else jnp.arange(row_blocks, dtype=jnp.int32)
    head = jnp.stack([t, d, tallies[0], t]).astype(jnp.int32)
    scal = jnp.concatenate([head, row_slots, slots])

    texts_in = captions.reshape(pairs * length, width)
    c_hid2, p_hid2 = c_hid.reshape(hidden // LANES, LANES), p_hid.reshape(hidden // LANES, LANES)
    blk = (row_blocks, width // row_blocks, n)
    vm = pltpu.VMEM
    sem = pltpu.SemaphoreType.DMA
    half_hid = (n, hidden // 2)
    chunk = width + 2 * LANES
    a_t, qkv, o_t, m, c_t, gp_keep, gp_send, text_send, emb, r = call(
        text_forward_kernel, "text_forward",
        [SMEM, ANY, VMEM, VMEM, VMEM, ANY, ANY, ANY, ANY],
        [(blk, BF16), ((n, 3 * width), BF16), (blk, BF16), ((n, width), F32), (blk, BF16),
         (half_hid, BF16), (half_hid, BF16), ((chips, caps, chunk), BF16),
         ((caps, width), F32), ((caps, LANES), F32)],
        [ANY] * 7 + [VMEM] * 3,
        [vm((n, width), BF16), vm((width, 3 * width), BF16), vm((width, width), BF16),
         vm((width, hidden), BF16), vm((hidden, width), BF16), vm((1, 3 * width), F32),
         vm((1, hidden), F32),
         vm((n, width), BF16), vm((n, width), BF16), vm((caps, hidden), F32), vm(blk, BF16), vm((n, 3 * width), BF16),
         vm(blk, BF16), vm((n, width), F32), vm(blk, BF16), vm(half_hid, BF16),
         vm(half_hid, BF16), sem((5,)), sem((7,))],
        (scal, texts_in, c_gains, c_biases, c_hid2, c_wq, c_wp, c_we, c_wr),
        int(2 * n * width * (4 * width + hidden)), 20_000_000,
    )
    c_far = xor_permute(c_t, "tower", 1)
    gp_far = xor_permute(gp_send, "tower", 1)
    text_all = lax.all_to_all(text_send, "dp", 0, 0, tiled=True)

    rows = caps * PAD
    groups = bit_groups(chips)
    (image,) = call(
        image_forward_kernel, "image_forward",
        [SMEM, ANY, VMEM, VMEM, VMEM, ANY, ANY, ANY, ANY],
        [((caps, width), BF16)],
        [VMEM],
        [vm((img_len, pairs, width), BF16), vm((width // LANES, img_len * caps, LANES), F32),
         vm((rows, width), F32), vm((rows, width), BF16),
         vm((rows + 16, 3 * width), BF16), vm((rows, width), F32), vm((caps, width), F32),
         vm((caps, hidden), F32), vm((width, 3 * width), BF16), vm((width, width), BF16),
         vm((width, hidden), BF16), vm((hidden, width), BF16), vm((1, 3 * width), F32),
         vm((1, hidden), F32),
         vm((1, width), F32), sem((5,))],
        (scal, jnp.transpose(pictures, (1, 0, 2)), p_gains, p_biases, p_hid2,
         p_wq, p_wp, p_we, p_wr),
        int(2 * rows * width * (4 * width + hidden)), 20_000_000,
    )
    image, text_all = lax.optimization_barrier((image, text_all))
    text_par = xor_permute(text_all, "tower", 1)
    got = hop([image[None]] * len(reaches(groups[0])), groups[0])
    for group in groups[1:]:
        whole = jnp.concatenate(got, axis=0)
        got = hop([whole] * len(reaches(group)), group)
    par_all = xor_permute(jnp.concatenate(got, axis=0), "tower", 1)
    small_slice = total <= 768
    if not small_slice:
        got = [jnp.concatenate(got, axis=0)]

    block = total if small_slice else 96
    held = chips if small_slice else 1
    share = hidden // (2 * chips)
    piece_shape = (width // 2, width)
    (loss, temp, ea, eb, ec, ed, g_all, images_all, texts_all, gall, extra, dc, dy, hid_grad) = call(
        partial(loss_kernel, block, len(got)), "loss",
        [SMEM] + [ANY] * len(got) + [ANY, ANY, ANY, SMEM, VMEM, VMEM] + [ANY] * 6,
        [((1, 1), F32), ((1, 1), F32)] + [(piece_shape, BF16)] * 4
        + [((total, total), BF16), ((total, width), BF16), ((total, width), BF16),
           ((total, LANES), BF16), ((total, LANES), F32), ((n, width), F32), ((caps, width), F32),
           ((1, hidden // 2), F32)],
        [VMEM, VMEM] + [ANY] * 10 + [VMEM, VMEM],
        [vm((held, caps, width), BF16), vm((held, caps, width), BF16),
         vm((held, caps, chunk), BF16), vm((held, caps, chunk), BF16),
         vm((total, width), BF16), vm((total, width), BF16), vm((total, LANES), F32),
         vm((total, LANES), BF16), vm((8, total), F32),
         vm((block, total), F32), vm((block, total), BF16), vm((2 * caps, total), BF16),
         vm(half_hid, BF16), vm(half_hid, BF16), vm((2,) + blk, BF16),
         vm((width, hidden // 2), BF16), vm((hidden // 2, width), BF16),
         vm((n, width), F32), vm((2, width, hidden // 4), BF16), sem((16,)), sem((14,))],
        (scal, *got, par_all, text_all, text_par, exponent, emb, r, gp_keep, gp_far,
         c_t, c_far, c_we, c_wr),
        int(3 * n * width * hidden), 20_000_000,
    )

    def widen(x):
        return x.astype(F32)

    def narrow(x):
        return x.astype(BF16)

    e_hops = [xor_permute(ea, "dp", 1), xor_permute(eb, "dp", 2)] if relative else []
    dm, dqkv, vec = call(
        middle_back_kernel, "middle_back",
        [SMEM, ANY, VMEM, ANY, ANY, VMEM] + [ANY] * 4,
        [((n, width), F32), ((n, 3 * width), BF16), ((8, width), F32)],
        [ANY, ANY, VMEM],
        [vm((n, width), F32), vm(half_hid, BF16), vm((n, width), F32),
         vm((width, hidden // 2), BF16), vm((hidden // 2, width), BF16), vm((width, width), BF16),
         vm((n, 3 * width), BF16), vm((n, width), F32), vm((n, width), BF16),
         vm((n, width), BF16), vm((n, 3 * width), BF16), sem((12,))],
        (scal, dc, dy, gp_send, m, c_gains, c_we, c_wr, c_wp, qkv),
        int(2 * n * width * (hidden + 4 * width)), 20_000_000,
    )
    b_shape = (width // 2, width + LANES)
    quarter_shape = (width // 4, width)
    qa_keep, qb_keep, qa_send, qb_send, *turned = call(
        partial(weight_grad_kernel, relative), "weight_grad",
        [SMEM] + [ANY] * 5 + [VMEM] * 4 + [ANY] * (4 if relative else 0),
        [((2,) + piece_shape, BF16), ((2,) + b_shape, BF16)] * 2
        + ([(quarter_shape, F32)] * 2 + [(quarter_shape, BF16)] * 2 if relative else []),
        [ANY] * 4 + [VMEM] * (4 if relative else 0),
        [vm((n, width), F32), vm(blk, BF16), vm(blk, BF16), vm((n, width), BF16),
         vm((n, 3 * width), BF16), vm((row_blocks, width // row_blocks, 3 * width), BF16),
         vm((2, 4, width, width // 2), BF16), vm((2, width, LANES), BF16), vm((width, LANES), F32),
         vm((row_blocks, width // row_blocks, LANES), F32), sem((8 + row_blocks,)), sem((40,))]
        + ([vm(piece_shape, BF16)] * 4 + [sem((4,))] if relative else []),
        (scal, dm, dqkv, a_t, o_t, c_wq, c_gains, c_biases, vec, hid_grad)
        + ((ec, e_hops[0], ed, e_hops[1]) if relative else ()),
        int(2 * n * width * 4 * width), 20_000_000,
    )
    qa_back = xor_permute(qa_send, "tower", 1)
    qb_back = xor_permute(qb_send, "tower", 1)
    cols = width // chips
    if relative:
        e_parts = (
            turned[0], turned[1], xor_permute(turned[2], "dp", 2), xor_permute(turned[3], "dp", 1)
        )
        wire_a, wire_b = call(
            partial(wire_kernel, width), "wire", [ANY] * 6,
            [(piece_shape, BF16), (b_shape, BF16)], [VMEM] * 2,
            [vm(piece_shape, BF16)] * 2 + [vm(b_shape, BF16)] * 2 + [sem((4,))],
            (qa_keep, qa_back, qb_keep, qb_back, *e_parts[2:]), 1_000_000, 4_000_000,
        )
        q_hops = [xor_permute(wire_a, "dp", 1), xor_permute(wire_b, "dp", 2)]
    else:
        q_sums = [
            from_wire(x[i], width) + from_wire(y[i], width)
            for i in range(2)
            for x, y in ((qa_keep, qa_back), (qb_keep, qb_back))
        ]
        tails = jnp.transpose(hid_grad.reshape(chips, 2, cols), (0, 2, 1)).reshape(width, 2)
        tails = jnp.pad(tails, ((0, 0), (width + 4, 64 - 6)))
        quarter = width // 4
        for i in (1, 3):
            q_sums[i] = q_sums[i] + jnp.concatenate(
                [tails[q * quarter : (q + 1) * quarter] for q in QUARTERS[i]], axis=0
            )
        wire_b = qb_back
        q_hops = []
    tok_keep, tok_send = call(
        input_back_kernel, "input_back",
        [SMEM, ANY, ANY, VMEM, ANY, ANY, ANY],
        [((caps, length // 2, width), F32), ((caps, length // 2, width), BF16)],
        [VMEM] * 2,
        [vm((n, width), BF16), vm((width, 3 * width), BF16), vm((n, width), F32),
         vm((n, 3 * width), BF16), vm((n, width), F32), sem((4,))],
        (scal, dm, texts_in, c_gains, dqkv, c_wq, wire_b),
        int(2 * n * width * 3 * width), 9_000_000,
    )
    reduce_grad, rbias = call(
        partial(reduce_grad_kernel, block, length), "reduce_grad",
        [SMEM] + [ANY] * 6,
        [((share, width), F32), ((8, width), F32)],
        [VMEM, VMEM],
        [vm((block, total), BF16), vm((total, width), BF16), vm((block, width), BF16),
         vm((block, LANES), BF16), vm((block, LANES), F32), vm((LANES, width), F32), sem((5,))],
        (exponent, g_all, images_all, texts_all, gall, extra, q_hops[0] if relative else wire_b),
        int(2 * total * total * width), 6_000_000,
    )

    tok_back = widen(xor_permute(tok_send, "tower", 1))
    grad_tokens = jnp.concatenate(
        [jnp.where(t == 0, tok_keep, tok_back), jnp.where(t == 0, tok_back, tok_keep)], axis=0
    )
    half, third = width // 2, width // 4

    def plain(sums):
        sides = []
        for side in range(2):
            at = {}
            for i in (side, side + 2):
                for j, q in enumerate(QUARTERS[i]):
                    at[q] = sums[i][j * third : (j + 1) * third]
            x = jnp.concatenate([at[q] for q in range(4)], axis=0)
            x = flip_by(x.reshape((chips, cols) + x.shape[1:]), d, chips)
            x = x[order].reshape((width,) + x.shape[2:])
            sides.append(
                scatter_sum(x, groups, lambda v: to_wire(v, width), lambda v: from_wire(v, width))
            )
        return sides

    if not relative:
        expand_grad = jnp.concatenate(plain([widen(x) for x in (ea, eb, ec, ed)]), axis=1)
        side_a, side_b = plain(q_sums)
        small = side_b[:, width : width + 8].T
        last = jnp.where(
            t == 0, small[3], lax.dynamic_slice_in_dim(rbias[0], d * cols, cols, 0)
        )
        return (
            loss.reshape(1), temp.reshape(1), grad_tokens, small[0:1], jnp.stack([small[1], small[2], last]),
            small[4:6].reshape(2 * cols),
            jnp.concatenate([side_a[:, half:], side_b[:, :width]], axis=1), side_a[:, :half],
            expand_grad, reduce_grad,
        )

    def second_hops(side_a, side_b, stacked, name):
        count = len(side_a)
        shapes = [x.shape[-2:] for x in (*side_a, *side_b)]
        small = shapes[-1][1] - width
        kept_a, kept_b, next_a, next_b = call(
            partial(turn_kernel, width, stacked, count), name, [ANY] * (2 * count),
            [((third, width), F32), ((third, width + small // 2), F32),
             ((third, width), BF16), ((third, width + small), BF16)],
            [VMEM] * 4, [vm(x, BF16) for x in shapes] + [sem((2 * count,))],
            (*side_a, *side_b), 1_000_000, 4_000_000,
        )
        return kept_a, kept_b, xor_permute(next_a, "dp", 2), xor_permute(next_b, "dp", 1)

    def merge(parts, after, name):
        f32_cols = parts[0].shape[1] + parts[1].shape[1]
        bf_cols = parts[2].shape[1] + parts[3].shape[1]
        return call(
            partial(merge_kernel, width), name, [VMEM] * 4 + [ANY] * len(after),
            [((cols, f32_cols), F32)] + [((cols, bf_cols), BF16)] * 3, [VMEM] * 4, [],
            (*parts, *after), 1_000_000, 3_000_000,
        )

    def z_hops(pieces):
        return [xor_permute(x, "dp", r) for x, r in zip(pieces, reaches(groups[0])[1:])]

    e_own, *e_far = merge(e_parts, (wire_b,), "merge_expand")
    e_back = z_hops(e_far)
    expand_grad = e_own + sum(widen(x) for x in e_back)
    q_parts = second_hops(
        (qa_keep, qa_back, q_hops[0]), (qb_keep, qb_back, q_hops[1]), 2, "turn_qkv"
    )
    q_own, *q_far = merge(q_parts, e_back, "merge_qkv")
    q_in = z_hops(q_far)
    qkv_grad, project_grad, gains_grad, biases_grad, hid_rows = call(
        partial(finish_kernel, width), "finish", [SMEM] + [VMEM] * 5,
        [((cols, 3 * half), F32), ((cols, half), F32), ((1, cols), F32), ((3, cols), F32),
         ((1, 2 * cols), F32)],
        [VMEM] * 5, [], (scal, q_own, *q_in, rbias), 1_000_000, 2_000_000,
    )
    return (
        loss.reshape(1), temp.reshape(1), grad_tokens, gains_grad, biases_grad, hid_rows.reshape(2 * cols),
        qkv_grad, project_grad, expand_grad, reduce_grad,
    )


def solution(mesh):
    in_specs = (P("dp", None, None), P("dp", None, None), P("dp")) + (P(),) * 15
    out_specs = (
        P(), P(), P("dp", "tower", None), P("tower", "dp"), P("tower", "dp"),
        P(("tower", "dp")), P("dp", "tower"), P("dp", "tower"), P("dp", "tower"),
        P(("tower", "dp"), None),
    )
    return jax.shard_map(body, mesh=mesh, in_specs=in_specs, out_specs=out_specs, check_vma=False)
```

```python
import math
from functools import partial

import jax
import jax.numpy as jnp
import numpy as np
from jax import lax
from jax.experimental import pallas as pl
from jax.experimental.pallas import tpu as pltpu
from jax.sharding import PartitionSpec as P

F32 = jnp.float32
BF16 = jnp.bfloat16
HEAD_DIM = 64
LANES = 128
EXTRA = 120
norm_eps = 1e-06
embed_eps = 1e-06
NEG = -1000000000.0
VMEM_LIMIT = 60 * 1024 * 1024
MARGIN = 8 * 1024 * 1024
SMALL = ("merge_expand", "merge_qkv", "finish", "reduce_grad")


def normal_cdf(x):
    return 0.5 + 0.5 * lax.erf(x * 0.7071067811865476)


def load(src, dst, sem):
    copy = pltpu.make_async_copy(src, dst, sem)
    copy.start()
    return copy


def dot(a, b):
    return jnp.dot(a, b, preferred_element_type=F32)


def dot_nt(a, b):
    return lax.dot_general(a, b, (((1,), (1,)), ((), ())), preferred_element_type=F32)


def dot_tn(a, b):
    return lax.dot_general(a, b, (((0,), (0,)), ((), ())), preferred_element_type=F32)


def norm_stats(x):
    mean = jnp.mean(x, axis=-1, keepdims=True)
    centered = x - mean
    rstd = lax.rsqrt(jnp.mean(centered * centered, axis=-1, keepdims=True) + norm_eps)
    return centered * rstd, rstd


def norm_back(dxhat, xhat, rstd):
    return rstd * (
        dxhat
        - jnp.mean(dxhat, axis=-1, keepdims=True)
        - xhat * jnp.mean(dxhat * xhat, axis=-1, keepdims=True)
    )


def row(ref, i):
    return ref[i : i + 1, :].astype(F32)


def head_masks():
    lane = lax.broadcasted_iota(jnp.int32, (1, LANES), 1)
    first = (lane < HEAD_DIM).astype(BF16)
    return first, (1 - first).astype(BF16)


def set_qkv_bias(out, biases):
    width = biases.shape[1]
    out[:, :width] = row(biases, 2)
    out[:, width : 2 * width] = jnp.zeros((1, width), F32)
    out[:, 2 * width :] = row(biases, 3)


def set_hidden_bias(out, hid):
    lines = hid[...].astype(F32)
    for i in range(hid.shape[0]):
        out[:, i * LANES : (i + 1) * LANES] = lines[i : i + 1]


def two_heads(x, masks):
    return jnp.concatenate([x * masks[0], x * masks[1]], axis=0)


def softmax_parts(scores, bias):
    keys = scores.shape[1] // 2
    parts = []
    for e in range(2):
        s = scores[:, e * keys : (e + 1) * keys] + bias
        parts.append(jnp.exp(s - jnp.max(s, axis=-1, keepdims=True)))
    return parts


def attend(q2, k2, v2, bias, masks):
    e0, e1 = softmax_parts(dot_nt(q2 * BF16(0.125), two_heads(k2, masks)), bias)
    weights = jnp.concatenate([e0.astype(BF16), e1.astype(BF16)], axis=1)
    ones = jnp.ones((k2.shape[0], LANES), BF16)
    right = jnp.concatenate([two_heads(v2, masks), two_heads(ones, masks)], axis=1)
    out = dot(weights, right)
    return (out[:, :LANES] / out[:, LANES:]).astype(BF16)


def split_dot(x, w):
    hi = x.astype(BF16)
    lo = (x - hi.astype(F32)).astype(BF16)
    n = x.shape[0]
    out = dot(jnp.concatenate([hi, lo], axis=0), w)
    return out[:n] + out[n:]


def text_forward_kernel(
    scal, h_any, gains, biases, hid, wq_any, wp_any, we_any, wr_any,
    a_any, qkv_any, o_any, m_any, c_any, gpk_any, gps_any, send_out, emb_out, r_out,
    h_v, wq, wp, we, wr, qb, hb, av, cv, gsum, a_out, qkv_out, o_out, m_out, c_out, gp_keep, gp_send,
    sems, out_sems,
):
    n, width = m_out.shape
    caps = emb_out.shape[0]
    length = n // caps
    hidden = hid.shape[0] * LANES
    t, d = scal[0], scal[1]
    load_h = load(h_any.at[pl.ds(pl.multiple_of(t * n, n), n)], h_v, sems.at[0])
    load_q = load(wq_any, wq, sems.at[1])
    load_h.wait()
    masks = head_masks()

    def put_transposed(out, src):
        count, rows = out.shape[:2]

        def turn(i, carry):
            lanes = pl.ds(pl.multiple_of(i * (width // 2), LANES), width // 2)
            turned = src[:, lanes].astype(F32).T.astype(BF16)
            for e in range(count // 2):
                out[scal[4 + i * (count // 2) + e]] = turned[e * rows : (e + 1) * rows, :]
            return carry

        lax.fori_loop(0, 2, turn, 0, unroll=2)

    h = h_v[...].astype(F32)
    xhat, _ = norm_stats(h)
    a = xhat * row(gains, 0) + row(biases, 0)
    av[...] = a.astype(BF16)
    load_q.wait()
    load_p = load(wp_any, wp, sems.at[2])
    load_e = load(we_any, we, sems.at[3])
    load_r = load(wr_any, wr, sems.at[4])
    set_qkv_bias(qb, biases)
    set_hidden_bias(hb, hid)

    def to_qkv(j, carry):
        cols = pl.ds(pl.multiple_of(j * 256, 256), 256)
        qkv_out[:, cols] = (dot(av[...], wq[:, cols]) + qb[:, cols]).astype(BF16)
        return carry

    lax.fori_loop(0, 3 * width // 256, to_qkv, 0, unroll=9)
    put_transposed(a_out, av)
    stores = [load(qkv_out, qkv_any, out_sems.at[0]), load(a_out, a_any, out_sems.at[1])]
    same = (
        lax.broadcasted_iota(jnp.int32, (LANES, LANES), 0) // length
        == lax.broadcasted_iota(jnp.int32, (LANES, LANES), 1) // length
    )
    bias = jnp.where(same, 0.0, -1e30)

    def attention(g, carry):
        rows = pl.ds(pl.multiple_of(g * LANES, LANES), LANES)
        for p in range(width // LANES):
            lanes = slice(p * LANES, (p + 1) * LANES)
            q2 = qkv_out[rows, lanes]
            k2 = qkv_out[rows, width + p * LANES : width + (p + 1) * LANES]
            v2 = qkv_out[rows, 2 * width + p * LANES : 2 * width + (p + 1) * LANES]
            av[rows, lanes] = attend(q2, k2, v2, bias, masks)
        return carry

    lax.fori_loop(0, n // LANES, attention, 0)
    load_p.wait()
    m = h_v[...].astype(F32) + dot(av[...], wp[...]) + row(biases, 4)
    m_out[...] = m
    stores.append(load(m_out, m_any, out_sems.at[2]))
    xhat, _ = norm_stats(m)
    c = xhat * row(gains, 1) + row(biases, 1)
    cv[...] = c.astype(BF16)
    put_transposed(c_out, cv)
    put_transposed(o_out, av)
    stores.append(load(c_out, c_any, out_sems.at[3]))
    stores.append(load(o_out, o_any, out_sems.at[4]))
    load_e.wait()
    half = hidden // 512

    def feed(rel, gp_out):
        def step(j, carry):
            local = pl.ds(pl.multiple_of(j * 256, 256), 256)
            at = jnp.bitwise_xor(t, rel) * half + j
            cols = pl.ds(pl.multiple_of(at * 256, 256), 256)
            f = dot(cv[...], we[:, cols]) + hb[:, cols]
            cdf = normal_cdf(f)
            density = jnp.exp(f * f * -0.5) * 0.3989422804014327
            gp_out[:, local] = (cdf + f * density).astype(BF16)
            gsum[:, cols] = jnp.sum((f * cdf).reshape(caps, length, 256), axis=1)
            return carry

        lax.fori_loop(0, half, step, 0, unroll=2)

    feed(1, gp_send)
    stores.append(load(gp_send, gps_any, out_sems.at[5]))
    feed(0, gp_keep)
    stores.append(load(gp_keep, gpk_any, out_sems.at[6]))
    load_r.wait()
    total = gsum[...]
    pooled = (
        jnp.mean(m_out[...].reshape(caps, length, width), axis=1)
        + split_dot(total * (1.0 / length), wr[...])
        + row(biases, 5)
    )
    r = lax.rsqrt(jnp.sum(pooled * pooled, axis=-1, keepdims=True) + embed_eps)
    emb_out[...] = pooled * r
    r_out[...] = jnp.broadcast_to(r, r_out.shape)
    chips = send_out.shape[0]
    share = hidden // (2 * chips)
    scaled = total * r
    hi = r.astype(BF16).astype(F32)
    mid = (r - hi).astype(BF16).astype(F32)
    slot = lax.broadcasted_iota(jnp.int32, (caps, LANES), 0) + t * caps
    lane = lax.broadcasted_iota(jnp.int32, (caps, LANES), 1)
    extra = jnp.where(lane == EXTRA, hi, 0.0)
    extra = jnp.where(lane == EXTRA + 1, mid, extra)
    extra = jnp.where(lane == EXTRA + 2, r - hi - mid, extra)
    extra = jnp.where((lane == EXTRA + 3) & (slot < scal[2]), 1.0, extra)
    for e in range(chips):
        send_out[e, :, :width] = (pooled * r).astype(BF16)
        for half_at in range(2):
            src = (half_at * chips + e) * share
            piece = jnp.concatenate([scaled[:, src : src + share], extra[:, share:]], axis=1)
            to = width + jnp.bitwise_xor(t, half_at) * LANES
            send_out[e, :, pl.ds(pl.multiple_of(to, LANES), LANES)] = piece.astype(BF16)
    for c in stores:
        c.wait()


PAD = 56


def image_forward_kernel(
    scal, x_any, gains, biases, hid, wq_any, wp_any, we_any, wr_any,
    out,
    x_v, xs, hv, av, qkv, mv, msum, gsum, wq, wp, we, wr, qb, hb, pb, sems,
):
    length, both_caps, width = x_v.shape
    caps = both_caps // 2
    n = caps * PAD
    hidden = hid.shape[0] * LANES
    t = scal[0]
    load_x = load(x_any, x_v, sems.at[0])
    load_q = load(wq_any, wq, sems.at[1])
    masks = head_masks()
    qkv[n:, :] = jnp.zeros((qkv.shape[0] - n, 3 * width), BF16)
    first = (jnp.zeros((1, 1), jnp.int32) + t) == 0
    load_x.wait()

    def pick(i, carry):
        x = x_v[i].astype(F32)
        x = jnp.where(first, x[:caps], x[caps:])
        for k in range(width // LANES):
            xs[k, pl.ds(pl.multiple_of(i * caps, 8), caps), :] = x[:, k * LANES : (k + 1) * LANES]
        return carry

    lax.fori_loop(0, length, pick, 0, unroll=2)

    def first_norm(j, carry):
        base = pl.multiple_of(j * 2 * PAD, 16)
        for e in range(2):
            x = jnp.concatenate(
                [
                    xs[k, pl.ds(j * 2 + e, length, stride=caps), :]
                    for k in range(width // LANES)
                ],
                axis=1,
            )
            x = jnp.concatenate([x, jnp.zeros((PAD - length, width), F32)], axis=0)
            hv[pl.ds(base + e * PAD, PAD), :] = x
            xhat, _ = norm_stats(x)
            x = xhat * row(gains, 0) + row(biases, 0)
            if e == 0:
                kept = x
        av[pl.ds(base, 2 * PAD), :] = jnp.concatenate([kept, x], axis=0).astype(BF16)
        return carry

    lax.fori_loop(0, caps // 2, first_norm, 0, unroll=4)
    load_q.wait()
    load_p = load(wp_any, wp, sems.at[2])
    load_e = load(we_any, we, sems.at[3])
    load_r = load(wr_any, wr, sems.at[4])
    set_qkv_bias(qb, biases)
    set_hidden_bias(hb, hid)

    def to_qkv(j, carry):
        cols = pl.ds(pl.multiple_of(j * 256, 256), 256)
        qkv[:n, cols] = (dot(av[...], wq[:, cols]) + qb[:, cols]).astype(BF16)
        return carry

    lax.fori_loop(0, 3 * width // 256, to_qkv, 0, unroll=9)
    q_at = lax.broadcasted_iota(jnp.int32, (2 * PAD, LANES), 0)
    k_at = lax.broadcasted_iota(jnp.int32, (2 * PAD, LANES), 1)
    low = (q_at < PAD) & (k_at < length)
    high = (q_at >= PAD) & (k_at >= PAD) & (k_at < PAD + length)
    bias = jnp.where(low | high, 0.0, -1e30)

    def attention(j, carry):
        base = pl.multiple_of(j * 2 * PAD, 16)
        rows, keys = pl.ds(base, 2 * PAD), pl.ds(base, LANES)
        for p in range(width // LANES):
            lanes = slice(p * LANES, (p + 1) * LANES)
            q2 = qkv[rows, lanes]
            k2 = qkv[keys, width + p * LANES : width + (p + 1) * LANES]
            v2 = qkv[keys, 2 * width + p * LANES : 2 * width + (p + 1) * LANES]
            av[rows, lanes] = attend(q2, k2, v2, bias, masks)
        return carry

    lax.fori_loop(0, caps // 2, attention, 0, unroll=4)
    load_p.wait()
    pb[...] = row(biases, 4)

    def add_attended(j, carry):
        cols = pl.ds(pl.multiple_of(j * 256, 256), 256)
        mv[:, cols] = hv[:, cols] + dot(av[...], wp[:, cols]) + pb[:, cols]
        return carry

    lax.fori_loop(0, width // 256, add_attended, 0, unroll=3)
    group = 8 * PAD
    tail = (lax.broadcasted_iota(jnp.int32, (1, 8, 1), 1) < length - (PAD - 8)).astype(F32)

    def token_sum(x, count):
        tiles = x.reshape(count, PAD // 8, 8, x.shape[1])
        acc = tiles[:, PAD // 8 - 1] * tail
        for i in range(PAD // 8 - 1):
            acc = acc + tiles[:, i]
        return jnp.sum(acc, axis=1)

    def second_norm(j, carry):
        rows = pl.ds(pl.multiple_of(j * group, 16), group)
        m = mv[rows, :]
        xhat, _ = norm_stats(m)
        av[rows, :] = (xhat * row(gains, 1) + row(biases, 1)).astype(BF16)
        msum[pl.ds(pl.multiple_of(j * 8, 8), 8), :] = token_sum(m, 8)
        return carry

    lax.fori_loop(0, caps // 8, second_norm, 0, unroll=3)
    load_e.wait()

    def feed(j, carry):
        cols = pl.ds(pl.multiple_of(j * 256, 256), 256)
        f = dot(av[...], we[:, cols]) + hb[:, cols]
        gsum[:, cols] = token_sum(f * normal_cdf(f), caps)
        return carry

    lax.fori_loop(0, hidden // 256, feed, 0, unroll=3)
    load_r.wait()
    scale = 1.0 / length
    pooled = msum[...] * scale + split_dot(gsum[...] * scale, wr[...]) + row(biases, 5)
    r_img = lax.rsqrt(jnp.sum(pooled * pooled, axis=-1, keepdims=True) + embed_eps)
    out[...] = (pooled * r_img).astype(BF16)


QUARTERS = ((1, 3), (2, 3), (0, 2), (0, 1))


def loss_kernel(
    rows_block, parts, scal, *refs,
):
    own_any, refs = refs[:parts], refs[parts:]
    (par_any, text_any, text_par_any, expo, emb, r, gpk_any, gpr_any, ct_any, ctr_any,
     we_any, wr_any,
     loss_out, temp_out, ea, eb, ec, ed, g_any, images_any, texts_any, gall_any, extra_any,
     dc_any, dy_out, hid_out,
     own_v, par_v, text_v, text_par_v, texts, images, extra, gall, col_flag, sims, grad,
     chip_g, gpk, gpr, ct, we, wr, dc, exp_s, sems, out_sems) = refs
    chips, caps, width = par_any.shape
    staged = own_v.shape[0] == chips
    total = texts.shape[0]
    near_hidden = gpk.shape[1]
    n = dc.shape[0]
    length = n // caps
    t, d = scal[0], scal[1]
    first = (jnp.zeros((1, 1), jnp.int32) + t) == 0
    if staged:
        each = chips // parts
        waits = [
            load(par_any, par_v, sems.at[0]),
            load(text_any, text_v, sems.at[1]),
            load(text_par_any, text_par_v, sems.at[2]),
        ] + [
            load(own_any[i], own_v.at[pl.ds(i * each, each)], sems.at[3 + i]) for i in range(parts)
        ]
        for c in waits:
            c.wait()

    def place(e, carry):
        at, slot = e, scal[4 + 16 + e]
        if not staged:
            waits = [
                load(src.at[pl.ds(i, 1)], dst, sems.at[j])
                for j, (src, i, dst) in enumerate(
                    ((own_any[0], slot, own_v), (par_any, slot, par_v), (text_any, at, text_v),
                     (text_par_any, at, text_par_v))
                )
            ]
            for c in waits:
                c.wait()
            at = slot = 0

        def pair(x0, x1):
            x0, x1 = x0.astype(F32), x1.astype(F32)
            return jnp.concatenate([jnp.where(first, x0, x1), jnp.where(first, x1, x0)], axis=0)

        rows = pl.ds(pl.multiple_of(e * 2 * caps, 16), 2 * caps)
        images[rows, :] = pair(own_v[slot], par_v[slot]).astype(BF16)
        x0, x1 = text_v[at], text_par_v[at]
        texts[rows, :] = pair(x0[:, :width], x1[:, :width]).astype(BF16)
        last = pair(x0[:, width : width + LANES], x1[:, width + LANES :])
        extra[rows, :] = last
        gall[rows, :] = last.astype(BF16)
        return carry

    lax.fori_loop(0, chips, place, 0, unroll=2)
    half = near_hidden // 256
    later = [
        load(src, dst, sems.at[8 + i])
        for i, (src, dst) in enumerate(
            ((wr_any.at[pl.ds(pl.multiple_of(t * near_hidden, 256), near_hidden)], wr),
             (gpk_any, gpk), (gpr_any, gpr),
             (we_any.at[:, pl.ds(pl.multiple_of(t * near_hidden, 256), near_hidden)], we))
        )
    ]
    for i, src in enumerate((ct_any, ctr_any)):
        later.append(load(src, ct.at[i], sems.at[12 + i]))
    stores = [
        load(src, dst, out_sems.at[i])
        for i, (src, dst) in enumerate(
            ((images, images_any), (texts, texts_any), (gall, gall_any), (extra, extra_any))
        )
    ]
    pick = (lax.broadcasted_iota(jnp.int32, (8, LANES), 1) == EXTRA + 3).astype(F32)
    step = min(256, total)

    def flags(j, carry):
        cols = pl.ds(pl.multiple_of(j * step, step), step)
        col_flag[:, cols] = dot_nt(pick, extra[cols, :])
        return carry

    lax.fori_loop(0, total // step, flags, 0)
    scale = jnp.exp(jnp.full((1, 1), expo[0], F32))
    chunk = 48
    blocks = total // rows_block
    per_block = rows_block // chunk
    live = col_flag[0:1, :]

    def similarities(b):
        base = pl.multiple_of(b * rows_block, 16)

        def cols_step(j, carry):
            cols = pl.ds(pl.multiple_of(j * step, step), step)
            sims[:, cols] = scale * dot_nt(texts[pl.ds(base, rows_block), :], images[cols, :])
            return carry

        lax.fori_loop(0, total // step, cols_step, 0)

    def chunk_at(b, i):
        local = pl.ds(pl.multiple_of(i * chunk, 16), chunk)
        whole = pl.ds(pl.multiple_of(b * rows_block + i * chunk, 16), chunk)
        return local, whole

    def column_block(b, acc):
        similarities(b)

        def adding(i, acc):
            local, whole = chunk_at(b, i)
            live_row = extra[whole, EXTRA + 3 : EXTRA + 4]
            part = jnp.exp(sims[local, :]) * live_row
            return acc + jnp.sum(part.reshape(chunk // 8, 8, total), axis=0)

        return lax.fori_loop(0, per_block, adding, acc, unroll=2)

    col_acc = jnp.zeros((8, total), F32)
    if blocks == 1:
        col_acc = column_block(0, col_acc)
    else:
        col_acc = lax.fori_loop(0, blocks, column_block, col_acc)
    col_sum = jnp.sum(col_acc, axis=0, keepdims=True)
    col_part = 0.5 * live / col_sum

    def row_block(b, carry):
        if blocks > 1:
            similarities(b)

        def rows_step(i, acc):
            loss, temp, diag = acc
            local, whole = chunk_at(b, i)
            s = sims[local, :]
            flag = extra[whole, EXTRA + 3 : EXTRA + 4]
            at = lax.broadcasted_iota(jnp.int32, (chunk, total), 0) + (b * rows_block + i * chunk)
            eye = at == lax.broadcasted_iota(jnp.int32, (chunk, total), 1)
            expd = jnp.exp(s)
            rsum = jnp.sum(expd * live, axis=1, keepdims=True)
            g = expd * ((0.5 * flag / rsum) * live + flag * col_part)
            g = g - jnp.where(eye, 0.5 * (flag + live), 0.0)
            grad[local, :] = g.astype(BF16)
            temp = temp + jnp.sum((g * s).reshape(chunk // 8, 8, total), axis=0)
            diag = diag + jnp.sum(
                jnp.where(eye, s * flag, 0.0).reshape(chunk // 8, 8, total), axis=0
            )
            return loss + 0.5 * flag * jnp.log(rsum), temp, diag

        carry = lax.fori_loop(0, per_block, rows_step, carry, unroll=2)
        mine = d * (2 * caps) - b * rows_block

        @pl.when((mine >= 0) & (mine < rows_block))
        def _():
            chip_g[...] = grad[pl.ds(pl.multiple_of(mine, 16), 2 * caps), :]

        if blocks > 1:
            rows = pl.ds(pl.multiple_of(b * rows_block, 16), rows_block)
            load(grad, g_any.at[rows], out_sems.at[4]).wait()
        return carry

    start = (jnp.zeros((chunk, 1), F32), jnp.zeros((8, total), F32), jnp.zeros((8, total), F32))
    if blocks == 1:
        loss, temp, diag = row_block(0, start)
        stores.append(load(grad, g_any, out_sems.at[4]))
    else:
        loss, temp, diag = lax.fori_loop(0, blocks, row_block, start)
    def whole(x):
        return jnp.sum(jnp.sum(x, axis=0, keepdims=True), axis=1, keepdims=True)

    objective = whole(loss) + 0.5 * whole(live * jnp.log(col_sum)) - whole(diag)
    loss_out[...] = objective / whole(live)
    temp_out[...] = whole(temp)

    both_dt = scale * dot(chip_g[...], images[...])
    chip = pl.ds(pl.multiple_of(d * 2 * caps, 16), 2 * caps)
    inv = jnp.sum(extra[chip, EXTRA : EXTRA + 3], axis=1, keepdims=True)
    dt = jnp.where(first, both_dt[:caps], both_dt[caps:])
    dt_far = jnp.where(first, both_dt[caps:], both_dt[:caps])
    both_tx = texts[chip, :].astype(F32)
    tx_far = jnp.where(first, both_tx[caps:], both_tx[:caps])
    inv_far = jnp.where(first, inv[caps:], inv[:caps])

    def pooled_back(tx, dt, inv):
        return inv * (dt - tx * jnp.sum(tx * dt, axis=1, keepdims=True)) * (1.0 / length)

    dy = pooled_back(emb[...], dt, r[:, 0:1])
    dy_out[...] = dy
    dyb = jnp.concatenate([dy, pooled_back(tx_far, dt_far, inv_far)], axis=0).astype(BF16)
    for c in later:
        c.wait()
    dc[...] = jnp.zeros_like(dc)

    def near(j, carry):
        cols = pl.ds(pl.multiple_of(j * 256, 256), 256)
        dg = dot_nt(dyb, wr[cols, :])
        df = (gpk[:, cols].astype(F32).reshape(caps, length, 256) * dg[:caps][:, None, :]).reshape(
            n, 256
        )
        far = (gpr[:, cols].astype(F32).reshape(caps, length, 256) * dg[caps:][:, None, :]).reshape(
            n, 256
        )
        df, far = df.astype(BF16), far.astype(BF16)
        hid_out[0:1, cols] = jnp.sum(df.astype(F32) + far.astype(F32), axis=0, keepdims=True)
        dc[...] += dot_nt(df, we[:, cols])
        side = near_hidden // 512
        local = pl.ds(pl.multiple_of((j % side) * 256, 256), 256)
        exp_s[j // side, :, local] = (
            dot(ct[0].reshape(width, n), df) + dot(ct[1].reshape(width, n), far)
        ).astype(BF16)
        return carry

    lax.fori_loop(0, half, near, 0, unroll=2)
    quarter = width // 4
    for i, out in enumerate((ea, eb, ec, ed)):
        for j, q in enumerate(QUARTERS[i]):
            stores.append(
                load(
                    exp_s.at[i % 2, pl.ds(q * quarter, quarter)],
                    out.at[pl.ds(j * quarter, quarter)],
                    out_sems.at[5 + 2 * i + j],
                )
            )
    stores.append(load(dc, dc_any, out_sems.at[13]))
    for c in stores:
        c.wait()


def middle_back_kernel(
    scal, dc_any, dy, gps_any, m_any, gains, we_any, wr_any, wp_any, qkv_any,
    dm_any, dqkv_any, vec_out,
    dc, gps, mv, we, wr, wp, qkv, dm, dmb, dov, dqkv, sems,
):
    n, width = dm.shape
    caps = dy.shape[0]
    length = n // caps
    far_hidden = gps.shape[1]
    t = scal[0]
    away = pl.ds(pl.multiple_of((1 - t) * far_hidden, 256), far_hidden)
    half = far_hidden // 512
    parts = []
    for i in range(2):
        at = pl.ds(pl.multiple_of(((1 - t) * 2 + i) * half * 256, 256), half * 256)
        here = pl.ds(i * half * 256, half * 256)
        parts.append([
            load(wr_any.at[at], wr.at[here], sems.at[3 * i]),
            load(gps_any.at[:, here], gps.at[:, here], sems.at[3 * i + 1]),
            load(we_any.at[:, at], we.at[:, here], sems.at[3 * i + 2]),
        ])
        if i == 0:
            load_dc = load(dc_any, dc, sems.at[9])
    for c in parts[0]:
        c.wait()
    load_dc.wait()
    load_m = load(m_any, mv, sems.at[10])
    load_p = load(wp_any, wp, sems.at[11])
    load_qkv = load(qkv_any, qkv, sems.at[6])
    dyv = dy[...]
    dyb = dyv.astype(BF16)

    def feed(j, carry):
        cols = pl.ds(pl.multiple_of(j * 256, 256), 256)
        dg = dot_nt(dyb, wr[cols, :])
        df = gps[:, cols].astype(F32).reshape(caps, length, 256) * dg[:, None, :]
        dc[...] += dot_nt(df.reshape(n, 256).astype(BF16), we[:, cols])
        return carry

    lax.fori_loop(0, half, feed, 0, unroll=3)
    for c in parts[1]:
        c.wait()
    lax.fori_loop(half, 2 * half, feed, 0, unroll=3)
    load_m.wait()
    piece = 8 * length

    def norm(i, sums):
        rows = pl.ds(pl.multiple_of(i * piece, piece), piece)
        xhat, rstd = norm_stats(mv[rows, :])
        dcv = dc[rows, :]
        back = norm_back(dcv * row(gains, 1), xhat, rstd)
        dy_rows = dy[pl.ds(pl.multiple_of(i * 8, 8), 8), :]
        out = (back.reshape(piece // length, length, width) + dy_rows[:, None, :]).reshape(
            piece, width
        )
        dm[rows, :] = out
        low = out.astype(BF16)
        dmb[rows, :] = low

        def fold(x):
            return jnp.sum(x.reshape(piece // 8, 8, width), axis=0)

        return sums[0] + fold(dcv * xhat), sums[1] + fold(dcv), sums[2] + fold(low.astype(F32))

    blank = jnp.zeros((8, width), F32)
    sums = lax.fori_loop(0, n // piece, norm, (blank, blank, blank))
    store_dm = load(dm, dm_any, sems.at[7])
    load_p.wait()
    dov[...] = dot_nt(dmb[...], wp[...]).astype(BF16)
    load_qkv.wait()
    masks = head_masks()
    same = (
        lax.broadcasted_iota(jnp.int32, (LANES, LANES), 0) // length
        == lax.broadcasted_iota(jnp.int32, (LANES, LANES), 1) // length
    )
    bias = jnp.where(same, 0.0, -1e30)

    def attention(g, carry):
        rows = pl.ds(pl.multiple_of(g * LANES, LANES), LANES)
        for p in range(width // LANES):
            lanes = slice(p * LANES, (p + 1) * LANES)
            k_lanes = slice(width + p * LANES, width + (p + 1) * LANES)
            v_lanes = slice(2 * width + p * LANES, 2 * width + (p + 1) * LANES)
            q2 = qkv[rows, lanes] * BF16(0.125)
            km = two_heads(qkv[rows, k_lanes], masks)
            vm = two_heads(qkv[rows, v_lanes], masks)
            do2 = dov[rows, lanes]
            parts = softmax_parts(dot_nt(q2, km), bias)
            dp = dot_nt(do2, vm)
            pb, ds = [], []
            for e in range(2):
                prob = parts[e] * (1.0 / jnp.sum(parts[e], axis=-1, keepdims=True))
                dpe = dp[:, e * LANES : (e + 1) * LANES]
                inner = jnp.sum(prob * dpe, axis=-1, keepdims=True)
                pb.append(prob.astype(BF16))
                ds.append((prob * (dpe - inner)).astype(BF16))
            dqkv[rows, lanes] = (dot(jnp.concatenate(ds, axis=1), km) * 0.125).astype(BF16)
            dqkv[rows, k_lanes] = dot_tn(jnp.concatenate(ds, axis=0), two_heads(q2, masks)).astype(
                BF16
            )
            dqkv[rows, v_lanes] = dot_tn(
                jnp.concatenate(pb, axis=0), two_heads(do2, masks)
            ).astype(BF16)
        return carry

    lax.fori_loop(0, n // LANES, attention, 0)
    store = load(dqkv, dqkv_any, sems.at[8])
    for i in range(3):
        vec_out[i : i + 1, :] = jnp.sum(sums[i], axis=0, keepdims=True)
    vec_out[3:4, :] = jnp.sum(dqkv[:, :width].astype(F32), axis=0, keepdims=True)
    vec_out[4:5, :] = jnp.sum(dqkv[:, 2 * width :].astype(F32), axis=0, keepdims=True)
    vec_out[5:8, :] = jnp.zeros((3, width), F32)
    store_dm.wait()
    store.wait()


def weight_grad_kernel(with_hid, scal, dm_any, dqkv_any, at_any, ot_any, wq_any, gains, biases, vec,
                       hid, *rest):
    turn, rest = (rest[:4], rest[4:]) if with_hid else ((), rest)
    keep_a, keep_b, send_a, send_b = rest[:4]
    turned, rest = (rest[4:8], rest[8:]) if with_hid else ((), rest[4:])
    dm, at, ot, dmb, dqkv, wq, grads, tails, inner_v, small, sems, store_sems = rest[:12]
    held, turn_sems = rest[12:16], rest[16:]
    n, width = dm.shape
    t = scal[0]
    load_dm = load(dm_any, dm, sems.at[0])
    load_o = load(ot_any, ot, sems.at[1])
    load_qkv = load(dqkv_any, dqkv, sems.at[2])
    load_a = load(at_any, at, sems.at[3])
    blocks, block = at.shape[:2]
    load_dm.wait()
    dmb[...] = dm[...].astype(BF16)
    load_o.wait()
    loads_w = [
        load(wq_any.at[pl.ds(e * block, block)], wq.at[scal[4 + e]], sems.at[8 + e])
        for e in range(blocks)
    ]
    half, quarter = width // 2, width // 4

    def project(hh, carry):
        cols = pl.ds(pl.multiple_of(hh * half, LANES), half)
        grads[hh, 0] = dot(ot[...].reshape(width, n), dmb[:, cols]).astype(BF16)
        return carry

    lax.fori_loop(0, 2, project, 0)
    load_qkv.wait()
    load_a.wait()
    for c in loads_w:
        c.wait()
    inner_v[...] = jnp.zeros_like(inner_v)

    def attend_in(c, carry):
        cols = pl.ds(pl.multiple_of(c * half, LANES), half)
        value = dot(at[...].reshape(width, n), dqkv[:, cols])
        grads[c // 3, 1 + c % 3] = value.astype(BF16)
        prod = value * wq[:, :, cols].reshape(width, half).astype(F32)
        acc = inner_v[...]
        for k in range(half // LANES):
            acc = acc + prod[:, k * LANES : (k + 1) * LANES]
        inner_v[...] = acc
        return carry

    loads_t = [load(src, dst, turn_sems[0].at[i]) for i, (src, dst) in enumerate(zip(turn, held))]
    lax.fori_loop(0, 6, attend_in, 0, unroll=2)

    def move(src, out, side, lanes, slot):
        return [
            load(
                src.at[pl.ds(q * quarter, quarter)],
                out.at[i, pl.ds(j * quarter, quarter), pl.ds(lanes, src.shape[1])],
                store_sems.at[slot + 2 * i + j],
            )
            for i in range(2)
            for j, q in enumerate(QUARTERS[side + 2 * i])
        ]

    stores = []
    for k, (hh, out_a, out_b) in enumerate(((1 - t, send_a, send_b), (t, keep_a, keep_b))):
        for part in range(4):
            out = (out_a, out_b)[part // 2]
            stores += move(grads.at[hh, part], out, part // 2, (part % 2) * half, 20 * k + 4 * part)
    for c in loads_t:
        c.wait()
    for side in range(len(turned) // 2):
        total = held[2 * side][...].astype(F32) + held[2 * side + 1][...].astype(F32)
        turned[side][...] = total[:quarter]
        turned[2 + side][...] = total[quarter:].astype(BF16)
    inner = inner_v[...]
    inner = jnp.sum(inner, axis=1, keepdims=True)
    sums = jnp.sum(dqkv[...].astype(F32), axis=0, keepdims=True)
    hi = sums.astype(BF16)
    lo = (sums - hi.astype(F32)).astype(BF16)
    both = jnp.concatenate([hi, lo, jnp.zeros((14, 3 * width), BF16)], axis=0)
    shift1 = dot_nt(wq[...].reshape(width, 3 * width), both)
    shift1 = shift1[:, 0:1] + shift1[:, 1:2]
    first = (jnp.zeros((1, 1), jnp.int32) + t) == 0
    zero = jnp.zeros((1, width), F32)
    for_zero = jnp.concatenate([zero, zero, vec[1:2, :], vec[3:4, :], zero, zero], axis=0)
    for_one = jnp.concatenate([vec[0:1, :], vec[4:5, :], vec[2:3, :], zero, zero, zero], axis=0)
    ends = jnp.concatenate([1.0 / row(gains, 0), row(biases, 0)], axis=0)
    lines = jnp.concatenate([for_zero, ends, for_one, ends], axis=0).T
    lane = lax.broadcasted_iota(jnp.int32, (1, 8), 1)
    if with_hid:
        columns = jnp.broadcast_to(hid[...], (8, hid.shape[1])).T
    for e in range(blocks):
        at_block = slice(e * block, (e + 1) * block)
        if with_hid:
            pick = columns[2 * e * block : (2 * e + 1) * block] * (lane == 4).astype(F32)
            pick = pick + columns[(2 * e + 1) * block : (2 * e + 2) * block] * (lane == 5).astype(F32)
        else:
            pick = jnp.zeros((block, 8), F32)
        small[scal[4 + e]] = jnp.concatenate(
            [lines[at_block, :8], lines[at_block, 8:], pick,
             jnp.zeros((block, LANES - 24), F32)], axis=1
        )
    sv = small[...].reshape(width, LANES)
    zeros_set, ones_set, own = sv[:, :8], sv[:, 8:16], sv[:, 16:24]
    gain1 = zeros_set[:, 6:7] * (inner - zeros_set[:, 7:8] * shift1)
    zeros_set = zeros_set + gain1 * (lane == 0).astype(F32) + shift1 * (lane == 1).astype(F32)
    used = (lane < 4).astype(F32)
    zeros_set, ones_set = zeros_set * used, ones_set * used
    keep_set = jnp.where(first, zeros_set, ones_set) + own
    send_set = jnp.where(first, ones_set, zeros_set)
    for hh in range(2):
        value = jnp.where((jnp.zeros((1, 1), jnp.int32) + t) == hh, keep_set, send_set)
        hi = value.astype(BF16).astype(F32)
        fill = jnp.zeros((width, LANES // 2 - 8), F32)
        tails[hh] = jnp.concatenate([hi, fill, value - hi, fill], axis=1).astype(BF16)
    stores += move(tails.at[1 - t], send_b, 1, width, 16)
    stores += move(tails.at[t], keep_b, 1, width, 36)
    for c in stores:
        c.wait()


def input_back_kernel(
    scal, dm_any, h_any, gains, dqkv_any, wq_any, order_any,
    tok_keep, tok_send,
    h_v, wq, dm, dqkv, da, sems,
):
    n, width = dm.shape
    caps, half_len, _ = tok_keep.shape
    t = scal[0]
    loads = [
        load(src, dst, sems.at[i])
        for i, (src, dst) in enumerate(
            ((dqkv_any, dqkv), (wq_any, wq),
             (h_any.at[pl.ds(pl.multiple_of(t * n, n), n)], h_v), (dm_any, dm))
        )
    ]
    loads[0].wait()
    loads[1].wait()

    def back(j, carry):
        rows = pl.ds(pl.multiple_of(j * 256, 256), 256)
        da[:, rows] = dot_nt(dqkv[...], wq[rows, :])
        return carry

    lax.fori_loop(0, width // 256, back, 0, unroll=3)
    loads[2].wait()
    loads[3].wait()
    piece = 8 * 2 * half_len
    first = (jnp.zeros((1, 1, 1), jnp.int32) + t) == 0

    def norm(i, carry):
        rows = pl.ds(pl.multiple_of(i * piece, piece), piece)
        xhat, rstd = norm_stats(h_v[rows, :].astype(F32))
        grad = dm[rows, :] + norm_back(da[rows, :] * row(gains, 0), xhat, rstd)
        halves = grad.reshape(8, 2, half_len, width)
        at = pl.ds(pl.multiple_of(i * 8, 8), 8)
        tok_keep[at] = jnp.where(first, halves[:, 0], halves[:, 1])
        tok_send[at] = jnp.where(first, halves[:, 1], halves[:, 0]).astype(BF16)
        return carry

    lax.fori_loop(0, n // piece, norm, 0)


def reduce_grad_kernel(
    rows_block, length, expo, g_any, images_any, texts_any, gall_any, extra_any, order_any,
    red_out, bias_out,
    g_v, images, texts, gall, extra, acc, sems,
):
    total, width = images.shape
    blocks = total // rows_block
    share = red_out.shape[0]
    whole = load(images_any, images, sems.at[0])
    scale = jnp.exp(jnp.full((1, 1), expo[0], F32))
    acc[...] = jnp.zeros_like(acc)
    whole.wait()

    def block(b, rb):
        rows = pl.ds(pl.multiple_of(b * rows_block, 16), rows_block)
        waits = [
            load(src.at[rows], dst, sems.at[1 + i])
            for i, (src, dst) in enumerate(
                ((g_any, g_v), (texts_any, texts), (gall_any, gall), (extra_any, extra))
            )
        ]
        for c in waits:
            c.wait()
        def project(i, rb):
            at = pl.ds(pl.multiple_of(i * 96, 96), 96)
            dt = scale * dot(g_v[at, :], images[...])
            tx = texts[at, :].astype(F32)
            part = (dt - tx * jnp.sum(tx * dt, axis=1, keepdims=True)) * (1.0 / length)
            part = part.astype(BF16)
            texts[at, :] = part
            inv = jnp.sum(extra[at, EXTRA : EXTRA + 3], axis=1, keepdims=True)
            return rb + jnp.sum(part.astype(F32) * inv, axis=0, keepdims=True)

        rb = lax.fori_loop(0, rows_block // 96, project, rb)
        acc[...] += dot_tn(gall[...], texts[...])
        return rb

    rb = lax.fori_loop(0, blocks, block, jnp.zeros((1, width), F32))
    red_out[...] = acc[:share, :]
    bias_out[...] = jnp.broadcast_to(rb * float(length), bias_out.shape)


def to_wire(x, width):
    low = x.astype(BF16)
    if x.shape[1] == width:
        return low
    rest = x[:, width:] - low[:, width:].astype(F32)
    return jnp.concatenate([low, rest.astype(BF16)], axis=1)


def from_wire(x, width):
    y = x.astype(F32)
    if x.shape[1] == width:
        return y
    return jnp.concatenate([y[:, :width], y[:, width : width + 64] + y[:, width + 64 :]], axis=1)


def wire_kernel(width, qa, qa_back, qb, qb_back, far_a, far_b, wire_a, wire_b, a0, a1, b0, b1,
                sems):
    loads = [
        load(src.at[0], dst, sems.at[i])
        for i, (src, dst) in enumerate(((qa, a0), (qa_back, a1), (qb, b0), (qb_back, b1)))
    ]
    loads[0].wait()
    loads[1].wait()
    wire_a[...] = (a0[...].astype(F32) + a1[...].astype(F32)).astype(BF16)
    loads[2].wait()
    loads[3].wait()
    wire_b[...] = to_wire(from_wire(b0[...], width) + from_wire(b1[...], width), width)


def turn_kernel(width, stacked, count, *refs):
    ins, (kept_a, kept_b, next_a, next_b) = refs[: 2 * count], refs[2 * count : 2 * count + 4]
    scratch, sems = refs[2 * count + 4 : -1], refs[-1]
    loads = [
        load(src.at[1] if i % count < stacked else src, dst, sems.at[i])
        for i, (src, dst) in enumerate(zip(ins, scratch))
    ]
    half = kept_a.shape[0]
    for side, (kept, moved) in enumerate(((kept_a, next_a), (kept_b, next_b))):
        at = range(side * count, (side + 1) * count)
        for i in at:
            loads[i].wait()
        total = from_wire(scratch[at[0]][...], width)
        for i in at[1:]:
            total = total + from_wire(scratch[i][...], width)
        kept[...] = total[:half]
        moved[...] = to_wire(total[half:], width)


def merge_kernel(width, sum_a, sum_b, hop_a, hop_b, *rest):
    outs = rest[-4:]
    for i, out in enumerate(outs):
        rows = out.shape[0]
        at = slice(i * rows, (i + 1) * rows)
        a = sum_a[at, :] + hop_a[at, :].astype(F32)
        b = sum_b[at, :] + from_wire(hop_b[at, :], width)
        if i == 0:
            out[:, :width] = a
            out[:, width:] = b
        else:
            out[:, :width] = a.astype(BF16)
            out[:, width:] = to_wire(b, width)


def finish_kernel(width, scal, total, hop_1, hop_2, hop_3, rbias,
                  qkv_out, project_out, gains_out, biases_out, hid_out):
    half = width // 2
    rows, cols = project_out.shape[0], width
    t, d = scal[0], scal[1]
    acc = total[...]
    for hop in (hop_1, hop_2, hop_3):
        x = hop[...]
        acc = acc + jnp.concatenate(
            [x[:, :width].astype(F32), from_wire(x[:, width:], width)], axis=1
        )
    project_out[...] = acc[:, :half]
    qkv_out[...] = acc[:, half : 2 * width]
    small = acc[:, 2 * width : 2 * width + 8].T
    lane = lax.broadcasted_iota(jnp.int32, (rows, cols), 1)
    mine = lax.broadcasted_iota(jnp.int32, (rows, cols), 0) + d * rows
    last = jnp.sum(jnp.where(lane == mine, rbias[0:1, :], 0.0), axis=1, keepdims=True)
    last = jnp.broadcast_to(last, (rows, 8)).T
    first = (jnp.zeros((1, 1), jnp.int32) + t) == 0
    gains_out[...] = small[0:1]
    biases_out[...] = jnp.concatenate(
        [small[1:3], jnp.where(first, small[3:4], last[0:1])], axis=0
    )
    hid_out[...] = jnp.concatenate([small[4:5], small[5:6]], axis=1)


def xor_permute(x, axis, bit):
    return lax.ppermute(x, axis, [(i, i ^ bit) for i in range(lax.axis_size(axis))])


def bit_groups(count):
    bits = [1 << i for i in range(count.bit_length() - 1)]
    groups = [tuple(bits[i : i + 2]) for i in range(0, len(bits), 2)]
    return groups[::-1]


def reaches(group):
    out = [0]
    for bit in group:
        out = out + [r ^ bit for r in out]
    return out


def slot_reaches(count):
    order = [0]
    for group in bit_groups(count):
        order = [r ^ o for r in reaches(group) for o in order]
    return order


def hop(sends, group):
    return [x if r == 0 else xor_permute(x, "dp", r) for x, r in zip(sends, reaches(group))]


def scatter_sum(s, groups, to_wire=lambda x: x, from_wire=lambda x: x):
    for group in reversed(groups):
        hops = reaches(group)
        rows = s.shape[0] // len(hops)
        parts = [s[i * rows : (i + 1) * rows] for i in range(len(hops))]
        moved = [xor_permute(to_wire(parts[i]), "dp", r) for i, r in enumerate(hops) if r]
        s = parts[0]
        for piece in moved:
            s = s + from_wire(piece)
    return s


def flip_by(x, index, count):
    for i in range(count.bit_length() - 1):
        bit = 1 << i
        shape = x.shape
        pairs = x.reshape((count // (2 * bit), 2, bit) + shape[1:])
        x = jnp.where((index & bit) != 0, pairs[:, ::-1], pairs).reshape(shape)
    return x


SMEM = pl.BlockSpec(memory_space=pltpu.SMEM)
VMEM = pl.BlockSpec(memory_space=pltpu.VMEM)
ANY = pl.BlockSpec(memory_space=pl.ANY)


def padded_bytes(shape, dtype):
    size = jnp.dtype(dtype).itemsize
    shape = (1,) * (2 - len(shape)) + tuple(shape)
    rows = -(-shape[-2] // 16) * 16
    return math.prod(shape[:-2]) * rows * (-(-shape[-1] // LANES) * LANES) * size


def call(kernel, name, in_specs, outs, out_specs, scratch, args, flops, moved):
    held = [(x.shape, x.dtype) for x in scratch if jnp.issubdtype(x.dtype, jnp.floating)]
    held += [(a.shape, a.dtype) for a, spec in zip(args, in_specs) if spec is VMEM]
    held += [o for o, spec in zip(outs, out_specs) if spec is VMEM]
    limit = VMEM_LIMIT
    if name in SMALL:
        limit = min(limit, sum(padded_bytes(*x) for x in held) + MARGIN)
    return pl.pallas_call(
        kernel,
        name=name,
        in_specs=in_specs,
        out_shape=[jax.ShapeDtypeStruct(s, d) for s, d in outs],
        out_specs=out_specs,
        scratch_shapes=scratch,
        compiler_params=pltpu.CompilerParams(vmem_limit_bytes=limit),
        cost_estimate=pl.CostEstimate(flops=flops, bytes_accessed=moved, transcendentals=0),
    )(*args)


def body(
    pictures, captions, tallies, exponent,
    p_gains, p_biases, p_hid, p_wq, p_wp, p_we, p_wr,
    c_gains, c_biases, c_hid, c_wq, c_wp, c_we, c_wr,
):
    t = lax.axis_index("tower")
    d = lax.axis_index("dp")
    chips = lax.axis_size("dp")
    pairs, length, width = captions.shape
    img_len = pictures.shape[1]
    hidden = c_hid.shape[0]
    caps = pairs // 2
    n = caps * length
    total = pairs * chips
    row_blocks = 16
    order = np.array(slot_reaches(chips))
    away = jnp.arange(chips, dtype=jnp.int32) ^ d
    slots, stride = jnp.zeros(chips, jnp.int32), 1
    for group in bit_groups(chips):
        slots = slots + ((away >> (group[0].bit_length() - 1)) & (len(reaches(group)) - 1)) * stride
        stride *= len(reaches(group))
    relative = chips == row_blocks
    row_slots = slots if relative else jnp.arange(row_blocks, dtype=jnp.int32)
    head = jnp.stack([t, d, tallies[0], t]).astype(jnp.int32)
    scal = jnp.concatenate([head, row_slots, slots])

    texts_in = captions.reshape(pairs * length, width)
    c_hid2, p_hid2 = c_hid.reshape(hidden // LANES, LANES), p_hid.reshape(hidden // LANES, LANES)
    blk = (row_blocks, width // row_blocks, n)
    vm = pltpu.VMEM
    sem = pltpu.SemaphoreType.DMA
    half_hid = (n, hidden // 2)
    chunk = width + 2 * LANES
    a_t, qkv, o_t, m, c_t, gp_keep, gp_send, text_send, emb, r = call(
        text_forward_kernel, "text_forward",
        [SMEM, ANY, VMEM, VMEM, VMEM, ANY, ANY, ANY, ANY],
        [(blk, BF16), ((n, 3 * width), BF16), (blk, BF16), ((n, width), F32), (blk, BF16),
         (half_hid, BF16), (half_hid, BF16), ((chips, caps, chunk), BF16),
         ((caps, width), F32), ((caps, LANES), F32)],
        [ANY] * 7 + [VMEM] * 3,
        [vm((n, width), BF16), vm((width, 3 * width), BF16), vm((width, width), BF16),
         vm((width, hidden), BF16), vm((hidden, width), BF16), vm((1, 3 * width), F32),
         vm((1, hidden), F32),
         vm((n, width), BF16), vm((n, width), BF16), vm((caps, hidden), F32), vm(blk, BF16), vm((n, 3 * width), BF16),
         vm(blk, BF16), vm((n, width), F32), vm(blk, BF16), vm(half_hid, BF16),
         vm(half_hid, BF16), sem((5,)), sem((7,))],
        (scal, texts_in, c_gains, c_biases, c_hid2, c_wq, c_wp, c_we, c_wr),
        int(2 * n * width * (4 * width + hidden)), 20_000_000,
    )
    c_far = xor_permute(c_t, "tower", 1)
    gp_far = xor_permute(gp_send, "tower", 1)
    text_all = lax.all_to_all(text_send, "dp", 0, 0, tiled=True)

    rows = caps * PAD
    groups = bit_groups(chips)
    (image,) = call(
        image_forward_kernel, "image_forward",
        [SMEM, ANY, VMEM, VMEM, VMEM, ANY, ANY, ANY, ANY],
        [((caps, width), BF16)],
        [VMEM],
        [vm((img_len, pairs, width), BF16), vm((width // LANES, img_len * caps, LANES), F32),
         vm((rows, width), F32), vm((rows, width), BF16),
         vm((rows + 16, 3 * width), BF16), vm((rows, width), F32), vm((caps, width), F32),
         vm((caps, hidden), F32), vm((width, 3 * width), BF16), vm((width, width), BF16),
         vm((width, hidden), BF16), vm((hidden, width), BF16), vm((1, 3 * width), F32),
         vm((1, hidden), F32),
         vm((1, width), F32), sem((5,))],
        (scal, jnp.transpose(pictures, (1, 0, 2)), p_gains, p_biases, p_hid2,
         p_wq, p_wp, p_we, p_wr),
        int(2 * rows * width * (4 * width + hidden)), 20_000_000,
    )
    image, text_all = lax.optimization_barrier((image, text_all))
    text_par = xor_permute(text_all, "tower", 1)
    got = hop([image[None]] * len(reaches(groups[0])), groups[0])
    for group in groups[1:]:
        whole = jnp.concatenate(got, axis=0)
        got = hop([whole] * len(reaches(group)), group)
    par_all = xor_permute(jnp.concatenate(got, axis=0), "tower", 1)
    small_slice = total <= 768
    if not small_slice:
        got = [jnp.concatenate(got, axis=0)]

    block = total if small_slice else 96
    held = chips if small_slice else 1
    share = hidden // (2 * chips)
    piece_shape = (width // 2, width)
    (loss, temp, ea, eb, ec, ed, g_all, images_all, texts_all, gall, extra, dc, dy, hid_grad) = call(
        partial(loss_kernel, block, len(got)), "loss",
        [SMEM] + [ANY] * len(got) + [ANY, ANY, ANY, SMEM, VMEM, VMEM] + [ANY] * 6,
        [((1, 1), F32), ((1, 1), F32)] + [(piece_shape, BF16)] * 4
        + [((total, total), BF16), ((total, width), BF16), ((total, width), BF16),
           ((total, LANES), BF16), ((total, LANES), F32), ((n, width), F32), ((caps, width), F32),
           ((1, hidden // 2), F32)],
        [VMEM, VMEM] + [ANY] * 10 + [VMEM, VMEM],
        [vm((held, caps, width), BF16), vm((held, caps, width), BF16),
         vm((held, caps, chunk), BF16), vm((held, caps, chunk), BF16),
         vm((total, width), BF16), vm((total, width), BF16), vm((total, LANES), F32),
         vm((total, LANES), BF16), vm((8, total), F32),
         vm((block, total), F32), vm((block, total), BF16), vm((2 * caps, total), BF16),
         vm(half_hid, BF16), vm(half_hid, BF16), vm((2,) + blk, BF16),
         vm((width, hidden // 2), BF16), vm((hidden // 2, width), BF16),
         vm((n, width), F32), vm((2, width, hidden // 4), BF16), sem((16,)), sem((14,))],
        (scal, *got, par_all, text_all, text_par, exponent, emb, r, gp_keep, gp_far,
         c_t, c_far, c_we, c_wr),
        int(3 * n * width * hidden), 20_000_000,
    )

    def widen(x):
        return x.astype(F32)

    def narrow(x):
        return x.astype(BF16)

    e_hops = [xor_permute(ea, "dp", 1), xor_permute(eb, "dp", 2)] if relative else []
    dm, dqkv, vec = call(
        middle_back_kernel, "middle_back",
        [SMEM, ANY, VMEM, ANY, ANY, VMEM] + [ANY] * 4,
        [((n, width), F32), ((n, 3 * width), BF16), ((8, width), F32)],
        [ANY, ANY, VMEM],
        [vm((n, width), F32), vm(half_hid, BF16), vm((n, width), F32),
         vm((width, hidden // 2), BF16), vm((hidden // 2, width), BF16), vm((width, width), BF16),
         vm((n, 3 * width), BF16), vm((n, width), F32), vm((n, width), BF16),
         vm((n, width), BF16), vm((n, 3 * width), BF16), sem((12,))],
        (scal, dc, dy, gp_send, m, c_gains, c_we, c_wr, c_wp, qkv),
        int(2 * n * width * (hidden + 4 * width)), 20_000_000,
    )
    b_shape = (width // 2, width + LANES)
    quarter_shape = (width // 4, width)
    qa_keep, qb_keep, qa_send, qb_send, *turned = call(
        partial(weight_grad_kernel, relative), "weight_grad",
        [SMEM] + [ANY] * 5 + [VMEM] * 4 + [ANY] * (4 if relative else 0),
        [((2,) + piece_shape, BF16), ((2,) + b_shape, BF16)] * 2
        + ([(quarter_shape, F32)] * 2 + [(quarter_shape, BF16)] * 2 if relative else []),
        [ANY] * 4 + [VMEM] * (4 if relative else 0),
        [vm((n, width), F32), vm(blk, BF16), vm(blk, BF16), vm((n, width), BF16),
         vm((n, 3 * width), BF16), vm((row_blocks, width // row_blocks, 3 * width), BF16),
         vm((2, 4, width, width // 2), BF16), vm((2, width, LANES), BF16), vm((width, LANES), F32),
         vm((row_blocks, width // row_blocks, LANES), F32), sem((8 + row_blocks,)), sem((40,))]
        + ([vm(piece_shape, BF16)] * 4 + [sem((4,))] if relative else []),
        (scal, dm, dqkv, a_t, o_t, c_wq, c_gains, c_biases, vec, hid_grad)
        + ((ec, e_hops[0], ed, e_hops[1]) if relative else ()),
        int(2 * n * width * 4 * width), 20_000_000,
    )
    qa_back = xor_permute(qa_send, "tower", 1)
    qb_back = xor_permute(qb_send, "tower", 1)
    cols = width // chips
    if relative:
        e_parts = (
            turned[0], turned[1], xor_permute(turned[2], "dp", 2), xor_permute(turned[3], "dp", 1)
        )
        wire_a, wire_b = call(
            partial(wire_kernel, width), "wire", [ANY] * 6,
            [(piece_shape, BF16), (b_shape, BF16)], [VMEM] * 2,
            [vm(piece_shape, BF16)] * 2 + [vm(b_shape, BF16)] * 2 + [sem((4,))],
            (qa_keep, qa_back, qb_keep, qb_back, *e_parts[2:]), 1_000_000, 4_000_000,
        )
        q_hops = [xor_permute(wire_a, "dp", 1), xor_permute(wire_b, "dp", 2)]
    else:
        q_sums = [
            from_wire(x[i], width) + from_wire(y[i], width)
            for i in range(2)
            for x, y in ((qa_keep, qa_back), (qb_keep, qb_back))
        ]
        tails = jnp.transpose(hid_grad.reshape(chips, 2, cols), (0, 2, 1)).reshape(width, 2)
        tails = jnp.pad(tails, ((0, 0), (width + 4, 64 - 6)))
        quarter = width // 4
        for i in (1, 3):
            q_sums[i] = q_sums[i] + jnp.concatenate(
                [tails[q * quarter : (q + 1) * quarter] for q in QUARTERS[i]], axis=0
            )
        wire_b = qb_back
        q_hops = []
    tok_keep, tok_send = call(
        input_back_kernel, "input_back",
        [SMEM, ANY, ANY, VMEM, ANY, ANY, ANY],
        [((caps, length // 2, width), F32), ((caps, length // 2, width), BF16)],
        [VMEM] * 2,
        [vm((n, width), BF16), vm((width, 3 * width), BF16), vm((n, width), F32),
         vm((n, 3 * width), BF16), vm((n, width), F32), sem((4,))],
        (scal, dm, texts_in, c_gains, dqkv, c_wq, wire_b),
        int(2 * n * width * 3 * width), 9_000_000,
    )
    reduce_grad, rbias = call(
        partial(reduce_grad_kernel, block, length), "reduce_grad",
        [SMEM] + [ANY] * 6,
        [((share, width), F32), ((8, width), F32)],
        [VMEM, VMEM],
        [vm((block, total), BF16), vm((total, width), BF16), vm((block, width), BF16),
         vm((block, LANES), BF16), vm((block, LANES), F32), vm((LANES, width), F32), sem((5,))],
        (exponent, g_all, images_all, texts_all, gall, extra, q_hops[0] if relative else wire_b),
        int(2 * total * total * width), 6_000_000,
    )

    tok_back = widen(xor_permute(tok_send, "tower", 1))
    grad_tokens = jnp.concatenate(
        [jnp.where(t == 0, tok_keep, tok_back), jnp.where(t == 0, tok_back, tok_keep)], axis=0
    )
    half, third = width // 2, width // 4

    def plain(sums):
        sides = []
        for side in range(2):
            at = {}
            for i in (side, side + 2):
                for j, q in enumerate(QUARTERS[i]):
                    at[q] = sums[i][j * third : (j + 1) * third]
            x = jnp.concatenate([at[q] for q in range(4)], axis=0)
            x = flip_by(x.reshape((chips, cols) + x.shape[1:]), d, chips)
            x = x[order].reshape((width,) + x.shape[2:])
            sides.append(
                scatter_sum(x, groups, lambda v: to_wire(v, width), lambda v: from_wire(v, width))
            )
        return sides

    if not relative:
        expand_grad = jnp.concatenate(plain([widen(x) for x in (ea, eb, ec, ed)]), axis=1)
        side_a, side_b = plain(q_sums)
        small = side_b[:, width : width + 8].T
        last = jnp.where(
            t == 0, small[3], lax.dynamic_slice_in_dim(rbias[0], d * cols, cols, 0)
        )
        return (
            loss.reshape(1), temp.reshape(1), grad_tokens, small[0:1], jnp.stack([small[1], small[2], last]),
            small[4:6].reshape(2 * cols),
            jnp.concatenate([side_a[:, half:], side_b[:, :width]], axis=1), side_a[:, :half],
            expand_grad, reduce_grad,
        )

    def second_hops(side_a, side_b, stacked, name):
        count = len(side_a)
        shapes = [x.shape[-2:] for x in (*side_a, *side_b)]
        small = shapes[-1][1] - width
        kept_a, kept_b, next_a, next_b = call(
            partial(turn_kernel, width, stacked, count), name, [ANY] * (2 * count),
            [((third, width), F32), ((third, width + small // 2), F32),
             ((third, width), BF16), ((third, width + small), BF16)],
            [VMEM] * 4, [vm(x, BF16) for x in shapes] + [sem((2 * count,))],
            (*side_a, *side_b), 1_000_000, 4_000_000,
        )
        return kept_a, kept_b, xor_permute(next_a, "dp", 2), xor_permute(next_b, "dp", 1)

    def merge(parts, after, name):
        f32_cols = parts[0].shape[1] + parts[1].shape[1]
        bf_cols = parts[2].shape[1] + parts[3].shape[1]
        return call(
            partial(merge_kernel, width), name, [VMEM] * 4 + [ANY] * len(after),
            [((cols, f32_cols), F32)] + [((cols, bf_cols), BF16)] * 3, [VMEM] * 4, [],
            (*parts, *after), 1_000_000, 3_000_000,
        )

    def z_hops(pieces):
        return [xor_permute(x, "dp", r) for x, r in zip(pieces, reaches(groups[0])[1:])]

    e_own, *e_far = merge(e_parts, (wire_b,), "merge_expand")
    e_back = z_hops(e_far)
    expand_grad = e_own + sum(widen(x) for x in e_back)
    q_parts = second_hops(
        (qa_keep, qa_back, q_hops[0]), (qb_keep, qb_back, q_hops[1]), 2, "turn_qkv"
    )
    q_own, *q_far = merge(q_parts, e_back, "merge_qkv")
    q_in = z_hops(q_far)
    qkv_grad, project_grad, gains_grad, biases_grad, hid_rows = call(
        partial(finish_kernel, width), "finish", [SMEM] + [VMEM] * 5,
        [((cols, 3 * half), F32), ((cols, half), F32), ((1, cols), F32), ((3, cols), F32),
         ((1, 2 * cols), F32)],
        [VMEM] * 5, [], (scal, q_own, *q_in, rbias), 1_000_000, 2_000_000,
    )
    return (
        loss.reshape(1), temp.reshape(1), grad_tokens, gains_grad, biases_grad, hid_rows.reshape(2 * cols),
        qkv_grad, project_grad, expand_grad, reduce_grad,
    )


def solution(mesh):
    in_specs = (P("dp", None, None), P("dp", None, None), P("dp")) + (P(),) * 15
    out_specs = (
        P(), P(), P("dp", "tower", None), P("tower", "dp"), P("tower", "dp"),
        P(("tower", "dp")), P("dp", "tower"), P("dp", "tower"), P("dp", "tower"),
        P(("tower", "dp"), None),
    )
    return jax.shard_map(body, mesh=mesh, in_specs=in_specs, out_specs=out_specs, check_vma=False)
```
